32 devices in a mesh: segment: 4 (over y, core), dp: 8 (over z, x).
Axes of the slice: x: 2, y: 2, z: 4, core: 2. Of those that a mesh axis runs over, the one named last changes fastest.
Arguments:
- images: bfloat16 [64, 256, 1024], P('dp'), may hold values from -6 to 6
- texts: bfloat16 [64, 64, 1536], P('dp'), may hold values from -6 to 6
- section_weights: bfloat16 [4, 21504, 128], P('segment'), may hold values from -0.15625 to 0.15625
- uniting_weights: bfloat16 [3584, 1024], P('dp'), may hold values from -0.125 to 0.125
- codebooks: float32 [8, 2, 256, 1024], P('dp'), may hold values from -3 to 3
- neg_bank: bfloat16 [8, 256, 1024], P('dp'), may hold values from -6 to 6
- item_cats: int32 [4, 16, 1], replicated, may hold values from 0 to 7; in each aligned block of 16 rows (0 to 15, 16 to 31, ..., all dimensions but the last counted through in order) at most 2 rows name the same one
- cat_slot: int32 [8], replicated, may hold values from 0 to 7, each once
- neg_index: int32 [4, 16, 128], replicated, may hold values from 0 to 255
Outputs:
- uniting_grad: float32 [3584, 1024], P('dp')
- codebook_grad: float32 [8, 2, 256, 1024], P('dp')
- owner_loss: float32 [8], P('dp')
The draws below stay inside these ranges and needn't reach their ends.
Inputs may be any that keep to these rules, and one draw needn't show every extreme that they name: `item_cats`: within one row of 128 no category appears more than 2 times, and in some row some category appears exactly 2 times. `cat_slot`: A permutation: every category has its own slot; slot t lies with owner t.
All inputs are finite; a program needn't handle non-finite values.
Results may differ from the reference program's by a relative error of at most 0.028.
Values may be sent and summed in bfloat16 or wider, within the bound.
No kernel may reach another device: no remote copies, remote signals or barrier semaphores. Data moves between devices by JAX's collectives and lax.ppermute only.
A program may use at most 128 MiB of HBM per device.

```python
import math
import jax
import jax.numpy as jnp
import numpy as np
from jax import lax

D_IMG = 1024
HEAD_IMG = 64
D_TXT = 1536
HEAD_TXT = 128
EMB = 1024
PATCH = 256
TXT_LEN = 64
ITEM_DEV = 8
MERGE_DEV = 2
ITEMS = 64
CAT_DEV = 1
CATS = 8
CAP = 2
LEVELS = 2
CODES = 256
BANK = 256
NEG = 128
MERGE_IN = 2560
MERGE_ROWS = 3584
SLOT_ROWS = 21504
N_SEGMENT = 4
N_DP = 8


def draw_codebooks(key, part):
    shape_all = (CATS, LEVELS, CODES, EMB)
    values = jnp.clip(0.5 * jax.random.normal(key, shape_all, jnp.float32), -3.0, 3.0)
    return values


def set_ends(drawn, own_key, low, top_value):
    shape = drawn.shape
    spot = [jax.random.randint(jax.random.fold_in(own_key, axis), (), 0, shape[axis]) for axis in range(len(shape))]
    drawn = drawn.at[tuple(spot)].set(low)
    longest = shape.index(max(shape))
    spot[longest] = (spot[longest] + 1) % shape[longest]
    return drawn.at[tuple(spot)].set(top_value)


def steps_of(own_key, extent, split, low, top_value):
    loudness = 1.0
    for dim, blocks in split:
        steps = jax.random.uniform(jax.random.fold_in(jax.random.fold_in(own_key, 6), dim), (blocks,), jnp.float32, low / len(split), top_value / len(split))
        loudness = loudness * jnp.repeat(jnp.exp(steps), extent[dim] // blocks).reshape((-1,) + (1,) * (len(extent) - 1 - dim))
    return loudness


def deal_out(key, own, number, rows, count, top, bound, lean):
    order = jax.random.permutation(key, count)
    crowded, ordinary = shares(count, rows * top, bound, lean, True), shares(count, rows * top, bound, lean, False)
    places = jnp.arange(count)

    def named(lengths, turn):
        used = int((lengths > 0).sum())
        fixed = max(1, used // 4)
        moved = fixed + (places - fixed + turn * (used - fixed)) % max(1, count - fixed)
        return jnp.zeros((count,), jnp.int32).at[order[jnp.where(places < fixed, places, moved)]].set(jnp.asarray(lengths, jnp.int32))

    lengths = jnp.where(number % 4 == 0, named(crowded, number // 4), named(ordinary, number - number // 4 - 1))
    mixed = jax.random.permutation(jax.random.fold_in(own, 3), count)
    giver, receiver = mixed[0:count // 2 * 2:2], mixed[1:count // 2 * 2:2]
    room = jnp.minimum(lengths[giver] - 1, bound - lengths[receiver]) // 2
    room = jnp.where((giver == order[0]) | (receiver == order[0]) | (lengths[receiver] == 0), 0, jnp.maximum(room, 0))
    moved = jax.random.randint(jax.random.fold_in(own, 4), (count // 2,), 0, 1 << 20) % (room + 1)
    lengths = lengths.at[giver].add(-moved).at[receiver].add(moved)
    members = jnp.searchsorted(jnp.cumsum(lengths), jnp.arange(rows * top), side="right").astype(jnp.int32)
    table = members.reshape(top, rows).T
    table = table[jax.random.permutation(jax.random.fold_in(own, 1), rows)]
    turn = jax.random.randint(jax.random.fold_in(own, 2), (rows, 1), 0, top)
    return jnp.take_along_axis(table, (jnp.arange(top)[None, :] + turn) % top, axis=1)


def shares(number_of, total, bound, slope, full):
    weights = [(1 << 20) // math.isqrt(standing ** slope) + 1 for standing in range(1, number_of + 1)]
    largest = bound if full else min(bound, max(-(-total // number_of), total * weights[0] // sum(weights)))
    least = 1 if total - largest >= number_of - 1 else 0
    counts, surplus = [largest] + [least] * (number_of - 1), total - largest - least * (number_of - 1)
    while surplus > 0:
        free = [i for i in range(1, number_of) if counts[i] < largest] or [i for i in range(1, number_of) if counts[i] < bound]
        pool, budget = sum([weights[i] for i in free]), surplus
        for i in free:
            addition = min(bound - counts[i], max(1, budget * weights[i] // pool), surplus)
            counts[i] = counts[i] + addition
            surplus = surplus - addition
    return np.array(counts)


def gaussian(key, extent, scale, bound, pieces=(), kind=jnp.bfloat16):
    level = steps_of(key, extent, pieces, -0.22, 0.18) if pieces else 1.0
    result = jax.random.normal(key, extent, jnp.float32) * scale * level
    return jnp.minimum(jnp.maximum(result, -bound), bound).astype(kind)


def setup_inputs(seed: int = 0) -> dict:
    key_list = jax.random.split(jax.random.key(seed), 10)
    images = gaussian(key_list[0], (ITEMS, PATCH, D_IMG), 1.0, 6.0, ((0, 8),))
    texts = gaussian(key_list[1], (ITEMS, TXT_LEN, D_TXT), 1.0, 6.0, ((0, 8),))
    section_weights = gaussian(key_list[2], (N_SEGMENT, SLOT_ROWS, 128), D_TXT ** -0.5, 0.15625, ((0, 4),))
    uniting_weights = gaussian(key_list[3], (MERGE_ROWS, EMB), MERGE_IN ** -0.5, 0.125, ((0, 8),))
    codebooks = draw_codebooks(jax.random.fold_in(key_list[9], 71), 0)
    neg_bank = gaussian(key_list[5], (CATS, BANK, EMB), 1.0, 6.0, ((0, 8),))
    item_cats_keys = jax.random.split(jax.random.fold_in(key_list[6], 1), N_SEGMENT * (N_DP * MERGE_DEV) // (N_DP * MERGE_DEV))
    item_cats_turns = jax.random.permutation(jax.random.fold_in(key_list[6], 3), N_SEGMENT * (N_DP * MERGE_DEV) // (N_DP * MERGE_DEV))
    item_cats = jax.vmap(lambda own, number: deal_out(jax.random.fold_in(key_list[6], 2), own, number, N_DP * MERGE_DEV, CATS, 1, CAP, 2))(item_cats_keys, item_cats_turns).reshape((N_SEGMENT, N_DP * MERGE_DEV, 1))
    cat_slot = jax.random.permutation(key_list[7], CATS).astype(jnp.int32)
    neg_index = set_ends(jax.random.randint(key_list[8], (N_SEGMENT, N_DP * MERGE_DEV, NEG), 0, BANK), jax.random.fold_in(key_list[8], 1), 0, BANK - 1).astype(jnp.int32)
    return {"images": images, "texts": texts, "section_weights": section_weights, "uniting_weights": uniting_weights, "codebooks": codebooks, "neg_bank": neg_bank, "item_cats": item_cats, "cat_slot": cat_slot, "neg_index": neg_index}


norm_eps = 1e-06
rope_theta = 1000000.0
contrast_temp = 0.1
beta_weight = 1.0
highest = lax.Precision.HIGHEST

def operand(tensor):
    return tensor.astype(jnp.float32)

def gelu_value(inputs_f):
    return 0.5 * inputs_f * (1.0 + lax.erf(inputs_f / math.sqrt(2.0)))

def gelu_slope(inputs_f):
    return 0.5 * (1.0 + lax.erf(inputs_f / math.sqrt(2.0))) + inputs_f * jnp.exp(-0.5 * inputs_f * inputs_f) / math.sqrt(2.0 * math.pi)

def rotate_pairs(tensor, positions):
    half_dim = tensor.shape[-1] // 2
    exponents = jnp.arange(half_dim).astype(jnp.float32) * (2.0 / tensor.shape[-1])
    inverse_freq = jnp.exp(-math.log(rope_theta) * exponents)
    angles = positions[:, None] * inverse_freq[None, :]
    cosine = jnp.concatenate([jnp.cos(angles), jnp.cos(angles)], axis=-1)[:, None, :]
    sine = jnp.concatenate([jnp.sin(angles), jnp.sin(angles)], axis=-1)[:, None, :]
    rotated = jnp.concatenate([-tensor[..., half_dim:], tensor[..., :half_dim]], axis=-1)
    return tensor * cosine + rotated * sine

def softmax_rows(scores):
    scores = scores - lax.optimization_barrier(jnp.max(scores, axis=-1, keepdims=True))
    exp_scores = jnp.exp(scores)
    return (exp_scores / lax.optimization_barrier(jnp.sum(exp_scores, axis=-1, keepdims=True))).astype(jnp.bfloat16)

def image_attention(images, flat_slot):
    item_count, patch_count, model_width = images.shape
    half_width = model_width // 2
    head_count = half_width // HEAD_IMG
    qkv_size = model_width * 3 * half_width
    w_qkv = flat_slot[:qkv_size].reshape(model_width, 3 * half_width)
    w_out = flat_slot[qkv_size:qkv_size + half_width * model_width].reshape(half_width, model_width)
    float_tokens = images.astype(jnp.float32)
    centred = float_tokens - lax.optimization_barrier(jnp.mean(float_tokens, axis=-1, keepdims=True))
    variance = lax.optimization_barrier(jnp.mean(centred * centred, axis=-1, keepdims=True))
    normed = (centred * lax.rsqrt(variance + norm_eps)).astype(jnp.bfloat16)
    projections = jnp.einsum('bpd,de->bpe', operand(normed), operand(w_qkv), preferred_element_type=jnp.float32).astype(jnp.bfloat16)
    queries = projections[..., :half_width].reshape(item_count, patch_count, head_count, HEAD_IMG)
    key_rows = projections[..., half_width:2 * half_width].reshape(item_count, patch_count, head_count, HEAD_IMG)
    value_rows = projections[..., 2 * half_width:].reshape(item_count, patch_count, head_count, HEAD_IMG)
    scores = jnp.einsum('bqhc,bkhc->bhqk', operand(queries), operand(key_rows), preferred_element_type=jnp.float32) / math.sqrt(HEAD_IMG)
    probabilities = softmax_rows(scores)
    attended = jnp.einsum('bhqk,bkhc->bqhc', operand(probabilities), operand(value_rows), preferred_element_type=jnp.float32).astype(jnp.bfloat16)
    attended = attended.reshape(item_count, patch_count, half_width)
    projected = jnp.einsum('bpc,cd->bpd', operand(attended), operand(w_out), preferred_element_type=jnp.float32)
    return lax.optimization_barrier(jnp.mean(projected, axis=1))

def text_attention(texts, flat_slot):
    item_count, token_count, model_width = texts.shape
    half_width = model_width // 2
    head_count = half_width // HEAD_TXT
    inner_width = half_width + 2 * HEAD_TXT
    qkv_size = model_width * inner_width
    w_qkv = flat_slot[:qkv_size].reshape(model_width, inner_width)
    w_out = flat_slot[qkv_size:qkv_size + half_width * model_width].reshape(half_width, model_width)
    float_tokens = texts.astype(jnp.float32)
    normed = (float_tokens * lax.rsqrt(lax.optimization_barrier(jnp.mean(float_tokens * float_tokens, axis=-1, keepdims=True)) + norm_eps)).astype(jnp.bfloat16)
    projections = jnp.einsum('btd,de->bte', operand(normed), operand(w_qkv), preferred_element_type=jnp.float32)
    positions = jnp.arange(token_count).astype(jnp.float32)
    queries = rotate_pairs(projections[..., :half_width].reshape(item_count, token_count, head_count, HEAD_TXT), positions).astype(jnp.bfloat16)
    key_rows = rotate_pairs(projections[..., half_width:half_width + HEAD_TXT].reshape(item_count, token_count, 1, HEAD_TXT), positions)[:, :, 0, :].astype(jnp.bfloat16)
    value_rows = projections[..., half_width + HEAD_TXT:].astype(jnp.bfloat16)
    scores = jnp.einsum('bqhc,bkc->bhqk', operand(queries), operand(key_rows), preferred_element_type=jnp.float32) / math.sqrt(HEAD_TXT)
    causal = jnp.arange(token_count)[:, None] >= jnp.arange(token_count)[None, :]
    scores = jnp.where(causal, scores, -1e+30)
    probabilities = softmax_rows(scores)
    attended = jnp.einsum('bhqk,bkc->bqhc', operand(probabilities), operand(value_rows), preferred_element_type=jnp.float32).astype(jnp.bfloat16)
    attended = attended.reshape(item_count, token_count, half_width)
    projected = jnp.einsum('btc,cd->btd', operand(attended), operand(w_out), preferred_element_type=jnp.float32)
    return lax.optimization_barrier(jnp.mean(projected, axis=1))

def merge_forward(embedded, stacked):
    first_rows = embedded.shape[1]
    float_embed = embedded.astype(jnp.float32)
    normed = (float_embed * lax.rsqrt(lax.optimization_barrier(jnp.mean(float_embed * float_embed, axis=1, keepdims=True)) + norm_eps)).astype(jnp.bfloat16)
    hidden = jnp.dot(normed, stacked[:first_rows], preferred_element_type=jnp.float32)
    activated = gelu_value(hidden).astype(jnp.bfloat16)
    merged = jnp.dot(activated, stacked[first_rows:], preferred_element_type=jnp.float32).astype(jnp.bfloat16)
    return (normed, hidden, activated, merged)

def merge_backward(hidden, stacked, out_grad, first_rows):
    w_second = stacked[first_rows:]
    act_grad = lax.dot_general(out_grad, w_second, (((1,), (1,)), ((), ())), preferred_element_type=jnp.float32)
    return (act_grad * gelu_slope(hidden)).astype(jnp.bfloat16)

def item_loss(merged_row, book_rows, negatives):
    emb_width = merged_row.shape[0]
    quant_tau = math.sqrt(emb_width) / 2.0
    residual = merged_row * lax.rsqrt(jnp.mean(merged_row * merged_row) + norm_eps)
    quantized = jnp.zeros_like(merged_row)
    for level_index in range(book_rows.shape[0]):
        code_rows = book_rows[level_index]
        cross_terms = jnp.dot(code_rows, residual, precision=highest)
        logits = (2.0 * cross_terms - lax.optimization_barrier(jnp.sum(code_rows * code_rows, axis=1))) / quant_tau
        logits = logits - lax.stop_gradient(jnp.max(logits))
        exp_logits = jnp.exp(logits)
        chosen = jnp.dot(exp_logits / jnp.sum(exp_logits), code_rows, precision=highest)
        residual = residual - chosen
        quantized = quantized + chosen
    recon_error = jnp.mean(residual * residual)
    anchor = quantized * lax.rsqrt(jnp.mean(quantized * quantized) + norm_eps)
    candidates = jnp.concatenate([merged_row[None, :], negatives.astype(jnp.float32)], axis=0)
    cand_unit = candidates * lax.rsqrt(lax.optimization_barrier(jnp.mean(candidates * candidates, axis=1, keepdims=True)) + norm_eps)
    similarity = jnp.dot(cand_unit, anchor, precision=highest) / (emb_width * contrast_temp)
    top_score = lax.stop_gradient(jnp.max(similarity))
    contrast = top_score + jnp.log(jnp.sum(jnp.exp(similarity - top_score))) - similarity[0]
    return contrast + beta_weight * recon_error

def to_rows(tensor):
    return tensor.reshape(N_DP, N_SEGMENT, MERGE_DEV, -1).transpose(1, 0, 2, 3).reshape(N_SEGMENT * N_DP * MERGE_DEV, -1)

def from_rows(tensor):
    return tensor.reshape(N_SEGMENT, N_DP, MERGE_DEV, -1).transpose(1, 0, 2, 3).reshape(ITEMS, -1)

def reference(images, texts, section_weights, uniting_weights, codebooks, neg_bank, item_cats, cat_slot, neg_index):
    slot_table = section_weights.reshape(N_SEGMENT, -1)
    image_blocks = images.reshape(ITEMS // ITEM_DEV, ITEM_DEV, PATCH, D_IMG)
    text_blocks = texts.reshape(ITEMS // ITEM_DEV, ITEM_DEV, TXT_LEN, D_TXT)
    image_embed = lax.optimization_barrier(jnp.mean(images.astype(jnp.float32), axis=1))
    text_embed = lax.optimization_barrier(jnp.mean(texts.astype(jnp.float32), axis=1))
    for group_index in range(2):
        image_slot = slot_table[group_index]
        text_slot = slot_table[2 + group_index]
        image_embed = image_embed + lax.map(lambda item_block: image_attention(item_block, image_slot), image_blocks).reshape(ITEMS, D_IMG)
        text_embed = text_embed + lax.map(lambda item_block: text_attention(item_block, text_slot), text_blocks).reshape(ITEMS, D_TXT)
    embedded = jnp.concatenate([image_embed, text_embed], axis=1).astype(jnp.bfloat16)
    normed, hidden, activated, merged = merge_forward(embedded, uniting_weights)
    merged_rows = to_rows(merged).astype(jnp.float32)
    cats_flat = item_cats.reshape(-1).astype(jnp.int32)
    negs_flat = neg_index.reshape(-1, NEG).astype(jnp.int32)
    loss_scale = 1.0 / math.sqrt(ITEMS)

    def visit(grad_total, inputs):
        merged_row, category, negative_ids = inputs
        slot_id = cat_slot[category]
        book_rows = lax.dynamic_index_in_dim(codebooks, slot_id, 0, keepdims=False)
        bank_rows = lax.dynamic_index_in_dim(neg_bank, slot_id, 0, keepdims=False)
        negatives = jnp.take(bank_rows, negative_ids, axis=0)

        def scaled(row_value, book_value):
            return item_loss(row_value, book_value, negatives) * loss_scale
        loss_value, pullback = jax.vjp(scaled, merged_row, book_rows)
        row_grad, book_grad = pullback(jnp.ones((), jnp.float32))
        current = lax.dynamic_index_in_dim(grad_total, slot_id, 0, keepdims=False)
        grad_total = lax.dynamic_update_index_in_dim(grad_total, current + book_grad, slot_id, 0)
        return (grad_total, (row_grad, loss_value))
    book_total, (row_grads, row_losses) = lax.scan(visit, jnp.zeros(codebooks.shape, jnp.float32), (merged_rows, cats_flat, negs_flat))
    row_owner = jnp.take(cat_slot, cats_flat) // CAT_DEV
    owner_match = row_owner[None, :] == jnp.arange(N_DP)[:, None]
    owner_loss = lax.optimization_barrier(jnp.sum(jnp.where(owner_match, row_losses[None, :], 0.0), axis=1))
    out_grad = from_rows(row_grads).astype(jnp.bfloat16)
    hidden_grad = merge_backward(hidden, uniting_weights, out_grad, MERGE_IN)
    grad_first = jnp.dot(normed.T, hidden_grad, preferred_element_type=jnp.float32)
    grad_second = jnp.dot(activated.T, out_grad, preferred_element_type=jnp.float32)
    return (jnp.concatenate([grad_first, grad_second], axis=0), book_total, owner_loss)
```

```python
import functools
import math

import jax
import jax.numpy as jnp
import numpy as np
from jax import lax
from jax.experimental import pallas as pl
from jax.experimental.pallas import tpu as pltpu
from jax.sharding import PartitionSpec as P

F32 = jnp.float32
BF16 = jnp.bfloat16

HEAD_IMG = 64
HEAD_TXT = 128
CAP = 2


norm_eps = 1e-06
rope_theta = 1000000.0
contrast_temp = 0.1
beta_weight = 1.0
highest = lax.Precision.HIGHEST


def gelu_value(inputs_f):
    return 0.5 * inputs_f * (1.0 + lax.erf(inputs_f / math.sqrt(2.0)))


def gelu_slope(inputs_f):
    return 0.5 * (1.0 + lax.erf(inputs_f / math.sqrt(2.0))) + inputs_f * jnp.exp(
        -0.5 * inputs_f * inputs_f
    ) / math.sqrt(2.0 * math.pi)


def dot_nt(a, b):
    return lax.dot_general(a, b, (((1,), (1,)), ((), ())), preferred_element_type=F32)

def dot_nn(a, b):
    return jnp.dot(a, b, preferred_element_type=F32)

def two_parts(value):
    high = value.astype(BF16)
    return jnp.concatenate([high, (value - high.astype(F32)).astype(BF16)], axis=0)

def dot_two(value, weights):
    rows = value.shape[0]
    both = dot_nn(two_parts(value), weights)
    return both[:rows] + both[rows:]

def unfold(slot_ref, first, out_ref, wide_ref, row_step):
    rows, columns = out_ref.shape
    blocks = columns // 128
    def body(step, carry):
        start = pl.multiple_of(step * row_step, row_step)
        source = pl.multiple_of(first + step * (row_step * blocks), 16)
        wide_ref[0 : row_step * blocks, :] = slot_ref[0, pl.ds(source, row_step * blocks), :].astype(F32)
        for block in range(blocks):
            piece = wide_ref[pl.ds(block, row_step, stride=blocks), :]
            out_ref[pl.ds(start, row_step), block * 128 : (block + 1) * 128] = piece.astype(BF16)
        return carry
    lax.fori_loop(0, rows // row_step, body, 0)

def image_kernel(flag_ref, image_ref, slot_ref, pooled_ref, w_in, w_out, wide, heads_mean):
    step = pl.program_id(0)
    item_count, model_width = pooled_ref.shape
    half_width = model_width // 2
    head_count = half_width // HEAD_IMG
    patch_count = image_ref.shape[1]

    @pl.when(step == 0)
    def _():
        unfold(slot_ref, 0, w_in, wide, 128)
        unfold(slot_ref, model_width * 12, w_out, wide, 128)

    tokens = image_ref[0].astype(F32)
    centred = tokens - jnp.mean(tokens, axis=1, keepdims=True)
    variance = jnp.mean(centred * centred, axis=1, keepdims=True)
    normed = (centred * lax.rsqrt(variance + norm_eps)).astype(BF16)
    queries = (dot_nn(normed, w_in[:, :half_width]).astype(BF16) * (1.0 / math.sqrt(HEAD_IMG))).astype(BF16)
    keys = dot_nn(normed, w_in[:, half_width : 2 * half_width]).astype(BF16)
    row_ids = lax.broadcasted_iota(jnp.int32, (head_count, patch_count), 0)
    weights = jnp.zeros((head_count, patch_count), F32)
    for head in range(head_count):
        span = slice(head * HEAD_IMG, (head + 1) * HEAD_IMG)
        scores = dot_nt(keys[:, span], queries[:, span])
        exps = jnp.exp(scores - jnp.max(scores, axis=0, keepdims=True))
        share = (1.0 / patch_count) / jnp.sum(exps, axis=0, keepdims=True)
        share = jnp.where(row_ids == head, share, 0.0).astype(BF16)
        weights = weights + dot_nt(share, exps.astype(BF16))
    heads_mean[pl.ds(step * head_count, head_count), :] = dot_two(weights, normed)
    residual = jnp.mean(tokens, axis=0, keepdims=True) * flag_ref[0].astype(F32)
    pooled_ref[pl.ds(step, 1), :] = residual

    @pl.when(step == item_count - 1)
    def _():
        values = dot_two(heads_mean[...], w_in[:, 2 * half_width :])
        rows = lax.broadcasted_iota(jnp.int32, values.shape, 0)
        columns = lax.broadcasted_iota(jnp.int32, values.shape, 1)
        values = jnp.where(rows % head_count == columns // HEAD_IMG, values, 0.0)
        attended = jnp.sum(values.reshape(item_count, head_count, half_width), axis=1)
        pooled_ref[...] += dot_two(attended, w_out[...])

def image_pooled(images, slot, flag):
    item_count, patch_count, model_width = images.shape
    half_width = model_width // 2
    head_count = half_width // HEAD_IMG
    return pl.pallas_call(
        image_kernel,
        grid=(item_count,),
        in_specs=[
            pl.BlockSpec(memory_space=pltpu.SMEM),
            pl.BlockSpec((1, patch_count, model_width), lambda i: (i, 0, 0)),
            pl.BlockSpec((1, 16 * model_width, 128), lambda i: (0, 0, 0), pipeline_mode=pl.Buffered(1)),
        ],
        out_specs=pl.BlockSpec((item_count, model_width), lambda i: (0, 0)),
        out_shape=jax.ShapeDtypeStruct((item_count, model_width), F32),
        scratch_shapes=[
            pltpu.VMEM((model_width, 3 * half_width), BF16),
            pltpu.VMEM((half_width, model_width), BF16),
            pltpu.VMEM((128 * 12, 128), F32),
            pltpu.VMEM((item_count * head_count, model_width), F32),
        ],
        compiler_params=pltpu.CompilerParams(vmem_limit_bytes=40 * 1024 * 1024),
    )(flag, images, slot)

def rope_tables(tokens, repeats):
    half = HEAD_TXT // 2
    exponents = np.arange(half).astype(np.float32) * np.float32(2.0 / HEAD_TXT)
    inverse = np.exp(np.float32(-math.log(rope_theta)) * exponents).astype(np.float32)
    angles = (np.arange(tokens).astype(np.float32)[:, None] * inverse[None, :]).astype(np.float32)
    cosine = np.concatenate([np.cos(angles), np.cos(angles)], axis=1)
    sine = np.concatenate([-np.sin(angles), np.sin(angles)], axis=1)
    return np.tile(cosine, (repeats, 1)).astype(np.float32), np.tile(sine, (repeats, 1)).astype(np.float32)

def text_kernel(flag_ref, text_ref, slot_ref, cos_ref, sin_ref, pooled_ref, w_in, w_out, wide, heads_mean):
    item_count, token_count, model_width = text_ref.shape
    half_width = model_width // 2
    head_count = half_width // HEAD_TXT
    unfold(slot_ref, 0, w_in, wide, 128)
    unfold(slot_ref, model_width * 8, w_out, wide, 128)
    tokens = text_ref[...].reshape(item_count * token_count, model_width).astype(F32)
    normed = (tokens * lax.rsqrt(jnp.mean(tokens * tokens, axis=1, keepdims=True) + norm_eps)).astype(BF16)
    residual = jnp.mean(tokens.reshape(item_count, token_count, model_width), axis=1)
    cosine, sine = cos_ref[...], sin_ref[...]

    def head_columns(head):
        return dot_nn(normed, w_in[:, head * HEAD_TXT : (head + 1) * HEAD_TXT])

    def turned(head, scale):
        part = head_columns(head)
        return ((part * cosine + pltpu.roll(part, HEAD_TXT // 2, 1) * sine).astype(BF16)).astype(F32) * scale

    queries = [(turned(head, 1.0)).astype(BF16) for head in range(head_count)]
    keys = turned(head_count, 1.0).astype(BF16)
    values = head_columns(head_count + 1).astype(BF16)
    wide_columns = head_count * token_count
    key_ids = lax.broadcasted_iota(jnp.int32, (token_count, wide_columns), 0)
    query_ids = lax.broadcasted_iota(jnp.int32, (token_count, wide_columns), 1) % token_count
    allowed = key_ids <= query_ids
    own_head = lax.broadcasted_iota(jnp.int32, (8, wide_columns), 0) == (
        lax.broadcasted_iota(jnp.int32, (8, wide_columns), 1) // token_count
    )
    for item in range(item_count):
        span = slice(item * token_count, (item + 1) * token_count)
        asked = jnp.concatenate([query[span] for query in queries], axis=0)
        scores = dot_nt(keys[span], asked) * (1.0 / math.sqrt(HEAD_TXT))
        scores = jnp.where(allowed, scores, -1e30)
        exps = jnp.exp(scores - jnp.max(scores, axis=0, keepdims=True))
        share = (1.0 / token_count) / jnp.sum(exps, axis=0, keepdims=True)
        share = jnp.where(own_head, share, 0.0).astype(BF16)
        weights = dot_nt(share, exps.astype(BF16))
        heads_mean[:, item, :] = dot_two(weights, values[span])
    pooled = residual * flag_ref[0].astype(F32)
    for head in range(head_count):
        pooled = pooled + dot_two(heads_mean[head], w_out[head * HEAD_TXT : (head + 1) * HEAD_TXT, :])
    pooled_ref[...] = pooled

def text_pooled(texts, slot, flag):
    item_count, token_count, model_width = texts.shape
    half_width = model_width // 2
    inner = half_width + 2 * HEAD_TXT
    cosine, sine = rope_tables(token_count, item_count)
    vm = pl.BlockSpec(memory_space=pltpu.VMEM)
    return pl.pallas_call(
        text_kernel,
        in_specs=[pl.BlockSpec(memory_space=pltpu.SMEM)] + [vm] * 4,
        out_specs=vm,
        out_shape=jax.ShapeDtypeStruct((item_count, model_width), F32),
        scratch_shapes=[
            pltpu.VMEM((model_width, inner), BF16),
            pltpu.VMEM((half_width, model_width), BF16),
            pltpu.VMEM((128 * 12, 128), F32),
            pltpu.VMEM((8, item_count, HEAD_TXT), F32),
        ],
        compiler_params=pltpu.CompilerParams(vmem_limit_bytes=40 * 1024 * 1024),
    )(flag, texts, slot, jnp.asarray(cosine), jnp.asarray(sine))

def merge_forward(embedded, stacked):
    first_rows = embedded.shape[1]
    float_embed = embedded.astype(jnp.float32)
    normed = (
        float_embed
        * lax.rsqrt(jnp.mean(float_embed * float_embed, axis=1, keepdims=True) + norm_eps)
    ).astype(jnp.bfloat16)
    hidden = jnp.dot(normed, stacked[:first_rows], preferred_element_type=jnp.float32)
    activated = gelu_value(hidden).astype(jnp.bfloat16)
    merged = jnp.dot(activated, stacked[first_rows:], preferred_element_type=jnp.float32).astype(
        jnp.bfloat16
    )
    return (normed, hidden, activated, merged)


def merge_backward(hidden, stacked, out_grad, first_rows):
    w_second = stacked[first_rows:]
    act_grad = lax.dot_general(
        out_grad, w_second, (((1,), (1,)), ((), ())), preferred_element_type=jnp.float32
    )
    return (act_grad * gelu_slope(hidden)).astype(jnp.bfloat16)


def item_loss(merged_row, book_rows, negatives):
    emb_width = merged_row.shape[0]
    quant_tau = math.sqrt(emb_width) / 2.0
    residual = merged_row * lax.rsqrt(jnp.mean(merged_row * merged_row) + norm_eps)
    quantized = jnp.zeros_like(merged_row)
    for level_index in range(book_rows.shape[0]):
        code_rows = book_rows[level_index]
        cross_terms = jnp.dot(code_rows, residual, precision=highest)
        logits = (2.0 * cross_terms - jnp.sum(code_rows * code_rows, axis=1)) / quant_tau
        logits = logits - lax.stop_gradient(jnp.max(logits))
        exp_logits = jnp.exp(logits)
        chosen = jnp.dot(exp_logits / jnp.sum(exp_logits), code_rows, precision=highest)
        residual = residual - chosen
        quantized = quantized + chosen
    recon_error = jnp.mean(residual * residual)
    anchor = quantized * lax.rsqrt(jnp.mean(quantized * quantized) + norm_eps)
    candidates = jnp.concatenate([merged_row[None, :], negatives.astype(jnp.float32)], axis=0)
    cand_unit = candidates * lax.rsqrt(
        jnp.mean(candidates * candidates, axis=1, keepdims=True) + norm_eps
    )
    similarity = jnp.dot(cand_unit, anchor, precision=highest) / (emb_width * contrast_temp)
    top_score = lax.stop_gradient(jnp.max(similarity))
    contrast = top_score + jnp.log(jnp.sum(jnp.exp(similarity - top_score))) - similarity[0]
    return contrast + beta_weight * recon_error


def stacked_term(columns, first_grad, second_grad, in_first):
    contract = (((0,), (0,)), ((), ()))
    first_term = lax.dot_general(columns, first_grad, contract, preferred_element_type=jnp.float32)
    second_term = lax.dot_general(
        columns, second_grad, contract, preferred_element_type=jnp.float32
    )
    return jnp.where(in_first[:, None], first_term, second_term)


def first_rows_in(shard, shard_rows, first_rows):
    return min(max(first_rows - shard * shard_rows, 0), shard_rows)


def unit_groups(shard_count, shard_rows, first_rows, segment_count):
    groups = []
    for shard in range(shard_count):
        inside = first_rows_in(shard, shard_rows, first_rows)
        if inside < shard_rows:
            share = (shard_rows - inside) // segment_count
            groups.append((shard, inside, shard * shard_rows + inside - first_rows, share))
    return groups


def message_kernel(groups, place_ref, rows_ref, message_ref):
    shard, segment = place_ref[0], place_ref[1]
    row_count, width = rows_ref.shape
    columns = message_ref.shape[1]
    first_last = groups[0][0]

    @pl.when(shard <= first_last)
    def _():
        wanted = lax.broadcasted_iota(jnp.int32, (width, columns), 1)
        unit = jnp.zeros_like(wanted)
        offset = 0
        for _, _, base, share in groups:
            inside = (wanted >= offset) & (wanted < offset + share)
            unit = jnp.where(inside, wanted - offset + base + share * segment, unit)
            offset += share
        chosen = (lax.broadcasted_iota(jnp.int32, (width, columns), 0) == unit).astype(F32).astype(BF16)
        message_ref[...] = dot_nn(rows_ref[...], chosen).astype(BF16)

    for group_shard, inside, _, share in groups:

        @pl.when(shard == group_shard)
        def _(inside=inside, share=share):
            start = pl.multiple_of(inside + share * segment, 16)
            for block in range(width // columns):
                message_ref[inside + block * share : inside + (block + 1) * share, :] = rows_ref[
                    pl.ds(start, share), block * columns : (block + 1) * columns
                ]


def weight_message(uniting_weights, place, groups, columns):
    vm = pl.BlockSpec(memory_space=pltpu.VMEM)
    return pl.pallas_call(
        functools.partial(message_kernel, groups),
        in_specs=[pl.BlockSpec(memory_space=pltpu.SMEM), vm],
        out_specs=vm,
        out_shape=jax.ShapeDtypeStruct((uniting_weights.shape[0], columns), BF16),
    )(place, uniting_weights)


def forward_kernel(
    groups,
    first_rows,
    place_ref,
    embedded_ref,
    own_ref,
    *refs,
):
    shard_count = (len(refs) - 6)
    piece_refs = refs[:shard_count]
    blocks_ref, hidden_ref, active_ref, second_ref, partial_ref, kept = refs[shard_count:]
    shard = place_ref[0]
    source_count, source_items, width = embedded_ref.shape
    items = source_count * source_items
    shard_rows, columns = piece_refs[0].shape
    embedded = embedded_ref[...].astype(F32).reshape(items, width)
    normed = embedded * lax.rsqrt(jnp.mean(embedded * embedded, axis=1, keepdims=True) + norm_eps)
    normed = normed.astype(BF16)
    for block in range(shard_count):
        inside = first_rows_in(block, shard_rows, first_rows)
        start = block * shard_rows
        if inside == shard_rows:
            blocks_ref[block] = normed[:, start : start + shard_rows]
        elif inside > 0:
            blocks_ref[block] = jnp.concatenate(
                [normed[:, start : start + inside], jnp.zeros((items, shard_rows - inside), BF16)], axis=1
            )
        else:
            blocks_ref[block] = jnp.zeros((items, shard_rows), BF16)
    hidden = jnp.zeros((items, columns), F32)
    first_group = groups[0][0]
    for turn in range(shard_count):
        source = lax.rem(shard - turn + shard_count, shard_count)
        hidden = hidden + dot_nn(blocks_ref[source], piece_refs[turn][...])

        @pl.when(source >= first_group)
        def _(turn=turn, source=source):
            kept[source - first_group] = piece_refs[turn][...]

    hidden_ref[...] = hidden
    active = gelu_value(hidden).astype(BF16)
    active_ref[...] = active
    offset = 0
    for index, (_, inside, _, share) in enumerate(groups):
        for block in range(partial_ref.shape[1] // columns):
            second_ref[offset : offset + share, block * columns : (block + 1) * columns] = kept[
                index, inside + block * share : inside + (block + 1) * share, :
            ]
        offset += share
    partial_ref[...] = dot_nn(dot_nn(own_ref[...], active).astype(BF16), second_ref[...])


def merge_quarter(embedded_all, pieces, own, place, groups, first_rows, width):
    shard_count, shard_rows, columns = len(pieces), pieces[0].shape[0], pieces[0].shape[1]
    items = embedded_all.shape[0] * embedded_all.shape[1]
    vm = pl.BlockSpec(memory_space=pltpu.VMEM)
    return pl.pallas_call(
        functools.partial(forward_kernel, groups, first_rows),
        in_specs=[pl.BlockSpec(memory_space=pltpu.SMEM)] + [vm] * (2 + shard_count),
        out_specs=[vm] * 5,
        out_shape=[
            jax.ShapeDtypeStruct((shard_count, items, shard_rows), BF16),
            jax.ShapeDtypeStruct((items, columns), F32),
            jax.ShapeDtypeStruct((items, columns), BF16),
            jax.ShapeDtypeStruct((columns, width), BF16),
            jax.ShapeDtypeStruct((own.shape[0], width), F32),
        ],
        scratch_shapes=[pltpu.VMEM((len(groups), shard_rows, columns), BF16)],
        compiler_params=pltpu.CompilerParams(vmem_limit_bytes=32 * 1024 * 1024),
    )(place, embedded_all, own, *pieces)


def split(value):
    high = value.astype(BF16)
    return high, (value - high.astype(F32)).astype(BF16)


def exact_nt(value, high, low):
    first, second = split(value)
    rows = value.shape[0]
    both = dot_nt(jnp.concatenate([first, second], axis=0), high)
    return both[:rows] + both[rows:] + dot_nt(first, low)


def exact_nn(value, high, low):
    first, second = split(value)
    rows = value.shape[0]
    both = dot_nn(jnp.concatenate([first, second], axis=0), high)
    return both[:rows] + both[rows:] + dot_nn(first, low)


def dot_tn(a, b):
    return lax.dot_general(a, b, (((0,), (0,)), ((), ())), preferred_element_type=F32)


def exact_tn(a, b):
    a_high, a_low = split(a)
    b_high, b_low = split(b)
    return dot_tn(
        jnp.concatenate([a_high, a_low, a_high], axis=0), jnp.concatenate([b_high, b_high, b_low], axis=0)
    )


def square_sums(value):
    high, low = split(value * value)
    ones = jnp.ones((8, value.shape[1]), BF16)
    return (dot_nt(ones, high) + dot_nt(ones, low))[:1]


def quantizer_kernel(loss_scale, merged_ref, book_ref, bank_ref, count_ref, book_grad_ref, merged_grad_ref, loss_ref, highs, lows):
    width = merged_ref.shape[1]
    levels = book_ref.shape[0]
    inverse_tau = 2.0 / math.sqrt(width)
    inverse_temp = 1.0 / (width * contrast_temp)
    merged = merged_ref[...].astype(BF16).astype(F32)
    merged_scale = lax.rsqrt(jnp.mean(merged * merged, axis=1, keepdims=True) + norm_eps)
    residuals = [merged * merged_scale]
    shares, chosen_rows = [], []
    for level in range(levels):
        codes = book_ref[level]
        high, low = split(codes)
        highs[level] = high
        lows[level] = low
        logits = (2.0 * exact_nt(residuals[level], high, low) - square_sums(codes)) * inverse_tau
        exps = jnp.exp(logits - jnp.max(logits, axis=1, keepdims=True))
        share = exps / jnp.sum(exps, axis=1, keepdims=True)
        chosen = exact_nn(share, high, low)
        shares.append(share)
        chosen_rows.append(chosen)
        residuals.append(residuals[level] - chosen)
    last = residuals[levels]
    quantized = chosen_rows[0]
    for chosen in chosen_rows[1:]:
        quantized = quantized + chosen
    anchor_scale = lax.rsqrt(jnp.mean(quantized * quantized, axis=1, keepdims=True) + norm_eps)
    anchor = quantized * anchor_scale
    own = jnp.sum(anchor * residuals[0], axis=1, keepdims=True) * inverse_temp
    bank = bank_ref[...]
    bank_wide = bank.astype(F32)
    bank_scale = lax.rsqrt(square_sums(bank_wide) * (1.0 / width) + norm_eps)
    anchor_parts = jnp.concatenate(split(anchor), axis=0)
    rows = anchor.shape[0]
    both = dot_nt(anchor_parts, bank)
    similar = (both[:rows] + both[rows:]) * bank_scale * inverse_temp
    counts = count_ref[...]
    named = counts > 0.0
    top = jnp.maximum(jnp.max(jnp.where(named, similar, own), axis=1, keepdims=True), own)
    bank_exps = jnp.where(named, jnp.exp(jnp.where(named, similar, top) - top), 0.0) * counts
    own_exp = jnp.exp(own - top)
    total = jnp.sum(bank_exps, axis=1, keepdims=True) + own_exp
    item_losses = top + jnp.log(total) - own + jnp.mean(last * last, axis=1, keepdims=True)
    loss_ref[...] = jnp.broadcast_to(jnp.sum(item_losses, axis=0, keepdims=True) * loss_scale, loss_ref.shape)

    bank_weight = bank_exps / total * (loss_scale * inverse_temp)
    own_weight = (own_exp / total - 1.0) * (loss_scale * inverse_temp)
    weight_parts = jnp.concatenate(split(bank_weight * bank_scale), axis=0)
    both = dot_nn(weight_parts, bank)
    anchor_grad = both[:rows] + both[rows:] + own_weight * residuals[0]
    unit_grad = own_weight * anchor
    quantized_grad = anchor_scale * (anchor_grad - anchor * jnp.mean(anchor * anchor_grad, axis=1, keepdims=True))
    residual_grad = last * (2.0 * loss_scale / width)
    ones = jnp.ones((rows, 128), F32)
    for level in reversed(range(levels)):
        high, low = highs[level], lows[level]
        chosen_grad = quantized_grad - residual_grad
        share_grad = exact_nt(chosen_grad, high, low)
        share = shares[level]
        logit_grad = share * (share_grad - jnp.sum(share * share_grad, axis=1, keepdims=True)) * (2.0 * inverse_tau)
        book_part = exact_tn(
            jnp.concatenate([share, logit_grad], axis=0), jnp.concatenate([chosen_grad, residuals[level]], axis=0)
        )
        totals = exact_tn(logit_grad, ones)
        for block in range(width // 128):
            span = slice(block * 128, (block + 1) * 128)
            book_grad_ref[level, :, span] = book_part[:, span] - totals * book_ref[level, :, span]
        residual_grad = residual_grad + exact_nn(logit_grad, high, low)
    unit_grad = unit_grad + residual_grad
    unit = residuals[0]
    merged_grad = merged_scale * (unit_grad - unit * jnp.mean(unit * unit_grad, axis=1, keepdims=True))
    merged_grad_ref[...] = merged_grad.astype(BF16)


def quantizer(merged, books, bank, counts, loss_scale):
    vm = pl.BlockSpec(memory_space=pltpu.VMEM)
    return pl.pallas_call(
        functools.partial(quantizer_kernel, loss_scale),
        in_specs=[vm] * 4,
        out_specs=[vm] * 3,
        out_shape=[
            jax.ShapeDtypeStruct(books.shape, F32),
            jax.ShapeDtypeStruct(merged.shape, BF16),
            jax.ShapeDtypeStruct((8, 128), F32),
        ],
        scratch_shapes=[pltpu.VMEM(books.shape, BF16), pltpu.VMEM(books.shape, BF16)],
        compiler_params=pltpu.CompilerParams(vmem_limit_bytes=32 * 1024 * 1024),
    )(merged, books, bank, counts)


def backward_kernel(gathered_ref, order_ref, hidden_ref, active_ref, second_ref, out_grad_ref, sent_ref):
    owners, places, width = gathered_ref.shape
    columns = hidden_ref.shape[1]
    gathered = gathered_ref[...].astype(F32).reshape(owners * places, width).astype(BF16)
    out_grad = dot_tn(order_ref[...], gathered).astype(BF16)
    out_grad_ref[...] = out_grad
    hidden_grad = dot_nt(out_grad, second_ref[...]) * gelu_slope(hidden_ref[...])
    sent_ref[:, :columns] = hidden_grad.astype(BF16)
    sent_ref[:, columns:] = active_ref[...]


def backward_quarter(gathered, order, hidden, active, second):
    items, columns = hidden.shape
    vm = pl.BlockSpec(memory_space=pltpu.VMEM)
    return pl.pallas_call(
        backward_kernel,
        in_specs=[vm] * 5,
        out_specs=[vm] * 2,
        out_shape=[
            jax.ShapeDtypeStruct((items, gathered.shape[2]), BF16),
            jax.ShapeDtypeStruct((items, 2 * columns), BF16),
        ],
        compiler_params=pltpu.CompilerParams(vmem_limit_bytes=32 * 1024 * 1024),
    )(gathered, order, hidden, active, second)


def weight_grad_kernel(groups, place_ref, block_ref, out_grad_ref, received_ref, grad_ref, hidden_grad, active):
    shard = place_ref[0]
    segment_count, items, doubled = received_ref.shape
    columns = doubled // 2
    shard_rows = block_ref.shape[1]
    for segment in range(segment_count):
        offset = 0
        for _, _, base, share in groups:
            spot = base + share * segment
            hidden_grad[:, spot : spot + share] = received_ref[segment, :, offset : offset + share]
            offset += share
    grad_ref[...] = dot_tn(block_ref[...], hidden_grad[...])
    for group_shard, inside, base, _ in groups:

        @pl.when(shard == group_shard)
        def _(inside=inside, base=base):
            for segment in range(segment_count):
                offset = columns
                for _, _, other, share in groups:
                    spot = other + share * segment
                    active[:, spot : spot + share] = received_ref[segment, :, offset : offset + share]
                    offset += share
            wanted = active[:, base : base + shard_rows - inside]
            grad_ref[inside:, :] = dot_tn(wanted, out_grad_ref[...])


def weight_grad(place, block, out_grad, received, groups):
    items, shard_rows = block.shape
    width = out_grad.shape[1]
    vm = pl.BlockSpec(memory_space=pltpu.VMEM)
    return pl.pallas_call(
        functools.partial(weight_grad_kernel, groups),
        in_specs=[pl.BlockSpec(memory_space=pltpu.SMEM)] + [vm] * 3,
        out_specs=vm,
        out_shape=jax.ShapeDtypeStruct((shard_rows, width), F32),
        scratch_shapes=[pltpu.VMEM((items, width), BF16), pltpu.VMEM((items, width), BF16)],
        compiler_params=pltpu.CompilerParams(vmem_limit_bytes=32 * 1024 * 1024),
    )(place, block, out_grad, received)


def spread(rows, axis_name, count):
    return lax.all_to_all(
        jnp.broadcast_to(rows[None], (count,) + rows.shape), axis_name, 0, 0, tiled=True
    )


def per_device_quarters(
    images, texts, section_weights, uniting_weights, codebooks, neg_bank, item_cats, cat_slot, neg_index
):
    segment_index = lax.axis_index("segment")
    segment_count = lax.axis_size("segment")
    dp_index = lax.axis_index("dp")
    dp_count = lax.axis_size("dp")
    item_count, _, image_width = images.shape
    text_width = texts.shape[2]
    first_rows = image_width + text_width
    shard_rows, width = uniting_weights.shape
    columns = width // segment_count
    groups = unit_groups(dp_count, shard_rows, first_rows, segment_count)
    place = jnp.stack([dp_index, segment_index]).astype(jnp.int32)
    message = weight_message(uniting_weights, place, groups, columns)
    pieces = [message] + [
        lax.ppermute(message, "dp", [(i, (i + turn) % dp_count) for i in range(dp_count)])
        for turn in range(1, dp_count)
    ]
    flag = (1 - segment_index % 2).astype(jnp.int32).reshape(1)
    pooled = pooled_features(images, texts, section_weights, segment_index, flag)
    pooled = pooled + lax.ppermute(pooled, "segment", [(i, i ^ 1) for i in range(segment_count)])
    mine = pooled.astype(BF16)
    other = lax.ppermute(mine, "segment", [(i, i ^ 2) for i in range(segment_count)])
    is_image = segment_index < 2
    embedded = jnp.concatenate(
        [jnp.where(is_image, mine, other)[:, :image_width], jnp.where(is_image, other, mine)], axis=1
    )
    embedded_all = spread(embedded, "dp", dp_count)

    pair = item_cats.shape[1] // dp_count
    cats = item_cats.reshape(segment_count, dp_count, pair).transpose(1, 0, 2).reshape(-1)
    items = cats.shape[0]
    slots = jnp.sum(
        jnp.where(cats[:, None] == jnp.arange(cat_slot.shape[0])[None, :], cat_slot[None, :], 0), axis=1
    )
    ids = jnp.arange(items)
    rank = jnp.sum(jnp.where((slots[None, :] == slots[:, None]) & (ids[None, :] < ids[:, None]), 1, 0), axis=1)
    owned = segment_count * CAP
    order = (ids[:, None] == (slots * owned + rank)[None, :]).astype(BF16)
    own = lax.dynamic_slice_in_dim(order, dp_index * owned, owned, 0)
    negatives = neg_index.reshape(segment_count, dp_count, pair, -1).transpose(1, 0, 2, 3).reshape(items, -1)
    own_negatives = jnp.dot(own.astype(F32), negatives.astype(F32), precision=highest)
    bank = neg_bank[0]
    bank_ids = jnp.arange(bank.shape[0]).astype(F32)
    counts = jnp.sum((own_negatives[:, :, None] == bank_ids[None, None, :]).astype(F32), axis=1)

    blocks, hidden, active, second, partial = merge_quarter(
        embedded_all, pieces, own, place, groups, first_rows, width
    )
    partial = partial + lax.ppermute(partial, "segment", [(i, i ^ 1) for i in range(segment_count)])
    merged = partial + lax.ppermute(partial, "segment", [(i, i ^ 2) for i in range(segment_count)])
    book_grad, merged_grad, loss = quantizer(merged, codebooks[0], bank, counts, 1.0 / math.sqrt(items))
    gathered = spread(merged_grad, "dp", dp_count)
    out_grad, sent = backward_quarter(gathered, order, hidden, active, second)
    received = lax.all_gather(sent, "segment", axis=0)
    block = lax.dynamic_index_in_dim(blocks, dp_index, 0, keepdims=False)
    uniting_grad = weight_grad(place, block, out_grad, received, groups)
    return (uniting_grad, book_grad[None], loss[0, :1])


def pooled_features(images, texts, section_weights, segment_index, flag):
    image_width, text_width = images.shape[2], texts.shape[2]

    def image_branch(operands):
        pooled = image_pooled(operands[0], operands[2], flag)
        return jnp.pad(pooled, ((0, 0), (0, text_width - image_width)))

    def text_branch(operands):
        return text_pooled(operands[1], operands[2], flag)

    return lax.cond(segment_index < 2, image_branch, text_branch, (images, texts, section_weights))


def per_device_gathered(
    images,
    texts,
    section_weights,
    uniting_weights,
    codebooks,
    neg_bank,
    item_cats,
    cat_slot,
    neg_index,
):
    segment_index = lax.axis_index("segment")
    segment_count = lax.axis_size("segment")
    dp_index = lax.axis_index("dp")
    dp_count = lax.axis_size("dp")
    group_index = segment_index % 2
    item_count = images.shape[0]

    flag = (1 - group_index).astype(jnp.int32).reshape(1)
    pooled = pooled_features(images, texts, section_weights, segment_index, flag)
    image_width = images.shape[2]
    is_image = segment_index < 2
    packed = jnp.concatenate(
        [jnp.where(is_image, pooled[:, :image_width], 0.0), jnp.where(is_image, 0.0, pooled)], axis=1
    )
    embedded = lax.psum_scatter(packed, "segment", scatter_dimension=0, tiled=True).astype(
        jnp.bfloat16
    )
    stacked = lax.all_gather(uniting_weights, "dp", axis=0, tiled=True)
    first_rows = embedded.shape[1]
    cat_per_dev = codebooks.shape[0]
    slot_count = cat_per_dev * CAP
    row_total = item_cats.shape[1]
    cats_all = item_cats.reshape(-1)
    entry_count = cats_all.shape[0]
    entry_ids = jnp.arange(entry_count)
    category_match = cats_all[:, None] == jnp.arange(cat_slot.shape[0])[None, :]
    entry_slots = jnp.sum(jnp.where(category_match, cat_slot[None, :], 0), axis=1)
    entry_owner = entry_slots // cat_per_dev
    entry_local = entry_slots % cat_per_dev
    entry_row = entry_ids // row_total
    earlier = entry_ids[None, :] < entry_ids[:, None]
    same_cat = (cats_all[:, None] == cats_all[None, :]) & (entry_row[:, None] == entry_row[None, :])
    entry_rank = jnp.sum(jnp.where(earlier & same_cat, 1, 0), axis=1)
    entry_place = entry_local * CAP + entry_rank
    entry_position = entry_row * slot_count + entry_place
    owned = entry_owner == dp_index
    all_slots = segment_count * slot_count
    slot_match_all = owned[None, :] & (entry_position[None, :] == jnp.arange(all_slots)[:, None])
    view_match = lax.dynamic_slice(
        slot_match_all,
        (segment_index * slot_count, segment_index * row_total),
        (slot_count, row_total),
    )
    view_base = segment_index * row_total
    view_slots = view_match.shape[0]
    selection = view_match.astype(jnp.bfloat16)
    valid = jnp.sum(view_match.astype(jnp.float32), axis=1)
    slot_item = jnp.sum(
        jnp.where(view_match, jnp.arange(view_match.shape[1])[None, :] + view_base, 0), axis=1
    )
    slot_negs = jnp.take(neg_index.reshape(entry_count, -1), slot_item, axis=0)
    slot_local = jnp.arange(view_slots) % slot_count // CAP
    bank_rows = neg_bank.reshape(-1, neg_bank.shape[2])
    negatives = jnp.take(bank_rows, slot_local[:, None] * neg_bank.shape[1] + slot_negs, axis=0)
    loss_scale = 1.0 / math.sqrt(dp_count * item_count)

    def owner_objective(merged_float, books):
        per_row = jax.vmap(item_loss)(merged_float, books[slot_local], negatives)
        return jnp.sum(per_row * valid) * loss_scale

    gathered = jnp.dot(
        selection,
        lax.all_gather(embedded, "dp", axis=0, tiled=True),
        preferred_element_type=jnp.float32,
    )
    gathered = gathered.astype(jnp.bfloat16)
    normed_all, hidden_all, activated_all, merged_all = merge_forward(gathered, stacked)
    loss_local, pullback = jax.vjp(owner_objective, merged_all.astype(jnp.float32), codebooks)
    grad_all, book_grad = pullback(jnp.ones((), jnp.float32))
    out_grad = grad_all.astype(jnp.bfloat16)
    hidden_grad = merge_backward(hidden_all, stacked, out_grad, first_rows)
    joined = jnp.concatenate([normed_all, activated_all], axis=1)
    book_total, loss_owner = lax.psum((book_grad, loss_local), "segment")
    shard_rows = uniting_weights.shape[0]
    shard_start = dp_index * shard_rows
    shard_first = shard_start + jnp.arange(shard_rows) < first_rows
    joined_piece = lax.all_gather(joined, "dp", axis=0, tiled=True)
    first_piece = lax.all_gather(hidden_grad, "dp", axis=0, tiled=True)
    second_piece = lax.all_gather(out_grad, "dp", axis=0, tiled=True)
    columns = lax.dynamic_slice_in_dim(joined_piece, shard_start, shard_rows, 1)
    segment_grad = stacked_term(columns, first_piece, second_piece, shard_first)
    uniting_grad = lax.psum(segment_grad, "segment")
    return (uniting_grad, book_total, loss_owner.reshape(1))


def per_device(*operands):
    images, texts, _, uniting_weights = operands[:4]
    segment_count, dp_count = lax.axis_size("segment"), lax.axis_size("dp")
    shard_rows = uniting_weights.shape[0]
    first_rows = images.shape[2] + texts.shape[2]
    groups = unit_groups(dp_count, shard_rows, first_rows, segment_count)
    whole_tiles = all(
        (shard_rows - inside) % (16 * segment_count) == 0 and inside % 16 == 0 for _, inside, _, _ in groups
    )
    if whole_tiles:
        return per_device_quarters(*operands)
    return per_device_gathered(*operands)


def solution(mesh):
    placed = (
        P("dp", None, None),
        P("dp", None, None),
        P("segment", None, None),
        P("dp", None),
        P("dp", None, None, None),
        P("dp", None, None),
        P(),
        P(),
        P(),
    )
    return jax.shard_map(
        per_device,
        mesh=mesh,
        in_specs=placed,
        out_specs=(P("dp", None), P("dp", None, None, None), P("dp")),
        check_vma=False,
    )
```

```python
import functools
import math

import jax
import jax.numpy as jnp
import numpy as np
from jax import lax
from jax.experimental import pallas as pl
from jax.experimental.pallas import tpu as pltpu
from jax.sharding import PartitionSpec as P

F32 = jnp.float32
BF16 = jnp.bfloat16

HEAD_IMG = 64
HEAD_TXT = 128
CAP = 2
SIDES = 2
TILE = 16


norm_eps = 1e-06
rope_theta = 1000000.0
contrast_temp = 0.1
beta_weight = 1.0
highest = lax.Precision.HIGHEST


def gelu_value(inputs_f):
    return 0.5 * inputs_f * (1.0 + lax.erf(inputs_f / math.sqrt(2.0)))


def gelu_slope(inputs_f):
    return 0.5 * (1.0 + lax.erf(inputs_f / math.sqrt(2.0))) + inputs_f * jnp.exp(
        -0.5 * inputs_f * inputs_f
    ) / math.sqrt(2.0 * math.pi)


def dot_nt(a, b):
    return lax.dot_general(a, b, (((1,), (1,)), ((), ())), preferred_element_type=F32)

def dot_nn(a, b):
    return jnp.dot(a, b, preferred_element_type=F32)

def two_parts(value):
    high = value.astype(BF16)
    return jnp.concatenate([high, (value - high.astype(F32)).astype(BF16)], axis=0)

def dot_two(value, weights):
    rows = value.shape[0]
    both = dot_nn(two_parts(value), weights)
    return both[:rows] + both[rows:]

def unfold(slot_ref, first, out_ref, wide_ref, row_step):
    rows, columns = out_ref.shape
    blocks = columns // 128
    def body(step, carry):
        start = pl.multiple_of(step * row_step, row_step)
        source = pl.multiple_of(first + step * (row_step * blocks), 16)
        wide_ref[0 : row_step * blocks, :] = slot_ref[0, pl.ds(source, row_step * blocks), :].astype(F32)
        for block in range(blocks):
            piece = wide_ref[pl.ds(block, row_step, stride=blocks), :]
            out_ref[pl.ds(start, row_step), block * 128 : (block + 1) * 128] = piece.astype(BF16)
        return carry
    lax.fori_loop(0, rows // row_step, body, 0)

def image_kernel(flag_ref, image_ref, slot_ref, pooled_ref, w_in, w_out, wide, heads_mean):
    step = pl.program_id(0)
    item_count, model_width = pooled_ref.shape
    half_width = model_width // 2
    head_count = half_width // HEAD_IMG
    patch_count = image_ref.shape[1]

    @pl.when(step == 0)
    def _():
        unfold(slot_ref, 0, w_in, wide, 128)
        unfold(slot_ref, model_width * 12, w_out, wide, 128)

    tokens = image_ref[0].astype(F32)
    centred = tokens - jnp.mean(tokens, axis=1, keepdims=True)
    variance = jnp.mean(centred * centred, axis=1, keepdims=True)
    normed = (centred * lax.rsqrt(variance + norm_eps)).astype(BF16)
    queries = (dot_nn(normed, w_in[:, :half_width]).astype(BF16) * (1.0 / math.sqrt(HEAD_IMG))).astype(BF16)
    keys = dot_nn(normed, w_in[:, half_width : 2 * half_width]).astype(BF16)
    row_ids = lax.broadcasted_iota(jnp.int32, (head_count, patch_count), 0)
    weights = jnp.zeros((head_count, patch_count), F32)
    for head in range(head_count):
        span = slice(head * HEAD_IMG, (head + 1) * HEAD_IMG)
        scores = dot_nt(keys[:, span], queries[:, span])
        exps = jnp.exp(scores - jnp.max(scores, axis=0, keepdims=True))
        share = (1.0 / patch_count) / jnp.sum(exps, axis=0, keepdims=True)
        share = jnp.where(row_ids == head, share, 0.0).astype(BF16)
        weights = weights + dot_nt(share, exps.astype(BF16))
    heads_mean[pl.ds(step * head_count, head_count), :] = dot_two(weights, normed)
    residual = jnp.mean(tokens, axis=0, keepdims=True) * flag_ref[0].astype(F32)
    pooled_ref[pl.ds(step, 1), :] = residual

    @pl.when(step == item_count - 1)
    def _():
        values = dot_two(heads_mean[...], w_in[:, 2 * half_width :])
        rows = lax.broadcasted_iota(jnp.int32, values.shape, 0)
        columns = lax.broadcasted_iota(jnp.int32, values.shape, 1)
        values = jnp.where(rows % head_count == columns // HEAD_IMG, values, 0.0)
        attended = jnp.sum(values.reshape(item_count, head_count, half_width), axis=1)
        pooled_ref[...] += dot_two(attended, w_out[...])

def image_pooled(images, slot, flag):
    item_count, patch_count, model_width = images.shape
    half_width = model_width // 2
    head_count = half_width // HEAD_IMG
    return pl.pallas_call(
        image_kernel,
        grid=(item_count,),
        in_specs=[
            pl.BlockSpec(memory_space=pltpu.SMEM),
            pl.BlockSpec((1, patch_count, model_width), lambda i: (i, 0, 0)),
            pl.BlockSpec((1, 16 * model_width, 128), lambda i: (0, 0, 0), pipeline_mode=pl.Buffered(1)),
        ],
        out_specs=pl.BlockSpec((item_count, model_width), lambda i: (0, 0)),
        out_shape=jax.ShapeDtypeStruct((item_count, model_width), F32),
        scratch_shapes=[
            pltpu.VMEM((model_width, 3 * half_width), BF16),
            pltpu.VMEM((half_width, model_width), BF16),
            pltpu.VMEM((128 * 12, 128), F32),
            pltpu.VMEM((item_count * head_count, model_width), F32),
        ],
        compiler_params=pltpu.CompilerParams(vmem_limit_bytes=40 * 1024 * 1024),
    )(flag, images, slot)

def rope_tables(tokens, repeats):
    half = HEAD_TXT // 2
    exponents = np.arange(half).astype(np.float32) * np.float32(2.0 / HEAD_TXT)
    inverse = np.exp(np.float32(-math.log(rope_theta)) * exponents).astype(np.float32)
    angles = (np.arange(tokens).astype(np.float32)[:, None] * inverse[None, :]).astype(np.float32)
    cosine = np.concatenate([np.cos(angles), np.cos(angles)], axis=1)
    sine = np.concatenate([-np.sin(angles), np.sin(angles)], axis=1)
    return np.tile(cosine, (repeats, 1)).astype(np.float32), np.tile(sine, (repeats, 1)).astype(np.float32)

def text_kernel(flag_ref, text_ref, slot_ref, cos_ref, sin_ref, pooled_ref, w_in, w_out, wide, heads_mean):
    item_count, token_count, model_width = text_ref.shape
    half_width = model_width // 2
    head_count = half_width // HEAD_TXT
    unfold(slot_ref, 0, w_in, wide, 128)
    unfold(slot_ref, model_width * 8, w_out, wide, 128)
    tokens = text_ref[...].reshape(item_count * token_count, model_width).astype(F32)
    normed = (tokens * lax.rsqrt(jnp.mean(tokens * tokens, axis=1, keepdims=True) + norm_eps)).astype(BF16)
    residual = jnp.mean(tokens.reshape(item_count, token_count, model_width), axis=1)
    cosine, sine = cos_ref[...], sin_ref[...]

    def head_columns(head):
        return dot_nn(normed, w_in[:, head * HEAD_TXT : (head + 1) * HEAD_TXT])

    def turned(head, scale):
        part = head_columns(head)
        return ((part * cosine + pltpu.roll(part, HEAD_TXT // 2, 1) * sine).astype(BF16)).astype(F32) * scale

    queries = [(turned(head, 1.0)).astype(BF16) for head in range(head_count)]
    keys = turned(head_count, 1.0).astype(BF16)
    values = head_columns(head_count + 1).astype(BF16)
    wide_columns = head_count * token_count
    key_ids = lax.broadcasted_iota(jnp.int32, (token_count, wide_columns), 0)
    query_ids = lax.broadcasted_iota(jnp.int32, (token_count, wide_columns), 1) % token_count
    allowed = key_ids <= query_ids
    own_head = lax.broadcasted_iota(jnp.int32, (8, wide_columns), 0) == (
        lax.broadcasted_iota(jnp.int32, (8, wide_columns), 1) // token_count
    )
    for item in range(item_count):
        span = slice(item * token_count, (item + 1) * token_count)
        asked = jnp.concatenate([query[span] for query in queries], axis=0)
        scores = dot_nt(keys[span], asked) * (1.0 / math.sqrt(HEAD_TXT))
        scores = jnp.where(allowed, scores, -1e30)
        exps = jnp.exp(scores - jnp.max(scores, axis=0, keepdims=True))
        share = (1.0 / token_count) / jnp.sum(exps, axis=0, keepdims=True)
        share = jnp.where(own_head, share, 0.0).astype(BF16)
        weights = dot_nt(share, exps.astype(BF16))
        heads_mean[:, item, :] = dot_two(weights, values[span])
    pooled = residual * flag_ref[0].astype(F32)
    for head in range(head_count):
        pooled = pooled + dot_two(heads_mean[head], w_out[head * HEAD_TXT : (head + 1) * HEAD_TXT, :])
    pooled_ref[...] = pooled

def text_pooled(texts, slot, flag):
    item_count, token_count, model_width = texts.shape
    half_width = model_width // 2
    inner = half_width + 2 * HEAD_TXT
    cosine, sine = rope_tables(token_count, item_count)
    vm = pl.BlockSpec(memory_space=pltpu.VMEM)
    return pl.pallas_call(
        text_kernel,
        in_specs=[pl.BlockSpec(memory_space=pltpu.SMEM)] + [vm] * 4,
        out_specs=vm,
        out_shape=jax.ShapeDtypeStruct((item_count, model_width), F32),
        scratch_shapes=[
            pltpu.VMEM((model_width, inner), BF16),
            pltpu.VMEM((half_width, model_width), BF16),
            pltpu.VMEM((128 * 12, 128), F32),
            pltpu.VMEM((8, item_count, HEAD_TXT), F32),
        ],
        compiler_params=pltpu.CompilerParams(vmem_limit_bytes=40 * 1024 * 1024),
    )(flag, texts, slot, jnp.asarray(cosine), jnp.asarray(sine))

def merge_forward(embedded, stacked):
    first_rows = embedded.shape[1]
    float_embed = embedded.astype(jnp.float32)
    normed = (
        float_embed
        * lax.rsqrt(jnp.mean(float_embed * float_embed, axis=1, keepdims=True) + norm_eps)
    ).astype(jnp.bfloat16)
    hidden = jnp.dot(normed, stacked[:first_rows], preferred_element_type=jnp.float32)
    activated = gelu_value(hidden).astype(jnp.bfloat16)
    merged = jnp.dot(activated, stacked[first_rows:], preferred_element_type=jnp.float32).astype(
        jnp.bfloat16
    )
    return (normed, hidden, activated, merged)


def merge_backward(hidden, stacked, out_grad, first_rows):
    w_second = stacked[first_rows:]
    act_grad = lax.dot_general(
        out_grad, w_second, (((1,), (1,)), ((), ())), preferred_element_type=jnp.float32
    )
    return (act_grad * gelu_slope(hidden)).astype(jnp.bfloat16)


def item_loss(merged_row, book_rows, negatives):
    emb_width = merged_row.shape[0]
    quant_tau = math.sqrt(emb_width) / 2.0
    residual = merged_row * lax.rsqrt(jnp.mean(merged_row * merged_row) + norm_eps)
    quantized = jnp.zeros_like(merged_row)
    for level_index in range(book_rows.shape[0]):
        code_rows = book_rows[level_index]
        cross_terms = jnp.dot(code_rows, residual, precision=highest)
        logits = (2.0 * cross_terms - jnp.sum(code_rows * code_rows, axis=1)) / quant_tau
        logits = logits - lax.stop_gradient(jnp.max(logits))
        exp_logits = jnp.exp(logits)
        chosen = jnp.dot(exp_logits / jnp.sum(exp_logits), code_rows, precision=highest)
        residual = residual - chosen
        quantized = quantized + chosen
    recon_error = jnp.mean(residual * residual)
    anchor = quantized * lax.rsqrt(jnp.mean(quantized * quantized) + norm_eps)
    candidates = jnp.concatenate([merged_row[None, :], negatives.astype(jnp.float32)], axis=0)
    cand_unit = candidates * lax.rsqrt(
        jnp.mean(candidates * candidates, axis=1, keepdims=True) + norm_eps
    )
    similarity = jnp.dot(cand_unit, anchor, precision=highest) / (emb_width * contrast_temp)
    top_score = lax.stop_gradient(jnp.max(similarity))
    contrast = top_score + jnp.log(jnp.sum(jnp.exp(similarity - top_score))) - similarity[0]
    return contrast + beta_weight * recon_error


def stacked_term(columns, first_grad, second_grad, in_first):
    contract = (((0,), (0,)), ((), ()))
    first_term = lax.dot_general(columns, first_grad, contract, preferred_element_type=jnp.float32)
    second_term = lax.dot_general(
        columns, second_grad, contract, preferred_element_type=jnp.float32
    )
    return jnp.where(in_first[:, None], first_term, second_term)


def first_rows_in(shard, shard_rows, first_rows):
    return min(max(first_rows - shard * shard_rows, 0), shard_rows)


def unit_groups(shard_count, shard_rows, first_rows, segment_count):
    shards = []
    for shard in range(shard_count):
        inside = first_rows_in(shard, shard_rows, first_rows)
        if inside < shard_rows:
            shards.append((shard, inside, shard * shard_rows + inside - first_rows, shard_rows - inside))
    tiles = [rows // (TILE * segment_count) for _, _, _, rows in shards]
    room = sum(tiles) // SIDES
    taken = [count // SIDES for count in tiles]
    for index, count in enumerate(tiles):
        if count % SIDES and sum(taken) < room:
            taken[index] += 1
    sides = [taken, [count - mine for count, mine in zip(tiles, taken)]]
    groups = []
    for index, (shard, inside, base, _) in enumerate(shards):
        starts, shares, start = [], [], 0
        for side in range(SIDES):
            share = sides[side][index] * TILE
            starts.append(start)
            shares.append(share)
            start += share * segment_count
        groups.append((shard, inside, base, tuple(starts), tuple(shares)))
    return groups


def even_units(groups, shard_rows, segment_count, width):
    return all(
        inside % TILE == 0 and sum(shares) * segment_count == shard_rows - inside and min(shares) > 0
        for _, inside, _, _, shares in groups
    ) and all(sum(group[4][side] for group in groups) * segment_count * SIDES == width for side in range(SIDES))


def piece_rows(groups, shard_rows, width, columns):
    return max([shard_rows] + [inside + width // columns * max(shares) for _, inside, _, _, shares in groups])


def message_kernel(groups, place_ref, rows_ref, message_ref):
    shard, segment = place_ref[0], place_ref[1]
    row_count, width = rows_ref.shape
    copies, _, columns = message_ref.shape
    first_last = groups[0][0]

    @pl.when(shard <= first_last)
    def _():
        wanted = lax.broadcasted_iota(jnp.int32, (width, SIDES * columns), 1)
        unit = jnp.zeros_like(wanted)
        offset = 0
        for side in range(SIDES):
            for _, _, base, starts, shares in groups:
                inside = (wanted >= offset) & (wanted < offset + shares[side])
                unit = jnp.where(inside, wanted - offset + base + starts[side] + shares[side] * segment, unit)
                offset += shares[side]
        chosen = (lax.broadcasted_iota(jnp.int32, (width, SIDES * columns), 0) == unit).astype(F32).astype(BF16)
        message = dot_nn(rows_ref[...], chosen).astype(BF16)
        for copy in range(copies):
            side = copy % SIDES
            message_ref[copy, :row_count, :] = message[:, side * columns : (side + 1) * columns]

    for group_shard, inside, _, starts, shares in groups:

        @pl.when(shard == group_shard)
        def _(inside=inside, starts=starts, shares=shares):
            for side in range(SIDES):
                share = shares[side]
                start = pl.multiple_of(inside + starts[side] + share * segment, TILE)
                for block in range(width // columns):
                    piece = rows_ref[pl.ds(start, share), block * columns : (block + 1) * columns]
                    for copy in range(side, copies, SIDES):
                        message_ref[copy, inside + block * share : inside + (block + 1) * share, :] = piece


def weight_message(uniting_weights, place, groups, copies, columns):
    shard_rows, width = uniting_weights.shape
    vm = pl.BlockSpec(memory_space=pltpu.VMEM)
    return pl.pallas_call(
        functools.partial(message_kernel, groups),
        in_specs=[pl.BlockSpec(memory_space=pltpu.SMEM), vm],
        out_specs=vm,
        out_shape=jax.ShapeDtypeStruct((copies, piece_rows(groups, shard_rows, width, columns), columns), BF16),
    )(place, uniting_weights)


def forward_kernel(
    groups,
    first_rows,
    place_ref,
    embedded_ref,
    own_ref,
    weights,
    blocks_ref,
    hidden_ref,
    active_ref,
    second_ref,
    partial_ref,
):
    shard_count, _, columns = weights.shape
    shard_rows = blocks_ref.shape[2]
    source_count, source_items, width = embedded_ref.shape
    items = source_count * source_items
    embedded = embedded_ref[...].astype(F32).reshape(items, width)
    normed = embedded * lax.rsqrt(jnp.mean(embedded * embedded, axis=1, keepdims=True) + norm_eps)
    normed = normed.astype(BF16)
    hidden = jnp.zeros((items, columns), F32)
    for block in range(shard_count):
        inside = first_rows_in(block, shard_rows, first_rows)
        start = block * shard_rows
        if inside > 0:
            rows = normed[:, start : start + inside]
            hidden = hidden + dot_nn(rows, weights[block, :inside])
            if inside < shard_rows:
                rows = jnp.concatenate([rows, jnp.zeros((items, shard_rows - inside), BF16)], axis=1)
            blocks_ref[block] = rows
        else:
            blocks_ref[block] = jnp.zeros((items, shard_rows), BF16)
    hidden_ref[...] = hidden
    active = gelu_value(hidden).astype(BF16)
    active_ref[...] = active
    for side in range(SIDES):

        @pl.when(lax.rem(place_ref[0], SIDES) == side)
        def _(side=side):
            offset = 0
            for block, inside, _, _, shares in groups:
                share = shares[side]
                for part in range(partial_ref.shape[1] // columns):
                    second_ref[offset : offset + share, part * columns : (part + 1) * columns] = weights[
                        block, inside + part * share : inside + (part + 1) * share, :
                    ]
                offset += share

    partial_ref[...] = dot_nn(dot_nn(own_ref[...], active).astype(BF16), second_ref[...])


def merge_part(embedded_all, pieces, own, place, groups, shard_rows, first_rows, width):
    shard_count, _, columns = pieces.shape
    items = embedded_all.shape[0] * embedded_all.shape[1]
    vm = pl.BlockSpec(memory_space=pltpu.VMEM)
    return pl.pallas_call(
        functools.partial(forward_kernel, groups, first_rows),
        in_specs=[pl.BlockSpec(memory_space=pltpu.SMEM), vm, vm, vm],
        out_specs=[vm] * 5,
        out_shape=[
            jax.ShapeDtypeStruct((shard_count, items, shard_rows), BF16),
            jax.ShapeDtypeStruct((items, columns), F32),
            jax.ShapeDtypeStruct((items, columns), BF16),
            jax.ShapeDtypeStruct((columns, width), BF16),
            jax.ShapeDtypeStruct((own.shape[0], width), F32),
        ],
        compiler_params=pltpu.CompilerParams(vmem_limit_bytes=32 * 1024 * 1024),
    )(place, embedded_all, own, pieces)


def split(value):
    high = value.astype(BF16)
    return high, (value - high.astype(F32)).astype(BF16)


def exact_nt(value, high, low):
    first, second = split(value)
    rows = value.shape[0]
    both = dot_nt(jnp.concatenate([first, second], axis=0), high)
    return both[:rows] + both[rows:] + dot_nt(first, low)


def exact_nn(value, high, low):
    first, second = split(value)
    rows = value.shape[0]
    both = dot_nn(jnp.concatenate([first, second], axis=0), high)
    return both[:rows] + both[rows:] + dot_nn(first, low)


def dot_tn(a, b):
    return lax.dot_general(a, b, (((0,), (0,)), ((), ())), preferred_element_type=F32)


def exact_tn(a, b):
    a_high, a_low = split(a)
    b_high, b_low = split(b)
    return dot_tn(
        jnp.concatenate([a_high, a_low, a_high], axis=0), jnp.concatenate([b_high, b_high, b_low], axis=0)
    )


def square_sums(value):
    high, low = split(value * value)
    ones = jnp.ones((8, value.shape[1]), BF16)
    return (dot_nt(ones, high) + dot_nt(ones, low))[:1]


def quantizer_kernel(loss_scale, merged_ref, book_ref, bank_ref, count_ref, book_grad_ref, merged_grad_ref, loss_ref, highs, lows):
    width = merged_ref.shape[1]
    levels = book_ref.shape[0]
    inverse_tau = 2.0 / math.sqrt(width)
    inverse_temp = 1.0 / (width * contrast_temp)
    merged = merged_ref[...].astype(BF16).astype(F32)
    merged_scale = lax.rsqrt(jnp.mean(merged * merged, axis=1, keepdims=True) + norm_eps)
    residuals = [merged * merged_scale]
    shares, chosen_rows = [], []
    for level in range(levels):
        codes = book_ref[level]
        high, low = split(codes)
        highs[level] = high
        lows[level] = low
        logits = (2.0 * exact_nt(residuals[level], high, low) - square_sums(codes)) * inverse_tau
        exps = jnp.exp(logits - jnp.max(logits, axis=1, keepdims=True))
        share = exps / jnp.sum(exps, axis=1, keepdims=True)
        chosen = exact_nn(share, high, low)
        shares.append(share)
        chosen_rows.append(chosen)
        residuals.append(residuals[level] - chosen)
    last = residuals[levels]
    quantized = chosen_rows[0]
    for chosen in chosen_rows[1:]:
        quantized = quantized + chosen
    anchor_scale = lax.rsqrt(jnp.mean(quantized * quantized, axis=1, keepdims=True) + norm_eps)
    anchor = quantized * anchor_scale
    own = jnp.sum(anchor * residuals[0], axis=1, keepdims=True) * inverse_temp
    bank = bank_ref[...]
    bank_wide = bank.astype(F32)
    bank_scale = lax.rsqrt(square_sums(bank_wide) * (1.0 / width) + norm_eps)
    anchor_parts = jnp.concatenate(split(anchor), axis=0)
    rows = anchor.shape[0]
    both = dot_nt(anchor_parts, bank)
    similar = (both[:rows] + both[rows:]) * bank_scale * inverse_temp
    counts = count_ref[...]
    named = counts > 0.0
    top = jnp.maximum(jnp.max(jnp.where(named, similar, own), axis=1, keepdims=True), own)
    bank_exps = jnp.where(named, jnp.exp(jnp.where(named, similar, top) - top), 0.0) * counts
    own_exp = jnp.exp(own - top)
    total = jnp.sum(bank_exps, axis=1, keepdims=True) + own_exp
    item_losses = top + jnp.log(total) - own + jnp.mean(last * last, axis=1, keepdims=True)
    loss_ref[...] = jnp.broadcast_to(jnp.sum(item_losses, axis=0, keepdims=True) * loss_scale, loss_ref.shape)

    bank_weight = bank_exps / total * (loss_scale * inverse_temp)
    own_weight = (own_exp / total - 1.0) * (loss_scale * inverse_temp)
    weight_parts = jnp.concatenate(split(bank_weight * bank_scale), axis=0)
    both = dot_nn(weight_parts, bank)
    anchor_grad = both[:rows] + both[rows:] + own_weight * residuals[0]
    unit_grad = own_weight * anchor
    quantized_grad = anchor_scale * (anchor_grad - anchor * jnp.mean(anchor * anchor_grad, axis=1, keepdims=True))
    residual_grad = last * (2.0 * loss_scale / width)
    ones = jnp.ones((rows, 128), F32)
    for level in reversed(range(levels)):
        high, low = highs[level], lows[level]
        chosen_grad = quantized_grad - residual_grad
        share_grad = exact_nt(chosen_grad, high, low)
        share = shares[level]
        logit_grad = share * (share_grad - jnp.sum(share * share_grad, axis=1, keepdims=True)) * (2.0 * inverse_tau)
        book_part = exact_tn(
            jnp.concatenate([share, logit_grad], axis=0), jnp.concatenate([chosen_grad, residuals[level]], axis=0)
        )
        totals = exact_tn(logit_grad, ones)
        for block in range(width // 128):
            span = slice(block * 128, (block + 1) * 128)
            book_grad_ref[level, :, span] = book_part[:, span] - totals * book_ref[level, :, span]
        residual_grad = residual_grad + exact_nn(logit_grad, high, low)
    unit_grad = unit_grad + residual_grad
    unit = residuals[0]
    merged_grad = merged_scale * (unit_grad - unit * jnp.mean(unit * unit_grad, axis=1, keepdims=True))
    merged_grad_ref[...] = merged_grad.astype(BF16)


def quantizer(merged, books, bank, counts, loss_scale):
    vm = pl.BlockSpec(memory_space=pltpu.VMEM)
    return pl.pallas_call(
        functools.partial(quantizer_kernel, loss_scale),
        in_specs=[vm] * 4,
        out_specs=[vm] * 3,
        out_shape=[
            jax.ShapeDtypeStruct(books.shape, F32),
            jax.ShapeDtypeStruct(merged.shape, BF16),
            jax.ShapeDtypeStruct((8, 128), F32),
        ],
        scratch_shapes=[pltpu.VMEM(books.shape, BF16), pltpu.VMEM(books.shape, BF16)],
        compiler_params=pltpu.CompilerParams(vmem_limit_bytes=32 * 1024 * 1024),
    )(merged, books, bank, counts)


def backward_kernel(gathered_ref, order_ref, hidden_ref, active_ref, second_ref, out_grad_ref, sent_ref):
    owners, places, width = gathered_ref.shape
    columns = hidden_ref.shape[1]
    gathered = gathered_ref[...].astype(F32).reshape(owners * places, width).astype(BF16)
    out_grad = dot_tn(order_ref[...], gathered).astype(BF16)
    out_grad_ref[...] = out_grad
    hidden_grad = dot_nt(out_grad, second_ref[...]) * gelu_slope(hidden_ref[...])
    sent_ref[:, :columns] = hidden_grad.astype(BF16)
    sent_ref[:, columns:] = active_ref[...]


def backward_part(gathered, order, hidden, active, second):
    items, columns = hidden.shape
    vm = pl.BlockSpec(memory_space=pltpu.VMEM)
    return pl.pallas_call(
        backward_kernel,
        in_specs=[vm] * 5,
        out_specs=[vm] * 2,
        out_shape=[
            jax.ShapeDtypeStruct((items, gathered.shape[2]), BF16),
            jax.ShapeDtypeStruct((items, 2 * columns), BF16),
        ],
        compiler_params=pltpu.CompilerParams(vmem_limit_bytes=32 * 1024 * 1024),
    )(gathered, order, hidden, active, second)


def weight_grad_kernel(
    groups, place_ref, block_ref, out_grad_ref, near_ref, across_ref, grad_ref, hidden_grad, active
):
    shard = place_ref[0]
    segment_count, items, doubled = near_ref.shape
    columns = doubled // 2
    shard_rows = block_ref.shape[1]
    here = lax.rem(shard, SIDES)

    def place_units(target, first):
        for side in range(SIDES):
            for segment in range(segment_count):
                near = near_ref[segment, :, first : first + columns]
                across = across_ref[segment, :, first : first + columns]
                part = jnp.where(here == side, near, across)
                offset = 0
                for _, _, base, starts, shares in groups:
                    spot = base + starts[side] + shares[side] * segment
                    target[:, spot : spot + shares[side]] = part[:, offset : offset + shares[side]]
                    offset += shares[side]

    place_units(hidden_grad, 0)
    grad_ref[...] = dot_tn(block_ref[...], hidden_grad[...])
    for group_shard, inside, base, _, _ in groups:

        @pl.when(shard == group_shard)
        def _(inside=inside, base=base):
            place_units(active, columns)
            wanted = active[:, base : base + shard_rows - inside]
            grad_ref[inside:, :] = dot_tn(wanted, out_grad_ref[...])


def weight_grad(place, block, out_grad, near, across, groups):
    items, shard_rows = block.shape
    width = out_grad.shape[1]
    vm = pl.BlockSpec(memory_space=pltpu.VMEM)
    return pl.pallas_call(
        functools.partial(weight_grad_kernel, groups),
        in_specs=[pl.BlockSpec(memory_space=pltpu.SMEM)] + [vm] * 4,
        out_specs=vm,
        out_shape=jax.ShapeDtypeStruct((shard_rows, width), F32),
        scratch_shapes=[pltpu.VMEM((items, width), BF16), pltpu.VMEM((items, width), BF16)],
        compiler_params=pltpu.CompilerParams(vmem_limit_bytes=32 * 1024 * 1024),
    )(place, block, out_grad, near, across)


def spread(rows, axis_name, count):
    return lax.all_to_all(
        jnp.broadcast_to(rows[None], (count,) + rows.shape), axis_name, 0, 0, tiled=True
    )


def per_device_parts(
    images, texts, section_weights, uniting_weights, codebooks, neg_bank, item_cats, cat_slot, neg_index
):
    segment_index = lax.axis_index("segment")
    segment_count = lax.axis_size("segment")
    dp_index = lax.axis_index("dp")
    dp_count = lax.axis_size("dp")
    item_count, _, image_width = images.shape
    text_width = texts.shape[2]
    first_rows = image_width + text_width
    shard_rows, width = uniting_weights.shape
    columns = width // (SIDES * segment_count)
    groups = unit_groups(dp_count, shard_rows, first_rows, segment_count)
    place = jnp.stack([dp_index, segment_index]).astype(jnp.int32)
    message = weight_message(uniting_weights, place, groups, dp_count, columns)
    pieces = lax.all_to_all(message, "dp", 0, 0, tiled=True)
    flag = (1 - segment_index % 2).astype(jnp.int32).reshape(1)
    pooled = pooled_features(images, texts, section_weights, segment_index, flag)
    pooled = pooled + lax.ppermute(pooled, "segment", [(i, i ^ 1) for i in range(segment_count)])
    mine = pooled.astype(BF16)
    other = lax.ppermute(mine, "segment", [(i, i ^ 2) for i in range(segment_count)])
    is_image = segment_index < 2
    embedded = jnp.concatenate(
        [jnp.where(is_image, mine, other)[:, :image_width], jnp.where(is_image, other, mine)], axis=1
    )
    embedded, pieces = lax.optimization_barrier((embedded, pieces))
    embedded_all = spread(embedded, "dp", dp_count)

    pair = item_cats.shape[1] // dp_count
    cats = item_cats.reshape(segment_count, dp_count, pair).transpose(1, 0, 2).reshape(-1)
    items = cats.shape[0]
    slots = jnp.sum(
        jnp.where(cats[:, None] == jnp.arange(cat_slot.shape[0])[None, :], cat_slot[None, :], 0), axis=1
    )
    ids = jnp.arange(items)
    rank = jnp.sum(jnp.where((slots[None, :] == slots[:, None]) & (ids[None, :] < ids[:, None]), 1, 0), axis=1)
    owned = segment_count * CAP
    order = (ids[:, None] == (slots * owned + rank)[None, :]).astype(BF16)
    own = lax.dynamic_slice_in_dim(order, dp_index * owned, owned, 0)
    across_own = lax.dynamic_slice_in_dim(order, (dp_index ^ 1) * owned, owned, 0)
    both_own = jnp.concatenate([own, across_own], axis=0)
    negatives = neg_index.reshape(segment_count, dp_count, pair, -1).transpose(1, 0, 2, 3).reshape(items, -1)
    own_negatives = jnp.dot(own.astype(F32), negatives.astype(F32), precision=highest)
    bank = neg_bank[0]
    bank_ids = jnp.arange(bank.shape[0]).astype(F32)
    counts = jnp.sum((own_negatives[:, :, None] == bank_ids[None, None, :]).astype(F32), axis=1)

    blocks, hidden, active, second, partial = merge_part(
        embedded_all, pieces, both_own, place, groups, shard_rows, first_rows, width
    )
    partial = partial + lax.ppermute(partial, "segment", [(i, i ^ 1) for i in range(segment_count)])
    partial = partial + lax.ppermute(partial, "segment", [(i, i ^ 2) for i in range(segment_count)])
    merged = partial[:owned] + lax.ppermute(partial[owned:], "dp", [(i, i ^ 1) for i in range(dp_count)])
    book_grad, merged_grad, loss = quantizer(merged, codebooks[0], bank, counts, 1.0 / math.sqrt(items))
    gathered = spread(merged_grad, "dp", dp_count)
    out_grad, sent = backward_part(gathered, order, hidden, active, second)
    near = lax.all_gather(sent, "segment", axis=0)
    across = lax.ppermute(near, "dp", [(i, i ^ 1) for i in range(dp_count)])
    block = lax.dynamic_index_in_dim(blocks, dp_index, 0, keepdims=False)
    uniting_grad = weight_grad(place, block, out_grad, near, across, groups)
    return (uniting_grad, book_grad[None], loss[0, :1])


def pooled_features(images, texts, section_weights, segment_index, flag):
    image_width, text_width = images.shape[2], texts.shape[2]

    def image_branch(operands):
        pooled = image_pooled(operands[0], operands[2], flag)
        return jnp.pad(pooled, ((0, 0), (0, text_width - image_width)))

    def text_branch(operands):
        return text_pooled(operands[1], operands[2], flag)

    return lax.cond(segment_index < 2, image_branch, text_branch, (images, texts, section_weights))


def per_device_gathered(
    images,
    texts,
    section_weights,
    uniting_weights,
    codebooks,
    neg_bank,
    item_cats,
    cat_slot,
    neg_index,
):
    segment_index = lax.axis_index("segment")
    segment_count = lax.axis_size("segment")
    dp_index = lax.axis_index("dp")
    dp_count = lax.axis_size("dp")
    group_index = segment_index % 2
    item_count = images.shape[0]

    flag = (1 - group_index).astype(jnp.int32).reshape(1)
    pooled = pooled_features(images, texts, section_weights, segment_index, flag)
    image_width = images.shape[2]
    is_image = segment_index < 2
    packed = jnp.concatenate(
        [jnp.where(is_image, pooled[:, :image_width], 0.0), jnp.where(is_image, 0.0, pooled)], axis=1
    )
    embedded = lax.psum_scatter(packed, "segment", scatter_dimension=0, tiled=True).astype(
        jnp.bfloat16
    )
    stacked = lax.all_gather(uniting_weights, "dp", axis=0, tiled=True)
    first_rows = embedded.shape[1]
    cat_per_dev = codebooks.shape[0]
    slot_count = cat_per_dev * CAP
    row_total = item_cats.shape[1]
    cats_all = item_cats.reshape(-1)
    entry_count = cats_all.shape[0]
    entry_ids = jnp.arange(entry_count)
    category_match = cats_all[:, None] == jnp.arange(cat_slot.shape[0])[None, :]
    entry_slots = jnp.sum(jnp.where(category_match, cat_slot[None, :], 0), axis=1)
    entry_owner = entry_slots // cat_per_dev
    entry_local = entry_slots % cat_per_dev
    entry_row = entry_ids // row_total
    earlier = entry_ids[None, :] < entry_ids[:, None]
    same_cat = (cats_all[:, None] == cats_all[None, :]) & (entry_row[:, None] == entry_row[None, :])
    entry_rank = jnp.sum(jnp.where(earlier & same_cat, 1, 0), axis=1)
    entry_place = entry_local * CAP + entry_rank
    entry_position = entry_row * slot_count + entry_place
    owned = entry_owner == dp_index
    all_slots = segment_count * slot_count
    slot_match_all = owned[None, :] & (entry_position[None, :] == jnp.arange(all_slots)[:, None])
    view_match = lax.dynamic_slice(
        slot_match_all,
        (segment_index * slot_count, segment_index * row_total),
        (slot_count, row_total),
    )
    view_base = segment_index * row_total
    view_slots = view_match.shape[0]
    selection = view_match.astype(jnp.bfloat16)
    valid = jnp.sum(view_match.astype(jnp.float32), axis=1)
    slot_item = jnp.sum(
        jnp.where(view_match, jnp.arange(view_match.shape[1])[None, :] + view_base, 0), axis=1
    )
    slot_negs = jnp.take(neg_index.reshape(entry_count, -1), slot_item, axis=0)
    slot_local = jnp.arange(view_slots) % slot_count // CAP
    bank_rows = neg_bank.reshape(-1, neg_bank.shape[2])
    negatives = jnp.take(bank_rows, slot_local[:, None] * neg_bank.shape[1] + slot_negs, axis=0)
    loss_scale = 1.0 / math.sqrt(dp_count * item_count)

    def owner_objective(merged_float, books):
        per_row = jax.vmap(item_loss)(merged_float, books[slot_local], negatives)
        return jnp.sum(per_row * valid) * loss_scale

    gathered = jnp.dot(
        selection,
        lax.all_gather(embedded, "dp", axis=0, tiled=True),
        preferred_element_type=jnp.float32,
    )
    gathered = gathered.astype(jnp.bfloat16)
    normed_all, hidden_all, activated_all, merged_all = merge_forward(gathered, stacked)
    loss_local, pullback = jax.vjp(owner_objective, merged_all.astype(jnp.float32), codebooks)
    grad_all, book_grad = pullback(jnp.ones((), jnp.float32))
    out_grad = grad_all.astype(jnp.bfloat16)
    hidden_grad = merge_backward(hidden_all, stacked, out_grad, first_rows)
    joined = jnp.concatenate([normed_all, activated_all], axis=1)
    book_total, loss_owner = lax.psum((book_grad, loss_local), "segment")
    shard_rows = uniting_weights.shape[0]
    shard_start = dp_index * shard_rows
    shard_first = shard_start + jnp.arange(shard_rows) < first_rows
    joined_piece = lax.all_gather(joined, "dp", axis=0, tiled=True)
    first_piece = lax.all_gather(hidden_grad, "dp", axis=0, tiled=True)
    second_piece = lax.all_gather(out_grad, "dp", axis=0, tiled=True)
    columns = lax.dynamic_slice_in_dim(joined_piece, shard_start, shard_rows, 1)
    segment_grad = stacked_term(columns, first_piece, second_piece, shard_first)
    uniting_grad = lax.psum(segment_grad, "segment")
    return (uniting_grad, book_total, loss_owner.reshape(1))


def per_device(*operands):
    images, texts, _, uniting_weights = operands[:4]
    segment_count, dp_count = lax.axis_size("segment"), lax.axis_size("dp")
    shard_rows = uniting_weights.shape[0]
    first_rows = images.shape[2] + texts.shape[2]
    groups = unit_groups(dp_count, shard_rows, first_rows, segment_count)
    if dp_count % SIDES == 0 and even_units(groups, shard_rows, segment_count, uniting_weights.shape[1]):
        return per_device_parts(*operands)
    return per_device_gathered(*operands)


def solution(mesh):
    placed = (
        P("dp", None, None),
        P("dp", None, None),
        P("segment", None, None),
        P("dp", None),
        P("dp", None, None, None),
        P("dp", None, None),
        P(),
        P(),
        P(),
    )
    return jax.shard_map(
        per_device,
        mesh=mesh,
        in_specs=placed,
        out_specs=(P("dp", None), P("dp", None, None, None), P("dp")),
        check_vma=False,
    )
```

```python
import functools
import math

import jax
import jax.numpy as jnp
import numpy as np
from jax import lax
from jax.experimental import pallas as pl
from jax.experimental.pallas import tpu as pltpu
from jax.sharding import PartitionSpec as P

F32 = jnp.float32
BF16 = jnp.bfloat16

HEAD_IMG = 64
HEAD_TXT = 128
CAP = 2
IMAGE_GROUP = 4
LOG2_E = 1.4426950408889634
SIDES = 2
TILE = 16


norm_eps = 1e-06
rope_theta = 1000000.0
contrast_temp = 0.1
beta_weight = 1.0
highest = lax.Precision.HIGHEST


def gelu_value(inputs_f):
    return 0.5 * inputs_f * (1.0 + lax.erf(inputs_f / math.sqrt(2.0)))


def gelu_slope(inputs_f):
    return 0.5 * (1.0 + lax.erf(inputs_f / math.sqrt(2.0))) + inputs_f * jnp.exp(
        -0.5 * inputs_f * inputs_f
    ) / math.sqrt(2.0 * math.pi)


def dot_nt(a, b):
    return lax.dot_general(a, b, (((1,), (1,)), ((), ())), preferred_element_type=F32)

def dot_nn(a, b):
    return jnp.dot(a, b, preferred_element_type=F32)

def two_parts(value):
    high = value.astype(BF16)
    return jnp.concatenate([high, (value - high.astype(F32)).astype(BF16)], axis=0)

def dot_two(value, weights):
    rows = value.shape[0]
    both = dot_nn(two_parts(value), weights)
    return both[:rows] + both[rows:]

def unfold(slot_ref, first, out_ref, wide_ref, row_step):
    rows, columns = out_ref.shape
    blocks = columns // 128
    def body(step, carry):
        start = pl.multiple_of(step * row_step, row_step)
        source = pl.multiple_of(first + step * (row_step * blocks), 16)
        wide_ref[0 : row_step * blocks, :] = slot_ref[0, pl.ds(source, row_step * blocks), :].astype(F32)
        for block in range(blocks):
            piece = wide_ref[pl.ds(block, row_step, stride=blocks), :]
            out_ref[pl.ds(start, row_step), block * 128 : (block + 1) * 128] = piece.astype(BF16)
        return carry
    lax.fori_loop(0, rows // row_step, body, 0)

def image_kernel(flag_ref, image_ref, slot_ref, pooled_ref, w_in, w_out, wide, heads_mean):
    step = pl.program_id(0)
    item_count, model_width = pooled_ref.shape
    half_width = model_width // 2
    head_count = half_width // HEAD_IMG
    group, patch_count, _ = image_ref.shape

    @pl.when(step == 0)
    def _():
        unfold(slot_ref, 0, w_in, wide, 128)
        unfold(slot_ref, model_width * 12, w_out, wide, 128)

    tokens = image_ref[...].reshape(group * patch_count, model_width).astype(F32)
    centred = tokens - jnp.mean(tokens, axis=1, keepdims=True)
    variance = jnp.mean(centred * centred, axis=1, keepdims=True)
    normed = (centred * lax.rsqrt(variance + norm_eps)).astype(BF16)
    queries = (dot_nn(normed, w_in[:, :half_width]) * (LOG2_E / math.sqrt(HEAD_IMG))).astype(BF16)
    keys = dot_nn(normed, w_in[:, half_width : 2 * half_width]).astype(BF16)
    row_ids = lax.broadcasted_iota(jnp.int32, (head_count, patch_count), 0)
    flag = flag_ref[0].astype(F32)
    for member in range(group):
        rows = slice(member * patch_count, (member + 1) * patch_count)
        weights = jnp.zeros((head_count, patch_count), F32)
        for head in range(head_count):
            span = slice(head * HEAD_IMG, (head + 1) * HEAD_IMG)
            scores = dot_nt(queries[rows, span], keys[rows, span])
            exps = jnp.exp2(scores - jnp.max(scores, axis=1, keepdims=True))
            share = (1.0 / patch_count) / jnp.sum(exps, axis=1, keepdims=True)
            mean_share = jnp.sum(exps * share, axis=0, keepdims=True)
            weights = weights + jnp.where(row_ids == head, mean_share, 0.0)
        item = step * group + member
        heads_mean[pl.ds(item * head_count, head_count), :] = dot_two(weights, normed[rows])
        pooled_ref[pl.ds(item, 1), :] = jnp.mean(tokens[rows], axis=0, keepdims=True) * flag

    @pl.when(step == item_count // group - 1)
    def _():
        values = dot_two(heads_mean[...], w_in[:, 2 * half_width :])
        rows = lax.broadcasted_iota(jnp.int32, values.shape, 0)
        columns = lax.broadcasted_iota(jnp.int32, values.shape, 1)
        values = jnp.where(rows % head_count == columns // HEAD_IMG, values, 0.0)
        attended = jnp.sum(values.reshape(item_count, head_count, half_width), axis=1)
        pooled_ref[...] += dot_two(attended, w_out[...])

def image_pooled(images, slot, flag):
    item_count, patch_count, model_width = images.shape
    half_width = model_width // 2
    head_count = half_width // HEAD_IMG
    return pl.pallas_call(
        image_kernel,
        grid=(item_count // IMAGE_GROUP,),
        in_specs=[
            pl.BlockSpec(memory_space=pltpu.SMEM),
            pl.BlockSpec((IMAGE_GROUP, patch_count, model_width), lambda i: (i, 0, 0)),
            pl.BlockSpec((1, 16 * model_width, 128), lambda i: (0, 0, 0), pipeline_mode=pl.Buffered(1)),
        ],
        out_specs=pl.BlockSpec((item_count, model_width), lambda i: (0, 0)),
        out_shape=jax.ShapeDtypeStruct((item_count, model_width), F32),
        scratch_shapes=[
            pltpu.VMEM((model_width, 3 * half_width), BF16),
            pltpu.VMEM((half_width, model_width), BF16),
            pltpu.VMEM((128 * 12, 128), F32),
            pltpu.VMEM((item_count * head_count, model_width), F32),
        ],
        compiler_params=pltpu.CompilerParams(vmem_limit_bytes=40 * 1024 * 1024),
    )(flag, images, slot)

def rope_tables(tokens, repeats):
    half = HEAD_TXT // 2
    exponents = np.arange(half).astype(np.float32) * np.float32(2.0 / HEAD_TXT)
    inverse = np.exp(np.float32(-math.log(rope_theta)) * exponents).astype(np.float32)
    angles = (np.arange(tokens).astype(np.float32)[:, None] * inverse[None, :]).astype(np.float32)
    cosine = np.concatenate([np.cos(angles), np.cos(angles)], axis=1)
    sine = np.concatenate([-np.sin(angles), np.sin(angles)], axis=1)
    return np.tile(cosine, (repeats, 1)).astype(np.float32), np.tile(sine, (repeats, 1)).astype(np.float32)

def text_kernel(flag_ref, text_ref, slot_ref, cos_ref, sin_ref, pooled_ref, w_in, w_out, wide, heads_mean):
    item_count, token_count, model_width = text_ref.shape
    half_width = model_width // 2
    head_count = half_width // HEAD_TXT
    unfold(slot_ref, 0, w_in, wide, 128)
    unfold(slot_ref, model_width * 8, w_out, wide, 128)
    tokens = text_ref[...].reshape(item_count * token_count, model_width).astype(F32)
    normed = (tokens * lax.rsqrt(jnp.mean(tokens * tokens, axis=1, keepdims=True) + norm_eps)).astype(BF16)
    residual = jnp.mean(tokens.reshape(item_count, token_count, model_width), axis=1)
    cosine, sine = cos_ref[...], sin_ref[...]

    def head_columns(head):
        return dot_nn(normed, w_in[:, head * HEAD_TXT : (head + 1) * HEAD_TXT])

    def turned(head, scale):
        part = head_columns(head)
        return ((part * cosine + pltpu.roll(part, HEAD_TXT // 2, 1) * sine).astype(BF16)).astype(F32) * scale

    queries = [(turned(head, 1.0)).astype(BF16) for head in range(head_count)]
    keys = turned(head_count, 1.0).astype(BF16)
    values = head_columns(head_count + 1).astype(BF16)
    wide_columns = head_count * token_count
    key_ids = lax.broadcasted_iota(jnp.int32, (token_count, wide_columns), 0)
    query_ids = lax.broadcasted_iota(jnp.int32, (token_count, wide_columns), 1) % token_count
    allowed = key_ids <= query_ids
    own_head = lax.broadcasted_iota(jnp.int32, (8, wide_columns), 0) == (
        lax.broadcasted_iota(jnp.int32, (8, wide_columns), 1) // token_count
    )
    for item in range(item_count):
        span = slice(item * token_count, (item + 1) * token_count)
        asked = jnp.concatenate([query[span] for query in queries], axis=0)
        scores = dot_nt(keys[span], asked) * (1.0 / math.sqrt(HEAD_TXT))
        scores = jnp.where(allowed, scores, -1e30)
        exps = jnp.exp(scores - jnp.max(scores, axis=0, keepdims=True))
        share = (1.0 / token_count) / jnp.sum(exps, axis=0, keepdims=True)
        share = jnp.where(own_head, share, 0.0).astype(BF16)
        weights = dot_nt(share, exps.astype(BF16))
        heads_mean[:, item, :] = dot_two(weights, values[span])
    pooled = residual * flag_ref[0].astype(F32)
    for head in range(head_count):
        pooled = pooled + dot_two(heads_mean[head], w_out[head * HEAD_TXT : (head + 1) * HEAD_TXT, :])
    pooled_ref[...] = pooled

def text_pooled(texts, slot, flag):
    item_count, token_count, model_width = texts.shape
    half_width = model_width // 2
    inner = half_width + 2 * HEAD_TXT
    cosine, sine = rope_tables(token_count, item_count)
    vm = pl.BlockSpec(memory_space=pltpu.VMEM)
    return pl.pallas_call(
        text_kernel,
        in_specs=[pl.BlockSpec(memory_space=pltpu.SMEM)] + [vm] * 4,
        out_specs=vm,
        out_shape=jax.ShapeDtypeStruct((item_count, model_width), F32),
        scratch_shapes=[
            pltpu.VMEM((model_width, inner), BF16),
            pltpu.VMEM((half_width, model_width), BF16),
            pltpu.VMEM((128 * 12, 128), F32),
            pltpu.VMEM((8, item_count, HEAD_TXT), F32),
        ],
        compiler_params=pltpu.CompilerParams(vmem_limit_bytes=40 * 1024 * 1024),
    )(flag, texts, slot, jnp.asarray(cosine), jnp.asarray(sine))

def merge_forward(embedded, stacked):
    first_rows = embedded.shape[1]
    float_embed = embedded.astype(jnp.float32)
    normed = (
        float_embed
        * lax.rsqrt(jnp.mean(float_embed * float_embed, axis=1, keepdims=True) + norm_eps)
    ).astype(jnp.bfloat16)
    hidden = jnp.dot(normed, stacked[:first_rows], preferred_element_type=jnp.float32)
    activated = gelu_value(hidden).astype(jnp.bfloat16)
    merged = jnp.dot(activated, stacked[first_rows:], preferred_element_type=jnp.float32).astype(
        jnp.bfloat16
    )
    return (normed, hidden, activated, merged)


def merge_backward(hidden, stacked, out_grad, first_rows):
    w_second = stacked[first_rows:]
    act_grad = lax.dot_general(
        out_grad, w_second, (((1,), (1,)), ((), ())), preferred_element_type=jnp.float32
    )
    return (act_grad * gelu_slope(hidden)).astype(jnp.bfloat16)


def item_loss(merged_row, book_rows, negatives):
    emb_width = merged_row.shape[0]
    quant_tau = math.sqrt(emb_width) / 2.0
    residual = merged_row * lax.rsqrt(jnp.mean(merged_row * merged_row) + norm_eps)
    quantized = jnp.zeros_like(merged_row)
    for level_index in range(book_rows.shape[0]):
        code_rows = book_rows[level_index]
        cross_terms = jnp.dot(code_rows, residual, precision=highest)
        logits = (2.0 * cross_terms - jnp.sum(code_rows * code_rows, axis=1)) / quant_tau
        logits = logits - lax.stop_gradient(jnp.max(logits))
        exp_logits = jnp.exp(logits)
        chosen = jnp.dot(exp_logits / jnp.sum(exp_logits), code_rows, precision=highest)
        residual = residual - chosen
        quantized = quantized + chosen
    recon_error = jnp.mean(residual * residual)
    anchor = quantized * lax.rsqrt(jnp.mean(quantized * quantized) + norm_eps)
    candidates = jnp.concatenate([merged_row[None, :], negatives.astype(jnp.float32)], axis=0)
    cand_unit = candidates * lax.rsqrt(
        jnp.mean(candidates * candidates, axis=1, keepdims=True) + norm_eps
    )
    similarity = jnp.dot(cand_unit, anchor, precision=highest) / (emb_width * contrast_temp)
    top_score = lax.stop_gradient(jnp.max(similarity))
    contrast = top_score + jnp.log(jnp.sum(jnp.exp(similarity - top_score))) - similarity[0]
    return contrast + beta_weight * recon_error


def stacked_term(columns, first_grad, second_grad, in_first):
    contract = (((0,), (0,)), ((), ()))
    first_term = lax.dot_general(columns, first_grad, contract, preferred_element_type=jnp.float32)
    second_term = lax.dot_general(
        columns, second_grad, contract, preferred_element_type=jnp.float32
    )
    return jnp.where(in_first[:, None], first_term, second_term)


def first_rows_in(shard, shard_rows, first_rows):
    return min(max(first_rows - shard * shard_rows, 0), shard_rows)


def unit_groups(shard_count, shard_rows, first_rows, segment_count):
    shards = []
    for shard in range(shard_count):
        inside = first_rows_in(shard, shard_rows, first_rows)
        if inside < shard_rows:
            shards.append((shard, inside, shard * shard_rows + inside - first_rows, shard_rows - inside))
    tiles = [rows // (TILE * segment_count) for _, _, _, rows in shards]
    room = sum(tiles) // SIDES
    taken = [count // SIDES for count in tiles]
    for index, count in enumerate(tiles):
        if count % SIDES and sum(taken) < room:
            taken[index] += 1
    sides = [taken, [count - mine for count, mine in zip(tiles, taken)]]
    groups = []
    for index, (shard, inside, base, _) in enumerate(shards):
        starts, shares, start = [], [], 0
        for side in range(SIDES):
            share = sides[side][index] * TILE
            starts.append(start)
            shares.append(share)
            start += share * segment_count
        groups.append((shard, inside, base, tuple(starts), tuple(shares)))
    return groups


def even_units(groups, shard_rows, segment_count, width):
    return all(
        inside % TILE == 0 and sum(shares) * segment_count == shard_rows - inside and min(shares) > 0
        for _, inside, _, _, shares in groups
    ) and all(sum(group[4][side] for group in groups) * segment_count * SIDES == width for side in range(SIDES))


def piece_rows(groups, shard_rows, width, columns):
    return max([shard_rows] + [inside + width // columns * max(shares) for _, inside, _, _, shares in groups])


def message_kernel(groups, rows_ref, message_ref):
    shard, segment = lax.axis_index("dp"), lax.axis_index("segment")
    row_count, width = rows_ref.shape
    copies, _, columns = message_ref.shape
    segment_count = width // (SIDES * columns)
    first_last = groups[0][0]

    for part in range(segment_count):

        @pl.when((shard <= first_last) & (segment == part))
        def _(part=part):
            for side in range(SIDES):
                picked = [
                    rows_ref[:, base + starts[side] + shares[side] * part : base + starts[side] + shares[side] * (part + 1)]
                    for _, _, base, starts, shares in groups
                ]
                message = jnp.concatenate(picked, axis=1)
                for copy in range(side, copies, SIDES):
                    message_ref[copy, :row_count, :] = message

    for group_shard, inside, _, starts, shares in groups:

        @pl.when(shard == group_shard)
        def _(inside=inside, starts=starts, shares=shares):
            for side in range(SIDES):
                share = shares[side]
                start = pl.multiple_of(inside + starts[side] + share * segment, TILE)
                for block in range(width // columns):
                    piece = rows_ref[pl.ds(start, share), block * columns : (block + 1) * columns]
                    for copy in range(side, copies, SIDES):
                        message_ref[copy, inside + block * share : inside + (block + 1) * share, :] = piece


def weight_message(uniting_weights, groups, copies, columns):
    shard_rows, width = uniting_weights.shape
    vm = pl.BlockSpec(memory_space=pltpu.VMEM)
    return pl.pallas_call(
        functools.partial(message_kernel, groups),
        in_specs=[vm],
        out_specs=vm,
        out_shape=jax.ShapeDtypeStruct((copies, piece_rows(groups, shard_rows, width, columns), columns), BF16),
    )(uniting_weights)


def forward_kernel(
    groups,
    first_rows,
    embedded_ref,
    own_ref,
    weights,
    blocks_ref,
    hidden_ref,
    active_ref,
    second_ref,
    partial_ref,
):
    shard_count, _, columns = weights.shape
    shard_rows = blocks_ref.shape[2]
    source_count, source_items, width = embedded_ref.shape
    items = source_count * source_items
    embedded = embedded_ref[...].astype(F32).reshape(items, width)
    normed = embedded * lax.rsqrt(jnp.mean(embedded * embedded, axis=1, keepdims=True) + norm_eps)
    normed = normed.astype(BF16)
    hidden = jnp.zeros((items, columns), F32)
    for block in range(shard_count):
        inside = first_rows_in(block, shard_rows, first_rows)
        start = block * shard_rows
        if inside > 0:
            rows = normed[:, start : start + inside]
            hidden = hidden + dot_nn(rows, weights[block, :inside])
            if inside < shard_rows:
                rows = jnp.concatenate([rows, jnp.zeros((items, shard_rows - inside), BF16)], axis=1)
            blocks_ref[block] = rows
        else:
            blocks_ref[block] = jnp.zeros((items, shard_rows), BF16)
    hidden_ref[...] = hidden
    active = gelu_value(hidden).astype(BF16)
    active_ref[...] = active
    for side in range(SIDES):

        @pl.when(lax.rem(lax.axis_index("dp"), SIDES) == side)
        def _(side=side):
            offset = 0
            for block, inside, _, _, shares in groups:
                share = shares[side]
                for part in range(partial_ref.shape[1] // columns):
                    second_ref[offset : offset + share, part * columns : (part + 1) * columns] = weights[
                        block, inside + part * share : inside + (part + 1) * share, :
                    ]
                offset += share

    partial_ref[...] = dot_nn(dot_nn(own_ref[...], active).astype(BF16), second_ref[...])


def merge_part(embedded_all, pieces, own, groups, shard_rows, first_rows, width):
    shard_count, _, columns = pieces.shape
    items = embedded_all.shape[0] * embedded_all.shape[1]
    vm = pl.BlockSpec(memory_space=pltpu.VMEM)
    return pl.pallas_call(
        functools.partial(forward_kernel, groups, first_rows),
        in_specs=[vm] * 3,
        out_specs=[vm] * 5,
        out_shape=[
            jax.ShapeDtypeStruct((shard_count, items, shard_rows), BF16),
            jax.ShapeDtypeStruct((items, columns), F32),
            jax.ShapeDtypeStruct((items, columns), BF16),
            jax.ShapeDtypeStruct((columns, width), BF16),
            jax.ShapeDtypeStruct((own.shape[0], width), F32),
        ],
        compiler_params=pltpu.CompilerParams(vmem_limit_bytes=32 * 1024 * 1024),
    )(embedded_all, own, pieces)


def split(value):
    high = value.astype(BF16)
    return high, (value - high.astype(F32)).astype(BF16)


def exact_nt(value, high, low):
    first, second = split(value)
    rows = value.shape[0]
    both = dot_nt(jnp.concatenate([first, second], axis=0), high)
    return both[:rows] + both[rows:] + dot_nt(first, low)


def exact_nn(value, high, low):
    first, second = split(value)
    rows = value.shape[0]
    both = dot_nn(jnp.concatenate([first, second], axis=0), high)
    return both[:rows] + both[rows:] + dot_nn(first, low)


def dot_tn(a, b):
    return lax.dot_general(a, b, (((0,), (0,)), ((), ())), preferred_element_type=F32)


def exact_tn(a, b):
    a_high, a_low = split(a)
    b_high, b_low = split(b)
    return dot_tn(
        jnp.concatenate([a_high, a_low, a_high], axis=0), jnp.concatenate([b_high, b_high, b_low], axis=0)
    )


def square_sums(value):
    high, low = split(value * value)
    ones = jnp.ones((8, value.shape[1]), BF16)
    return (dot_nt(ones, high) + dot_nt(ones, low))[:1]


def quantizer_kernel(loss_scale, merged_ref, book_ref, bank_ref, count_ref, merged_grad_ref, loss_ref, left_ref, right_ref, highs, lows):
    width = merged_ref.shape[1]
    levels = book_ref.shape[0]
    inverse_tau = 2.0 / math.sqrt(width)
    inverse_temp = 1.0 / (width * contrast_temp)
    merged = merged_ref[...].astype(BF16).astype(F32)
    merged_scale = lax.rsqrt(jnp.mean(merged * merged, axis=1, keepdims=True) + norm_eps)
    residuals = [merged * merged_scale]
    shares, chosen_rows = [], []
    for level in range(levels):
        codes = book_ref[level]
        high, low = split(codes)
        highs[level] = high
        lows[level] = low
        logits = (2.0 * exact_nt(residuals[level], high, low) - square_sums(codes)) * inverse_tau
        exps = jnp.exp(logits - jnp.max(logits, axis=1, keepdims=True))
        share = exps / jnp.sum(exps, axis=1, keepdims=True)
        chosen = exact_nn(share, high, low)
        shares.append(share)
        chosen_rows.append(chosen)
        residuals.append(residuals[level] - chosen)
    last = residuals[levels]
    quantized = chosen_rows[0]
    for chosen in chosen_rows[1:]:
        quantized = quantized + chosen
    anchor_scale = lax.rsqrt(jnp.mean(quantized * quantized, axis=1, keepdims=True) + norm_eps)
    anchor = quantized * anchor_scale
    own = jnp.sum(anchor * residuals[0], axis=1, keepdims=True) * inverse_temp
    bank = bank_ref[...]
    bank_wide = bank.astype(F32)
    bank_scale = lax.rsqrt(square_sums(bank_wide) * (1.0 / width) + norm_eps)
    anchor_parts = jnp.concatenate(split(anchor), axis=0)
    rows = anchor.shape[0]
    both = dot_nt(anchor_parts, bank)
    similar = (both[:rows] + both[rows:]) * bank_scale * inverse_temp
    counts = count_ref[...]
    named = counts > 0.0
    top = jnp.maximum(jnp.max(jnp.where(named, similar, own), axis=1, keepdims=True), own)
    bank_exps = jnp.where(named, jnp.exp(jnp.where(named, similar, top) - top), 0.0) * counts
    own_exp = jnp.exp(own - top)
    total = jnp.sum(bank_exps, axis=1, keepdims=True) + own_exp
    item_losses = top + jnp.log(total) - own + jnp.mean(last * last, axis=1, keepdims=True)
    loss_ref[...] = jnp.broadcast_to(jnp.sum(item_losses, axis=0, keepdims=True) * loss_scale, loss_ref.shape)

    bank_weight = bank_exps / total * (loss_scale * inverse_temp)
    own_weight = (own_exp / total - 1.0) * (loss_scale * inverse_temp)
    weight_parts = jnp.concatenate(split(bank_weight * bank_scale), axis=0)
    both = dot_nn(weight_parts, bank)
    anchor_grad = both[:rows] + both[rows:] + own_weight * residuals[0]
    unit_grad = own_weight * anchor
    quantized_grad = anchor_scale * (anchor_grad - anchor * jnp.mean(anchor * anchor_grad, axis=1, keepdims=True))
    residual_grad = last * (2.0 * loss_scale / width)
    for level in reversed(range(levels)):
        high, low = highs[level], lows[level]
        chosen_grad = quantized_grad - residual_grad
        share_grad = exact_nt(chosen_grad, high, low)
        share = shares[level]
        logit_grad = share * (share_grad - jnp.sum(share * share_grad, axis=1, keepdims=True)) * (2.0 * inverse_tau)
        left_ref[level] = jnp.concatenate([share, logit_grad], axis=0)
        right_ref[level] = jnp.concatenate([chosen_grad, residuals[level]], axis=0)
        residual_grad = residual_grad + exact_nn(logit_grad, high, low)
    unit_grad = unit_grad + residual_grad
    unit = residuals[0]
    merged_grad = merged_scale * (unit_grad - unit * jnp.mean(unit * unit_grad, axis=1, keepdims=True))
    merged_grad_ref[...] = merged_grad.astype(BF16)


def quantizer(merged, books, bank, counts, loss_scale):
    levels, codes, width = books.shape
    rows = merged.shape[0]
    vm = pl.BlockSpec(memory_space=pltpu.VMEM)
    return pl.pallas_call(
        functools.partial(quantizer_kernel, loss_scale),
        in_specs=[vm] * 4,
        out_specs=[vm] * 4,
        out_shape=[
            jax.ShapeDtypeStruct(merged.shape, BF16),
            jax.ShapeDtypeStruct((8, 128), F32),
            jax.ShapeDtypeStruct((levels, 2 * rows, codes), F32),
            jax.ShapeDtypeStruct((levels, 2 * rows, width), F32),
        ],
        scratch_shapes=[pltpu.VMEM(books.shape, BF16), pltpu.VMEM(books.shape, BF16)],
        compiler_params=pltpu.CompilerParams(vmem_limit_bytes=32 * 1024 * 1024),
    )(merged, books, bank, counts)


def codebook_kernel(left_ref, right_ref, book_ref, grad_ref):
    levels, doubled, _ = left_ref.shape
    width = right_ref.shape[2]
    rows = doubled // 2
    ones = jnp.ones((rows, 128), F32)
    for level in range(levels):
        outer = exact_tn(left_ref[level], right_ref[level])
        totals = exact_tn(left_ref[level, rows:], ones)
        for block in range(width // 128):
            span = slice(block * 128, (block + 1) * 128)
            grad_ref[level, :, span] = outer[:, span] - totals * book_ref[level, :, span]


def codebook_grad(left, right, books):
    vm = pl.BlockSpec(memory_space=pltpu.VMEM)
    return pl.pallas_call(
        codebook_kernel,
        in_specs=[vm] * 3,
        out_specs=vm,
        out_shape=jax.ShapeDtypeStruct(books.shape, F32),
        compiler_params=pltpu.CompilerParams(vmem_limit_bytes=32 * 1024 * 1024),
    )(left, right, books)


def backward_kernel(gathered_ref, order_ref, hidden_ref, active_ref, second_ref, out_grad_ref, sent_ref):
    owners, places, width = gathered_ref.shape
    columns = hidden_ref.shape[1]
    gathered = gathered_ref[...].astype(F32).reshape(owners * places, width).astype(BF16)
    out_grad = dot_tn(order_ref[...], gathered).astype(BF16)
    out_grad_ref[...] = out_grad
    hidden_grad = dot_nt(out_grad, second_ref[...]) * gelu_slope(hidden_ref[...])
    sent_ref[:, :columns] = hidden_grad.astype(BF16)
    sent_ref[:, columns:] = active_ref[...]


def backward_part(gathered, order, hidden, active, second):
    items, columns = hidden.shape
    vm = pl.BlockSpec(memory_space=pltpu.VMEM)
    return pl.pallas_call(
        backward_kernel,
        in_specs=[vm] * 5,
        out_specs=[vm] * 2,
        out_shape=[
            jax.ShapeDtypeStruct((items, gathered.shape[2]), BF16),
            jax.ShapeDtypeStruct((items, 2 * columns), BF16),
        ],
        compiler_params=pltpu.CompilerParams(vmem_limit_bytes=32 * 1024 * 1024),
    )(gathered, order, hidden, active, second)


def weight_grad_kernel(
    groups, block_ref, out_grad_ref, here_ref, row_ref, side_ref, corner_ref, grad_ref, hidden_grad, active
):
    shard, segment = lax.axis_index("dp"), lax.axis_index("segment")
    cores, items, doubled = here_ref.shape
    columns = doubled // 2
    shard_rows = block_ref.shape[1]
    own_side, own_row = lax.rem(shard, SIDES), segment // cores
    segment_count = hidden_grad.shape[1] // (SIDES * columns)

    def place_units(target, first):
        for side in range(SIDES):
            for other in range(segment_count):
                parts = [ref[other % cores, :, first : first + columns] for ref in (here_ref, row_ref, side_ref, corner_ref)]
                same_row = own_row == other // cores
                near = jnp.where(same_row, parts[0], parts[1])
                across = jnp.where(same_row, parts[2], parts[3])
                part = jnp.where(own_side == side, near, across)
                offset = 0
                for _, _, base, starts, shares in groups:
                    spot = base + starts[side] + shares[side] * other
                    target[:, spot : spot + shares[side]] = part[:, offset : offset + shares[side]]
                    offset += shares[side]

    place_units(hidden_grad, 0)
    grad_ref[...] = dot_tn(block_ref[...], hidden_grad[...])
    for group_shard, inside, base, _, _ in groups:

        @pl.when(shard == group_shard)
        def _(inside=inside, base=base):
            place_units(active, columns)
            wanted = active[:, base : base + shard_rows - inside]
            grad_ref[inside:, :] = dot_tn(wanted, out_grad_ref[...])


def weight_grad(block, out_grad, parts, groups):
    items, shard_rows = block.shape
    width = out_grad.shape[1]
    vm = pl.BlockSpec(memory_space=pltpu.VMEM)
    return pl.pallas_call(
        functools.partial(weight_grad_kernel, groups),
        in_specs=[vm] * (2 + len(parts)),
        out_specs=vm,
        out_shape=jax.ShapeDtypeStruct((shard_rows, width), F32),
        scratch_shapes=[pltpu.VMEM((items, width), BF16), pltpu.VMEM((items, width), BF16)],
        compiler_params=pltpu.CompilerParams(vmem_limit_bytes=32 * 1024 * 1024),
    )(block, out_grad, *parts)


def around(near, across, segment_count, dp_count):
    row = lax.ppermute(near, "segment", [(j, j ^ 2) for j in range(segment_count)])
    side = lax.ppermute(across, "dp", [(i, i ^ 1) for i in range(dp_count)])
    corners = [
        (j * dp_count + i, (j ^ 2) * dp_count + (i ^ 1)) for j in range(segment_count) for i in range(dp_count)
    ]
    corner = lax.ppermute(across, ("segment", "dp"), corners)
    return row, side, corner


def spread(rows, axis_name, count):
    return lax.all_to_all(
        jnp.broadcast_to(rows[None], (count,) + rows.shape), axis_name, 0, 0, tiled=True
    )


def per_device_parts(
    images, texts, section_weights, uniting_weights, codebooks, neg_bank, item_cats, cat_slot, neg_index
):
    segment_index = lax.axis_index("segment")
    segment_count = lax.axis_size("segment")
    dp_index = lax.axis_index("dp")
    dp_count = lax.axis_size("dp")
    item_count, _, image_width = images.shape
    text_width = texts.shape[2]
    first_rows = image_width + text_width
    shard_rows, width = uniting_weights.shape
    columns = width // (SIDES * segment_count)
    groups = unit_groups(dp_count, shard_rows, first_rows, segment_count)
    message = weight_message(uniting_weights, groups, dp_count, columns)
    flag = (1 - segment_index % 2).astype(jnp.int32).reshape(1)
    flag, message = lax.optimization_barrier((flag, message))
    pieces = lax.all_to_all(message, "dp", 0, 0, tiled=True)
    pooled = pooled_features(images, texts, section_weights, segment_index, flag)
    pooled = pooled + lax.ppermute(pooled, "segment", [(i, i ^ 1) for i in range(segment_count)])
    mine = pooled.astype(BF16)
    other = lax.ppermute(mine, "segment", [(i, i ^ 2) for i in range(segment_count)])
    is_image = segment_index < 2
    embedded = jnp.concatenate(
        [jnp.where(is_image, mine, other)[:, :image_width], jnp.where(is_image, other, mine)], axis=1
    )
    embedded, pieces = lax.optimization_barrier((embedded, pieces))
    embedded_all = spread(embedded, "dp", dp_count)

    pair = item_cats.shape[1] // dp_count
    cats = item_cats.reshape(segment_count, dp_count, pair).transpose(1, 0, 2).reshape(-1)
    items = cats.shape[0]
    slots = jnp.sum(
        jnp.where(cats[:, None] == jnp.arange(cat_slot.shape[0])[None, :], cat_slot[None, :], 0), axis=1
    )
    ids = jnp.arange(items)
    rank = jnp.sum(jnp.where((slots[None, :] == slots[:, None]) & (ids[None, :] < ids[:, None]), 1, 0), axis=1)
    owned = segment_count * CAP
    order = (ids[:, None] == (slots * owned + rank)[None, :]).astype(BF16)
    own = lax.dynamic_slice_in_dim(order, dp_index * owned, owned, 0)
    across_own = lax.dynamic_slice_in_dim(order, (dp_index ^ 1) * owned, owned, 0)
    both_own = jnp.concatenate([own, across_own], axis=0)
    negatives = neg_index.reshape(segment_count, dp_count, pair, -1).transpose(1, 0, 2, 3).reshape(items, -1)
    own_negatives = jnp.dot(own.astype(F32), negatives.astype(F32), precision=highest)
    bank = neg_bank[0]
    bank_ids = jnp.arange(bank.shape[0]).astype(F32)
    counts = jnp.sum((own_negatives[:, :, None] == bank_ids[None, None, :]).astype(F32), axis=1)

    blocks, hidden, active, second, partial = merge_part(
        embedded_all, pieces, both_own, groups, shard_rows, first_rows, width
    )
    partial = partial + lax.ppermute(partial, "segment", [(i, i ^ 1) for i in range(segment_count)])
    row, side, corner = around(partial[:owned], partial[owned:], segment_count, dp_count)
    merged = (partial[:owned] + row) + (side + corner)
    merged_grad, loss, left, right = quantizer(merged, codebooks[0], bank, counts, 1.0 / math.sqrt(items))
    gathered = spread(merged_grad, "dp", dp_count)
    book_grad = codebook_grad(left, right, codebooks[0])
    out_grad, sent = backward_part(gathered, order, hidden, active, second)
    twin = lax.ppermute(sent, "segment", [(i, i ^ 1) for i in range(segment_count)])
    first_core = segment_index % 2 == 0
    here = jnp.stack([jnp.where(first_core, sent, twin), jnp.where(first_core, twin, sent)])
    parts = (here,) + around(here, here, segment_count, dp_count)
    block = lax.dynamic_index_in_dim(blocks, dp_index, 0, keepdims=False)
    uniting_grad = weight_grad(block, out_grad, parts, groups)
    return (uniting_grad, book_grad[None], loss[0, :1])


def pooled_features(images, texts, section_weights, segment_index, flag):
    image_width, text_width = images.shape[2], texts.shape[2]

    def image_branch(operands):
        pooled = image_pooled(operands[0], operands[2], flag)
        return jnp.pad(pooled, ((0, 0), (0, text_width - image_width)))

    def text_branch(operands):
        return text_pooled(operands[1], operands[2], flag)

    return lax.cond(segment_index < 2, image_branch, text_branch, (images, texts, section_weights))


def per_device_gathered(
    images,
    texts,
    section_weights,
    uniting_weights,
    codebooks,
    neg_bank,
    item_cats,
    cat_slot,
    neg_index,
):
    segment_index = lax.axis_index("segment")
    segment_count = lax.axis_size("segment")
    dp_index = lax.axis_index("dp")
    dp_count = lax.axis_size("dp")
    group_index = segment_index % 2
    item_count = images.shape[0]

    flag = (1 - group_index).astype(jnp.int32).reshape(1)
    pooled = pooled_features(images, texts, section_weights, segment_index, flag)
    image_width = images.shape[2]
    is_image = segment_index < 2
    packed = jnp.concatenate(
        [jnp.where(is_image, pooled[:, :image_width], 0.0), jnp.where(is_image, 0.0, pooled)], axis=1
    )
    embedded = lax.psum_scatter(packed, "segment", scatter_dimension=0, tiled=True).astype(
        jnp.bfloat16
    )
    stacked = lax.all_gather(uniting_weights, "dp", axis=0, tiled=True)
    first_rows = embedded.shape[1]
    cat_per_dev = codebooks.shape[0]
    slot_count = cat_per_dev * CAP
    row_total = item_cats.shape[1]
    cats_all = item_cats.reshape(-1)
    entry_count = cats_all.shape[0]
    entry_ids = jnp.arange(entry_count)
    category_match = cats_all[:, None] == jnp.arange(cat_slot.shape[0])[None, :]
    entry_slots = jnp.sum(jnp.where(category_match, cat_slot[None, :], 0), axis=1)
    entry_owner = entry_slots // cat_per_dev
    entry_local = entry_slots % cat_per_dev
    entry_row = entry_ids // row_total
    earlier = entry_ids[None, :] < entry_ids[:, None]
    same_cat = (cats_all[:, None] == cats_all[None, :]) & (entry_row[:, None] == entry_row[None, :])
    entry_rank = jnp.sum(jnp.where(earlier & same_cat, 1, 0), axis=1)
    entry_place = entry_local * CAP + entry_rank
    entry_position = entry_row * slot_count + entry_place
    owned = entry_owner == dp_index
    all_slots = segment_count * slot_count
    slot_match_all = owned[None, :] & (entry_position[None, :] == jnp.arange(all_slots)[:, None])
    view_match = lax.dynamic_slice(
        slot_match_all,
        (segment_index * slot_count, segment_index * row_total),
        (slot_count, row_total),
    )
    view_base = segment_index * row_total
    view_slots = view_match.shape[0]
    selection = view_match.astype(jnp.bfloat16)
    valid = jnp.sum(view_match.astype(jnp.float32), axis=1)
    slot_item = jnp.sum(
        jnp.where(view_match, jnp.arange(view_match.shape[1])[None, :] + view_base, 0), axis=1
    )
    slot_negs = jnp.take(neg_index.reshape(entry_count, -1), slot_item, axis=0)
    slot_local = jnp.arange(view_slots) % slot_count // CAP
    bank_rows = neg_bank.reshape(-1, neg_bank.shape[2])
    negatives = jnp.take(bank_rows, slot_local[:, None] * neg_bank.shape[1] + slot_negs, axis=0)
    loss_scale = 1.0 / math.sqrt(dp_count * item_count)

    def owner_objective(merged_float, books):
        per_row = jax.vmap(item_loss)(merged_float, books[slot_local], negatives)
        return jnp.sum(per_row * valid) * loss_scale

    gathered = jnp.dot(
        selection,
        lax.all_gather(embedded, "dp", axis=0, tiled=True),
        preferred_element_type=jnp.float32,
    )
    gathered = gathered.astype(jnp.bfloat16)
    normed_all, hidden_all, activated_all, merged_all = merge_forward(gathered, stacked)
    loss_local, pullback = jax.vjp(owner_objective, merged_all.astype(jnp.float32), codebooks)
    grad_all, book_grad = pullback(jnp.ones((), jnp.float32))
    out_grad = grad_all.astype(jnp.bfloat16)
    hidden_grad = merge_backward(hidden_all, stacked, out_grad, first_rows)
    joined = jnp.concatenate([normed_all, activated_all], axis=1)
    book_total, loss_owner = lax.psum((book_grad, loss_local), "segment")
    shard_rows = uniting_weights.shape[0]
    shard_start = dp_index * shard_rows
    shard_first = shard_start + jnp.arange(shard_rows) < first_rows
    joined_piece = lax.all_gather(joined, "dp", axis=0, tiled=True)
    first_piece = lax.all_gather(hidden_grad, "dp", axis=0, tiled=True)
    second_piece = lax.all_gather(out_grad, "dp", axis=0, tiled=True)
    columns = lax.dynamic_slice_in_dim(joined_piece, shard_start, shard_rows, 1)
    segment_grad = stacked_term(columns, first_piece, second_piece, shard_first)
    uniting_grad = lax.psum(segment_grad, "segment")
    return (uniting_grad, book_total, loss_owner.reshape(1))


def per_device(*operands):
    images, texts, _, uniting_weights = operands[:4]
    segment_count, dp_count = lax.axis_size("segment"), lax.axis_size("dp")
    shard_rows = uniting_weights.shape[0]
    first_rows = images.shape[2] + texts.shape[2]
    groups = unit_groups(dp_count, shard_rows, first_rows, segment_count)
    if dp_count % SIDES == 0 and even_units(groups, shard_rows, segment_count, uniting_weights.shape[1]):
        return per_device_parts(*operands)
    return per_device_gathered(*operands)


def solution(mesh):
    placed = (
        P("dp", None, None),
        P("dp", None, None),
        P("segment", None, None),
        P("dp", None),
        P("dp", None, None, None),
        P("dp", None, None),
        P(),
        P(),
        P(),
    )
    return jax.shard_map(
        per_device,
        mesh=mesh,
        in_specs=placed,
        out_specs=(P("dp", None), P("dp", None, None, None), P("dp")),
        check_vma=False,
    )
```

```python
import functools
import math

import jax
import jax.numpy as jnp
import numpy as np
from jax import lax
from jax.experimental import pallas as pl
from jax.experimental.pallas import tpu as pltpu
from jax.sharding import PartitionSpec as P

F32 = jnp.float32
BF16 = jnp.bfloat16

HEAD_IMG = 64
HEAD_TXT = 128
CAP = 2
OWNED = 4 * CAP
MIB = 1024 * 1024
IMAGE_GROUP = 4
LOG2_E = 1.4426950408889634
SIDES = 2
TILE = 8


norm_eps = 1e-06
rope_theta = 1000000.0
contrast_temp = 0.1
beta_weight = 1.0
highest = lax.Precision.HIGHEST


def gelu_value(inputs_f):
    return 0.5 * inputs_f * (1.0 + lax.erf(inputs_f / math.sqrt(2.0)))


def gelu_slope(inputs_f):
    return 0.5 * (1.0 + lax.erf(inputs_f / math.sqrt(2.0))) + inputs_f * jnp.exp(
        -0.5 * inputs_f * inputs_f
    ) / math.sqrt(2.0 * math.pi)


def dot_nt(a, b):
    return lax.dot_general(a, b, (((1,), (1,)), ((), ())), preferred_element_type=F32)

def dot_nn(a, b):
    return jnp.dot(a, b, preferred_element_type=F32)

def two_parts(value):
    high = value.astype(BF16)
    return jnp.concatenate([high, (value - high.astype(F32)).astype(BF16)], axis=0)

def dot_two(value, weights):
    rows = value.shape[0]
    both = dot_nn(two_parts(value), weights)
    return both[:rows] + both[rows:]

def unfold(slot_ref, first, out_ref, wide_ref, row_step):
    rows, columns = out_ref.shape
    blocks = columns // 128
    def body(step, carry):
        start = pl.multiple_of(step * row_step, row_step)
        source = pl.multiple_of(first + step * (row_step * blocks), 16)
        wide_ref[0 : row_step * blocks, :] = slot_ref[0, pl.ds(source, row_step * blocks), :].astype(F32)
        for block in range(blocks):
            piece = wide_ref[pl.ds(block, row_step, stride=blocks), :]
            out_ref[pl.ds(start, row_step), block * 128 : (block + 1) * 128] = piece.astype(BF16)
        return carry
    lax.fori_loop(0, rows // row_step, body, 0)

def image_kernel(flag_ref, image_ref, slot_ref, pooled_ref, w_in, w_out, wide, heads_mean):
    step = pl.program_id(0)
    item_count, model_width = pooled_ref.shape
    half_width = model_width // 2
    head_count = half_width // HEAD_IMG
    group, patch_count, _ = image_ref.shape

    @pl.when(step == 0)
    def _():
        unfold(slot_ref, 0, w_in, wide, 128)
        unfold(slot_ref, model_width * 12, w_out, wide, 128)

    tokens = image_ref[...].reshape(group * patch_count, model_width).astype(F32)
    centred = tokens - jnp.mean(tokens, axis=1, keepdims=True)
    variance = jnp.mean(centred * centred, axis=1, keepdims=True)
    normed = (centred * lax.rsqrt(variance + norm_eps)).astype(BF16)
    queries = (dot_nn(normed, w_in[:, :half_width]) * (LOG2_E / math.sqrt(HEAD_IMG))).astype(BF16)
    keys = dot_nn(normed, w_in[:, half_width : 2 * half_width]).astype(BF16)
    row_ids = lax.broadcasted_iota(jnp.int32, (head_count, patch_count), 0)
    flag = flag_ref[0].astype(F32)
    for member in range(group):
        rows = slice(member * patch_count, (member + 1) * patch_count)
        weights = jnp.zeros((head_count, patch_count), F32)
        for head in range(head_count):
            span = slice(head * HEAD_IMG, (head + 1) * HEAD_IMG)
            scores = dot_nt(queries[rows, span], keys[rows, span])
            exps = jnp.exp2(scores - jnp.max(scores, axis=1, keepdims=True))
            share = (1.0 / patch_count) / jnp.sum(exps, axis=1, keepdims=True)
            mean_share = jnp.sum(exps * share, axis=0, keepdims=True)
            weights = weights + jnp.where(row_ids == head, mean_share, 0.0)
        item = step * group + member
        heads_mean[pl.ds(item * head_count, head_count), :] = dot_two(weights, normed[rows])
        pooled_ref[pl.ds(item, 1), :] = jnp.mean(tokens[rows], axis=0, keepdims=True) * flag

    @pl.when(step == item_count // group - 1)
    def _():
        values = dot_two(heads_mean[...], w_in[:, 2 * half_width :])
        rows = lax.broadcasted_iota(jnp.int32, values.shape, 0)
        columns = lax.broadcasted_iota(jnp.int32, values.shape, 1)
        values = jnp.where(rows % head_count == columns // HEAD_IMG, values, 0.0)
        attended = jnp.sum(values.reshape(item_count, head_count, half_width), axis=1)
        pooled_ref[...] += dot_two(attended, w_out[...])

def image_pooled(images, slot, flag):
    item_count, patch_count, model_width = images.shape
    half_width = model_width // 2
    head_count = half_width // HEAD_IMG
    return pl.pallas_call(
        image_kernel,
        grid=(item_count // IMAGE_GROUP,),
        in_specs=[
            pl.BlockSpec(memory_space=pltpu.SMEM),
            pl.BlockSpec((IMAGE_GROUP, patch_count, model_width), lambda i: (i, 0, 0)),
            pl.BlockSpec((1, 16 * model_width, 128), lambda i: (0, 0, 0), pipeline_mode=pl.Buffered(1)),
        ],
        out_specs=pl.BlockSpec((item_count, model_width), lambda i: (0, 0)),
        out_shape=jax.ShapeDtypeStruct((item_count, model_width), F32),
        scratch_shapes=[
            pltpu.VMEM((model_width, 3 * half_width), BF16),
            pltpu.VMEM((half_width, model_width), BF16),
            pltpu.VMEM((128 * 12, 128), F32),
            pltpu.VMEM((item_count * head_count, model_width), F32),
        ],
        compiler_params=pltpu.CompilerParams(vmem_limit_bytes=40 * 1024 * 1024),
    )(flag, images, slot)

def rope_tables(tokens, repeats):
    half = HEAD_TXT // 2
    exponents = np.arange(half).astype(np.float32) * np.float32(2.0 / HEAD_TXT)
    inverse = np.exp(np.float32(-math.log(rope_theta)) * exponents).astype(np.float32)
    angles = (np.arange(tokens).astype(np.float32)[:, None] * inverse[None, :]).astype(np.float32)
    cosine = np.concatenate([np.cos(angles), np.cos(angles)], axis=1)
    sine = np.concatenate([-np.sin(angles), np.sin(angles)], axis=1)
    return np.tile(cosine, (repeats, 1)).astype(np.float32), np.tile(sine, (repeats, 1)).astype(np.float32)

def text_kernel(flag_ref, text_ref, slot_ref, cos_ref, sin_ref, pooled_ref, w_in, w_out, wide, heads_mean):
    item_count, token_count, model_width = text_ref.shape
    half_width = model_width // 2
    head_count = half_width // HEAD_TXT
    unfold(slot_ref, 0, w_in, wide, 128)
    unfold(slot_ref, model_width * 8, w_out, wide, 128)
    tokens = text_ref[...].reshape(item_count * token_count, model_width).astype(F32)
    normed = (tokens * lax.rsqrt(jnp.mean(tokens * tokens, axis=1, keepdims=True) + norm_eps)).astype(BF16)
    residual = jnp.mean(tokens.reshape(item_count, token_count, model_width), axis=1)
    cosine, sine = cos_ref[...], sin_ref[...]

    def head_columns(head):
        return dot_nn(normed, w_in[:, head * HEAD_TXT : (head + 1) * HEAD_TXT])

    def turned(head, scale):
        part = head_columns(head)
        return ((part * cosine + pltpu.roll(part, HEAD_TXT // 2, 1) * sine).astype(BF16)).astype(F32) * scale

    queries = [(turned(head, 1.0)).astype(BF16) for head in range(head_count)]
    keys = turned(head_count, 1.0).astype(BF16)
    values = head_columns(head_count + 1).astype(BF16)
    wide_columns = head_count * token_count
    key_ids = lax.broadcasted_iota(jnp.int32, (token_count, wide_columns), 0)
    query_ids = lax.broadcasted_iota(jnp.int32, (token_count, wide_columns), 1) % token_count
    allowed = key_ids <= query_ids
    own_head = lax.broadcasted_iota(jnp.int32, (8, wide_columns), 0) == (
        lax.broadcasted_iota(jnp.int32, (8, wide_columns), 1) // token_count
    )
    for item in range(item_count):
        span = slice(item * token_count, (item + 1) * token_count)
        asked = jnp.concatenate([query[span] for query in queries], axis=0)
        scores = dot_nt(keys[span], asked) * (1.0 / math.sqrt(HEAD_TXT))
        scores = jnp.where(allowed, scores, -1e30)
        exps = jnp.exp(scores - jnp.max(scores, axis=0, keepdims=True))
        share = (1.0 / token_count) / jnp.sum(exps, axis=0, keepdims=True)
        share = jnp.where(own_head, share, 0.0).astype(BF16)
        weights = dot_nt(share, exps.astype(BF16))
        heads_mean[:, item, :] = dot_two(weights, values[span])
    pooled = residual * flag_ref[0].astype(F32)
    for head in range(head_count):
        pooled = pooled + dot_two(heads_mean[head], w_out[head * HEAD_TXT : (head + 1) * HEAD_TXT, :])
    pooled_ref[...] = pooled

def text_pooled(texts, slot, flag):
    item_count, token_count, model_width = texts.shape
    half_width = model_width // 2
    inner = half_width + 2 * HEAD_TXT
    cosine, sine = rope_tables(token_count, item_count)
    vm = pl.BlockSpec(memory_space=pltpu.VMEM)
    return pl.pallas_call(
        text_kernel,
        in_specs=[pl.BlockSpec(memory_space=pltpu.SMEM)] + [vm] * 4,
        out_specs=vm,
        out_shape=jax.ShapeDtypeStruct((item_count, model_width), F32),
        scratch_shapes=[
            pltpu.VMEM((model_width, inner), BF16),
            pltpu.VMEM((half_width, model_width), BF16),
            pltpu.VMEM((128 * 12, 128), F32),
            pltpu.VMEM((8, item_count, HEAD_TXT), F32),
        ],
        compiler_params=pltpu.CompilerParams(vmem_limit_bytes=40 * 1024 * 1024),
    )(flag, texts, slot, jnp.asarray(cosine), jnp.asarray(sine))

def merge_forward(embedded, stacked):
    first_rows = embedded.shape[1]
    float_embed = embedded.astype(jnp.float32)
    normed = (
        float_embed
        * lax.rsqrt(jnp.mean(float_embed * float_embed, axis=1, keepdims=True) + norm_eps)
    ).astype(jnp.bfloat16)
    hidden = jnp.dot(normed, stacked[:first_rows], preferred_element_type=jnp.float32)
    activated = gelu_value(hidden).astype(jnp.bfloat16)
    merged = jnp.dot(activated, stacked[first_rows:], preferred_element_type=jnp.float32).astype(
        jnp.bfloat16
    )
    return (normed, hidden, activated, merged)


def merge_backward(hidden, stacked, out_grad, first_rows):
    w_second = stacked[first_rows:]
    act_grad = lax.dot_general(
        out_grad, w_second, (((1,), (1,)), ((), ())), preferred_element_type=jnp.float32
    )
    return (act_grad * gelu_slope(hidden)).astype(jnp.bfloat16)


def item_loss(merged_row, book_rows, negatives):
    emb_width = merged_row.shape[0]
    quant_tau = math.sqrt(emb_width) / 2.0
    residual = merged_row * lax.rsqrt(jnp.mean(merged_row * merged_row) + norm_eps)
    quantized = jnp.zeros_like(merged_row)
    for level_index in range(book_rows.shape[0]):
        code_rows = book_rows[level_index]
        cross_terms = jnp.dot(code_rows, residual, precision=highest)
        logits = (2.0 * cross_terms - jnp.sum(code_rows * code_rows, axis=1)) / quant_tau
        logits = logits - lax.stop_gradient(jnp.max(logits))
        exp_logits = jnp.exp(logits)
        chosen = jnp.dot(exp_logits / jnp.sum(exp_logits), code_rows, precision=highest)
        residual = residual - chosen
        quantized = quantized + chosen
    recon_error = jnp.mean(residual * residual)
    anchor = quantized * lax.rsqrt(jnp.mean(quantized * quantized) + norm_eps)
    candidates = jnp.concatenate([merged_row[None, :], negatives.astype(jnp.float32)], axis=0)
    cand_unit = candidates * lax.rsqrt(
        jnp.mean(candidates * candidates, axis=1, keepdims=True) + norm_eps
    )
    similarity = jnp.dot(cand_unit, anchor, precision=highest) / (emb_width * contrast_temp)
    top_score = lax.stop_gradient(jnp.max(similarity))
    contrast = top_score + jnp.log(jnp.sum(jnp.exp(similarity - top_score))) - similarity[0]
    return contrast + beta_weight * recon_error


def stacked_term(columns, first_grad, second_grad, in_first):
    contract = (((0,), (0,)), ((), ()))
    first_term = lax.dot_general(columns, first_grad, contract, preferred_element_type=jnp.float32)
    second_term = lax.dot_general(
        columns, second_grad, contract, preferred_element_type=jnp.float32
    )
    return jnp.where(in_first[:, None], first_term, second_term)


def cost(flops, moved):
    return pl.CostEstimate(flops=flops, bytes_accessed=moved, transcendentals=0)


def first_rows_in(shard, shard_rows, first_rows):
    return min(max(first_rows - shard * shard_rows, 0), shard_rows)


def unit_groups(shard_count, shard_rows, first_rows, part_count):
    groups = []
    for shard in range(shard_count):
        inside = first_rows_in(shard, shard_rows, first_rows)
        if inside < shard_rows:
            groups.append((shard, inside, shard * shard_rows + inside - first_rows, (shard_rows - inside) // part_count))
    return groups


def even_units(groups, shard_rows, part_count):
    return all(
        inside % TILE == 0 and share % TILE == 0 and inside + share * part_count == shard_rows
        for _, inside, _, share in groups
    )


def message_kernel(groups, rows_ref, message_ref, built, semaphores):
    shard, segment = lax.axis_index("dp"), lax.axis_index("segment")
    copies, _, columns = message_ref.shape
    shard_rows, width = rows_ref.shape
    segment_count = width // (SIDES * columns)
    first_last = groups[0][0]

    for part in range(segment_count):
        here = segment == part

        @pl.when((shard <= first_last) & here)
        def _(part=part):
            for side in range(SIDES):
                picked = []
                for _, _, base, share in groups:
                    start = base + share * (side * segment_count + part)
                    picked.append(rows_ref[:, start : start + share])
                built[side] = jnp.concatenate(picked, axis=1)

        for group_shard, inside, _, share in groups:

            @pl.when((shard == group_shard) & here)
            def _(part=part, inside=inside, share=share):
                for side in range(SIDES):
                    start = inside + share * (side * segment_count + part)
                    for block in range(width // columns):
                        lanes = slice(block * columns, (block + 1) * columns)
                        spot = inside + block * share
                        built[side, spot : spot + share, :] = rows_ref[start : start + share, lanes]

    sends = [
        pltpu.make_async_copy(built.at[copy % SIDES], message_ref.at[copy, :shard_rows], semaphores.at[copy]) for copy in range(copies)
    ]
    for send in sends:
        send.start()
    for send in sends:
        send.wait()


def weight_message(uniting_weights, groups, copies, columns):
    shard_rows = uniting_weights.shape[0]
    return pl.pallas_call(
        functools.partial(message_kernel, groups),
        in_specs=[pl.BlockSpec(memory_space=pltpu.VMEM)],
        out_specs=pl.BlockSpec(memory_space=pl.ANY),
        out_shape=jax.ShapeDtypeStruct((copies, shard_rows + 16, columns), BF16),
        scratch_shapes=[pltpu.VMEM((SIDES, shard_rows, columns), BF16), pltpu.SemaphoreType.DMA((copies,))],
        cost_estimate=cost(0, 4 * uniting_weights.size),
    )(uniting_weights)


def forward_kernel(
    groups,
    first_rows,
    embedded_ref,
    own_ref,
    weights,
    block_ref,
    hidden_ref,
    active_ref,
    second_ref,
    partial_ref,
):
    shard_count, _, columns = weights.shape
    shard_rows = block_ref.shape[1]
    shard = lax.axis_index("dp")
    source_count, source_items, width = embedded_ref.shape
    items = source_count * source_items
    embedded = embedded_ref[...].astype(F32).reshape(items, width)
    normed = embedded * lax.rsqrt(jnp.mean(embedded * embedded, axis=1, keepdims=True) + norm_eps)
    normed = normed.astype(BF16)
    hidden = jnp.zeros((items, columns), F32)
    own_block = jnp.zeros((items, shard_rows), BF16)
    for block in range(shard_count):
        inside = first_rows_in(block, shard_rows, first_rows)
        start = block * shard_rows
        if inside > 0:
            rows = normed[:, start : start + inside]
            hidden = hidden + dot_nn(rows, weights[block, :inside])
            if inside < shard_rows:
                rows = jnp.concatenate([rows, jnp.zeros((items, shard_rows - inside), BF16)], axis=1)
            own_block = jnp.where(shard == block, rows, own_block)
    block_ref[...] = own_block
    hidden_ref[...] = hidden
    active = gelu_value(hidden).astype(BF16)
    active_ref[...] = active
    offset = 0
    for block, inside, _, share in groups:
        for part in range(partial_ref.shape[1] // columns):
            second_ref[offset : offset + share, part * columns : (part + 1) * columns] = weights[
                block, inside + part * share : inside + (part + 1) * share, :
            ]
        offset += share
    partial_ref[...] = dot_nn(dot_nn(own_ref[...], active).astype(BF16), second_ref[...])


def merge_part(embedded_all, pieces, own, groups, shard_rows, first_rows, width):
    shard_count, _, columns = pieces.shape
    items = embedded_all.shape[0] * embedded_all.shape[1]
    vm = pl.BlockSpec(memory_space=pltpu.VMEM)
    return pl.pallas_call(
        functools.partial(forward_kernel, groups, first_rows),
        in_specs=[vm] * 3,
        out_specs=[vm] * 5,
        out_shape=[
            jax.ShapeDtypeStruct((items, shard_rows), BF16),
            jax.ShapeDtypeStruct((items, columns), F32),
            jax.ShapeDtypeStruct((items, columns), BF16),
            jax.ShapeDtypeStruct((columns, width), BF16),
            jax.ShapeDtypeStruct((own.shape[0], width), F32),
        ],
        cost_estimate=cost(2 * items * first_rows * columns, 2 * pieces.size),
        compiler_params=pltpu.CompilerParams(vmem_limit_bytes=8 * MIB),
    )(embedded_all, own, pieces)


def split(value):
    high = value.astype(BF16)
    return high, (value - high.astype(F32)).astype(BF16)


def exact_nt(value, high, low):
    first, second = split(value)
    rows = value.shape[0]
    both = dot_nt(jnp.concatenate([first, second], axis=0), high)
    return both[:rows] + both[rows:] + dot_nt(first, low)


def exact_nn(value, high, low):
    first, second = split(value)
    rows = value.shape[0]
    both = dot_nn(jnp.concatenate([first, second], axis=0), high)
    return both[:rows] + both[rows:] + dot_nn(first, low)


def dot_tn(a, b):
    return lax.dot_general(a, b, (((0,), (0,)), ((), ())), preferred_element_type=F32)


def exact_tn(a, b):
    a_high, a_low = split(a)
    b_high, b_low = split(b)
    return dot_tn(
        jnp.concatenate([a_high, a_low, a_high], axis=0), jnp.concatenate([b_high, b_high, b_low], axis=0)
    )


def square_sums(value):
    high, low = split(value * value)
    ones = jnp.ones((8, value.shape[1]), BF16)
    return dot_nt(ones, high) + dot_nt(ones, low)


def prepare_kernel(book_ref, bank_ref, high_ref, low_ref, norm_ref, scale_ref):
    width = bank_ref.shape[1]
    for level in range(book_ref.shape[0]):
        codes = book_ref[level]
        high, low = split(codes)
        high_ref[level] = high
        low_ref[level] = low
        norm_ref[level] = square_sums(codes)
    scale_ref[...] = lax.rsqrt(square_sums(bank_ref[...].astype(F32)) * (1.0 / width) + norm_eps)


def prepared(books, bank):
    levels, codes, _ = books.shape
    vm = pl.BlockSpec(memory_space=pltpu.VMEM)
    return pl.pallas_call(
        prepare_kernel,
        in_specs=[vm] * 2,
        out_specs=[vm] * 4,
        out_shape=[
            jax.ShapeDtypeStruct(books.shape, BF16),
            jax.ShapeDtypeStruct(books.shape, BF16),
            jax.ShapeDtypeStruct((levels, 8, codes), F32),
            jax.ShapeDtypeStruct((8, bank.shape[0]), F32),
        ],
        cost_estimate=cost(0, 12 * books.size),
        compiler_params=pltpu.CompilerParams(vmem_limit_bytes=10 * MIB),
    )(books, bank)


def quantizer_kernel(
    loss_scale,
    merged_ref,
    highs,
    lows,
    norm_ref,
    bank_ref,
    bank_scale_ref,
    count_ref,
    merged_grad_ref,
    loss_ref,
    left_ref,
    right_ref,
):
    width = merged_ref.shape[1]
    levels = highs.shape[0]
    inverse_tau = 2.0 / math.sqrt(width)
    inverse_temp = 1.0 / (width * contrast_temp)
    merged = merged_ref[...].astype(BF16).astype(F32)
    merged_scale = lax.rsqrt(jnp.mean(merged * merged, axis=1, keepdims=True) + norm_eps)
    residuals = [merged * merged_scale]
    shares, chosen_rows = [], []
    for level in range(levels):
        high, low = highs[level], lows[level]
        logits = (2.0 * exact_nt(residuals[level], high, low) - norm_ref[level]) * inverse_tau
        exps = jnp.exp(logits - jnp.max(logits, axis=1, keepdims=True))
        share = exps / jnp.sum(exps, axis=1, keepdims=True)
        chosen = exact_nn(share, high, low)
        shares.append(share)
        chosen_rows.append(chosen)
        residuals.append(residuals[level] - chosen)
    last = residuals[levels]
    quantized = chosen_rows[0]
    for chosen in chosen_rows[1:]:
        quantized = quantized + chosen
    anchor_scale = lax.rsqrt(jnp.mean(quantized * quantized, axis=1, keepdims=True) + norm_eps)
    anchor = quantized * anchor_scale
    own = jnp.sum(anchor * residuals[0], axis=1, keepdims=True) * inverse_temp
    bank = bank_ref[...]
    bank_scale = bank_scale_ref[...]
    anchor_parts = jnp.concatenate(split(anchor), axis=0)
    rows = anchor.shape[0]
    both = dot_nt(anchor_parts, bank)
    similar = (both[:rows] + both[rows:]) * bank_scale * inverse_temp
    counts = count_ref[...]
    named = counts > 0.0
    top = jnp.maximum(jnp.max(jnp.where(named, similar, own), axis=1, keepdims=True), own)
    bank_exps = jnp.where(named, jnp.exp(jnp.where(named, similar, top) - top), 0.0) * counts
    own_exp = jnp.exp(own - top)
    total = jnp.sum(bank_exps, axis=1, keepdims=True) + own_exp
    item_losses = top + jnp.log(total) - own + jnp.mean(last * last, axis=1, keepdims=True)
    loss_ref[0] = jnp.sum(item_losses) * loss_scale

    bank_weight = bank_exps / total * (loss_scale * inverse_temp)
    own_weight = (own_exp / total - 1.0) * (loss_scale * inverse_temp)
    weight_parts = jnp.concatenate(split(bank_weight * bank_scale), axis=0)
    both = dot_nn(weight_parts, bank)
    anchor_grad = both[:rows] + both[rows:] + own_weight * residuals[0]
    unit_grad = own_weight * anchor
    quantized_grad = anchor_scale * (anchor_grad - anchor * jnp.mean(anchor * anchor_grad, axis=1, keepdims=True))
    residual_grad = last * (2.0 * loss_scale / width)
    for level in reversed(range(levels)):
        high, low = highs[level], lows[level]
        chosen_grad = quantized_grad - residual_grad
        share_grad = exact_nt(chosen_grad, high, low)
        share = shares[level]
        logit_grad = share * (share_grad - jnp.sum(share * share_grad, axis=1, keepdims=True)) * (2.0 * inverse_tau)
        left_ref[level] = jnp.concatenate([share, logit_grad], axis=0)
        right_ref[level] = jnp.concatenate([chosen_grad, residuals[level]], axis=0)
        residual_grad = residual_grad + exact_nn(logit_grad, high, low)
    unit_grad = unit_grad + residual_grad
    unit = residuals[0]
    merged_grad = merged_scale * (unit_grad - unit * jnp.mean(unit * unit_grad, axis=1, keepdims=True))
    merged_grad_ref[...] = merged_grad.astype(BF16)


def quantizer(merged, ready, bank, counts, loss_scale):
    highs, lows, norms, bank_scale = ready
    levels, codes, width = highs.shape
    rows = merged.shape[0]
    vm = pl.BlockSpec(memory_space=pltpu.VMEM)
    return pl.pallas_call(
        functools.partial(quantizer_kernel, loss_scale),
        in_specs=[vm] * 7,
        out_specs=[vm, pl.BlockSpec(memory_space=pltpu.SMEM), vm, vm],
        out_shape=[
            jax.ShapeDtypeStruct(merged.shape, BF16),
            jax.ShapeDtypeStruct((1,), F32),
            jax.ShapeDtypeStruct((levels, 2 * rows, codes), F32),
            jax.ShapeDtypeStruct((levels, 2 * rows, width), F32),
        ],
        cost_estimate=cost(64 * highs.size, 4 * highs.size),
        compiler_params=pltpu.CompilerParams(vmem_limit_bytes=12 * MIB),
    )(merged, highs, lows, norms, bank, bank_scale, counts)


def codebook_kernel(left_ref, right_ref, book_ref, grad_ref):
    levels, doubled, _ = left_ref.shape
    width = right_ref.shape[2]
    rows = doubled // 2
    ones = jnp.ones((rows, 128), F32)
    for level in range(levels):
        outer = exact_tn(left_ref[level], right_ref[level])
        totals = exact_tn(left_ref[level, rows:], ones)
        for block in range(width // 128):
            span = slice(block * 128, (block + 1) * 128)
            grad_ref[level, :, span] = outer[:, span] - totals * book_ref[level, :, span]


def codebook_grad(left, right, books):
    vm = pl.BlockSpec(memory_space=pltpu.VMEM)
    return pl.pallas_call(
        codebook_kernel,
        in_specs=[vm] * 3,
        out_specs=vm,
        out_shape=jax.ShapeDtypeStruct(books.shape, F32),
        cost_estimate=cost(96 * books.size, 8 * books.size),
        compiler_params=pltpu.CompilerParams(vmem_limit_bytes=10 * MIB),
    )(left, right, books)


def backward_kernel(gathered_ref, order_ref, hidden_ref, active_ref, second_ref, out_grad_ref, sent_ref):
    owners, places, width = gathered_ref.shape
    columns = hidden_ref.shape[1]
    gathered = gathered_ref[...].astype(F32).reshape(owners * places, width).astype(BF16)
    out_grad = dot_tn(order_ref[...], gathered).astype(BF16)
    out_grad_ref[...] = out_grad
    hidden_grad = dot_nt(out_grad, second_ref[...]) * gelu_slope(hidden_ref[...])
    sent_ref[:, :columns] = hidden_grad.astype(BF16)
    sent_ref[:, columns:] = active_ref[...]


def backward_part(gathered, order, hidden, active, second):
    items, columns = hidden.shape
    vm = pl.BlockSpec(memory_space=pltpu.VMEM)
    return pl.pallas_call(
        backward_kernel,
        in_specs=[vm] * 5,
        out_specs=[vm] * 2,
        out_shape=[
            jax.ShapeDtypeStruct((items, gathered.shape[2]), BF16),
            jax.ShapeDtypeStruct((items, 2 * columns), BF16),
        ],
        cost_estimate=cost(2 * items * second.size, 2 * second.size),
        compiler_params=pltpu.CompilerParams(vmem_limit_bytes=8 * MIB),
    )(gathered, order, hidden, active, second)


def weight_grad_kernel(
    groups, block_ref, out_grad_ref, here_ref, row_ref, side_ref, corner_ref, grad_ref, hidden_grad, active
):
    shard, segment = lax.axis_index("dp"), lax.axis_index("segment")
    cores, items, doubled = here_ref.shape
    columns = doubled // 2
    shard_rows = block_ref.shape[1]
    own_side, own_row = lax.rem(shard, SIDES), segment // cores
    segment_count = hidden_grad.shape[1] // (SIDES * columns)

    def place_units(target, first):
        for side in range(SIDES):
            for other in range(segment_count):
                parts = [ref[other % cores, :, first : first + columns] for ref in (here_ref, row_ref, side_ref, corner_ref)]
                same_row = own_row == other // cores
                near = jnp.where(same_row, parts[0], parts[1])
                across = jnp.where(same_row, parts[2], parts[3])
                part = jnp.where(own_side == side, near, across)
                offset = 0
                for _, _, base, share in groups:
                    spot = base + share * (side * segment_count + other)
                    target[:, spot : spot + share] = part[:, offset : offset + share]
                    offset += share

    place_units(hidden_grad, 0)
    grad_ref[...] = dot_tn(block_ref[...], hidden_grad[...])
    for group_shard, inside, base, _ in groups:

        @pl.when(shard == group_shard)
        def _(inside=inside, base=base):
            place_units(active, columns)
            wanted = active[:, base : base + shard_rows - inside]
            grad_ref[inside:, :] = dot_tn(wanted, out_grad_ref[...])


def weight_grad(block, out_grad, parts, groups):
    items, shard_rows = block.shape
    width = out_grad.shape[1]
    vm = pl.BlockSpec(memory_space=pltpu.VMEM)
    return pl.pallas_call(
        functools.partial(weight_grad_kernel, groups),
        in_specs=[vm] * (2 + len(parts)),
        out_specs=vm,
        out_shape=jax.ShapeDtypeStruct((shard_rows, width), F32),
        scratch_shapes=[pltpu.VMEM((items, width), BF16), pltpu.VMEM((items, width), BF16)],
        cost_estimate=cost(2 * items * shard_rows * width, 4 * shard_rows * width),
        compiler_params=pltpu.CompilerParams(vmem_limit_bytes=8 * MIB),
    )(block, out_grad, *parts)


def around(near, across, segment_count, dp_count):
    row = lax.ppermute(near, "segment", [(j, j ^ 2) for j in range(segment_count)])
    side = lax.ppermute(across, "dp", [(i, i ^ 1) for i in range(dp_count)])
    corners = [
        (j * dp_count + i, (j ^ 2) * dp_count + (i ^ 1)) for j in range(segment_count) for i in range(dp_count)
    ]
    corner = lax.ppermute(across, ("segment", "dp"), corners)
    return row, side, corner


def spread(rows, axis_name, count):
    return lax.all_to_all(
        jnp.broadcast_to(rows[None], (count,) + rows.shape), axis_name, 0, 0, tiled=True
    )


def per_device_parts(
    images, texts, section_weights, uniting_weights, codebooks, neg_bank, item_cats, cat_slot, neg_index
):
    segment_index = lax.axis_index("segment")
    segment_count = lax.axis_size("segment")
    dp_index = lax.axis_index("dp")
    dp_count = lax.axis_size("dp")
    item_count, _, image_width = images.shape
    text_width = texts.shape[2]
    first_rows = image_width + text_width
    shard_rows, width = uniting_weights.shape
    columns = width // (SIDES * segment_count)
    groups = unit_groups(dp_count, shard_rows, first_rows, SIDES * segment_count)
    message = weight_message(uniting_weights, groups, dp_count, columns)
    flag = (1 - segment_index % 2).astype(jnp.int32).reshape(1)
    flag, message = lax.optimization_barrier((flag, message))
    pieces = lax.all_to_all(message, "dp", 0, 0, tiled=True)
    pooled = pooled_features(images, texts, section_weights, segment_index, flag)
    pooled = pooled + lax.ppermute(pooled, "segment", [(i, i ^ 1) for i in range(segment_count)])
    mine = pooled.astype(BF16)
    other = lax.ppermute(mine, "segment", [(i, i ^ 2) for i in range(segment_count)])
    is_image = segment_index < 2
    embedded = jnp.concatenate(
        [jnp.where(is_image, mine, other)[:, :image_width], jnp.where(is_image, other, mine)], axis=1
    )
    embedded, pieces, books = lax.optimization_barrier((embedded, pieces, codebooks[0]))
    embedded_all = spread(embedded, "dp", dp_count)

    pair = item_cats.shape[1] // dp_count
    cats = item_cats.reshape(segment_count, dp_count, pair).transpose(1, 0, 2).reshape(-1)
    items = cats.shape[0]
    slots = jnp.sum(
        jnp.where(cats[:, None] == jnp.arange(cat_slot.shape[0])[None, :], cat_slot[None, :], 0), axis=1
    )
    ids = jnp.arange(items)
    rank = jnp.sum(jnp.where((slots[None, :] == slots[:, None]) & (ids[None, :] < ids[:, None]), 1, 0), axis=1)
    owned = segment_count * CAP
    order = (ids[:, None] == (slots * owned + rank)[None, :]).astype(BF16)
    own = lax.dynamic_slice_in_dim(order, dp_index * owned, owned, 0)
    across_own = lax.dynamic_slice_in_dim(order, (dp_index ^ 1) * owned, owned, 0)
    both_own = jnp.concatenate([own, across_own], axis=0)
    negatives = neg_index.reshape(segment_count, dp_count, pair, -1).transpose(1, 0, 2, 3).reshape(items, -1)
    own_negatives = jnp.dot(own.astype(F32), negatives.astype(F32), precision=highest)
    bank = neg_bank[0]
    ready = prepared(books, bank)
    bank_ids = jnp.arange(bank.shape[0]).astype(F32)
    counts = jnp.sum((own_negatives[:, :, None] == bank_ids[None, None, :]).astype(F32), axis=1)

    block, hidden, active, second, partial = merge_part(
        embedded_all, pieces, both_own, groups, shard_rows, first_rows, width
    )
    partial = partial + lax.ppermute(partial, "segment", [(i, i ^ 1) for i in range(segment_count)])
    row, side, corner = around(partial[:owned], partial[owned:], segment_count, dp_count)
    merged = (partial[:owned] + row) + (side + corner)
    merged_grad, loss, left, right = quantizer(merged, ready, bank, counts, 1.0 / math.sqrt(items))
    gathered = spread(merged_grad, "dp", dp_count)
    book_grad = codebook_grad(left, right, books)
    out_grad, sent = backward_part(gathered, order, hidden, active, second)
    twin = lax.ppermute(sent, "segment", [(i, i ^ 1) for i in range(segment_count)])
    first_core = segment_index % 2 == 0
    here = jnp.stack([jnp.where(first_core, sent, twin), jnp.where(first_core, twin, sent)])
    parts = (here,) + around(here, here, segment_count, dp_count)
    uniting_grad = weight_grad(block, out_grad, parts, groups)
    return (uniting_grad, book_grad[None], loss)


def pooled_features(images, texts, section_weights, segment_index, flag):
    image_width, text_width = images.shape[2], texts.shape[2]

    def image_branch(operands):
        pooled = image_pooled(operands[0], operands[2], flag)
        return jnp.pad(pooled, ((0, 0), (0, text_width - image_width)))

    def text_branch(operands):
        return text_pooled(operands[1], operands[2], flag)

    return lax.cond(segment_index < 2, image_branch, text_branch, (images, texts, section_weights))


def per_device_gathered(
    images,
    texts,
    section_weights,
    uniting_weights,
    codebooks,
    neg_bank,
    item_cats,
    cat_slot,
    neg_index,
):
    segment_index = lax.axis_index("segment")
    segment_count = lax.axis_size("segment")
    dp_index = lax.axis_index("dp")
    dp_count = lax.axis_size("dp")
    group_index = segment_index % 2
    item_count = images.shape[0]

    flag = (1 - group_index).astype(jnp.int32).reshape(1)
    pooled = pooled_features(images, texts, section_weights, segment_index, flag)
    image_width = images.shape[2]
    is_image = segment_index < 2
    packed = jnp.concatenate(
        [jnp.where(is_image, pooled[:, :image_width], 0.0), jnp.where(is_image, 0.0, pooled)], axis=1
    )
    embedded = lax.psum_scatter(packed, "segment", scatter_dimension=0, tiled=True).astype(
        jnp.bfloat16
    )
    stacked = lax.all_gather(uniting_weights, "dp", axis=0, tiled=True)
    first_rows = embedded.shape[1]
    cat_per_dev = codebooks.shape[0]
    slot_count = cat_per_dev * CAP
    row_total = item_cats.shape[1]
    cats_all = item_cats.reshape(-1)
    entry_count = cats_all.shape[0]
    entry_ids = jnp.arange(entry_count)
    category_match = cats_all[:, None] == jnp.arange(cat_slot.shape[0])[None, :]
    entry_slots = jnp.sum(jnp.where(category_match, cat_slot[None, :], 0), axis=1)
    entry_owner = entry_slots // cat_per_dev
    entry_local = entry_slots % cat_per_dev
    entry_row = entry_ids // row_total
    earlier = entry_ids[None, :] < entry_ids[:, None]
    same_cat = (cats_all[:, None] == cats_all[None, :]) & (entry_row[:, None] == entry_row[None, :])
    entry_rank = jnp.sum(jnp.where(earlier & same_cat, 1, 0), axis=1)
    entry_place = entry_local * CAP + entry_rank
    entry_position = entry_row * slot_count + entry_place
    owned = entry_owner == dp_index
    all_slots = segment_count * slot_count
    slot_match_all = owned[None, :] & (entry_position[None, :] == jnp.arange(all_slots)[:, None])
    view_match = lax.dynamic_slice(
        slot_match_all,
        (segment_index * slot_count, segment_index * row_total),
        (slot_count, row_total),
    )
    view_base = segment_index * row_total
    view_slots = view_match.shape[0]
    selection = view_match.astype(jnp.bfloat16)
    valid = jnp.sum(view_match.astype(jnp.float32), axis=1)
    slot_item = jnp.sum(
        jnp.where(view_match, jnp.arange(view_match.shape[1])[None, :] + view_base, 0), axis=1
    )
    slot_negs = jnp.take(neg_index.reshape(entry_count, -1), slot_item, axis=0)
    slot_local = jnp.arange(view_slots) % slot_count // CAP
    bank_rows = neg_bank.reshape(-1, neg_bank.shape[2])
    negatives = jnp.take(bank_rows, slot_local[:, None] * neg_bank.shape[1] + slot_negs, axis=0)
    loss_scale = 1.0 / math.sqrt(dp_count * item_count)

    def owner_objective(merged_float, books):
        per_row = jax.vmap(item_loss)(merged_float, books[slot_local], negatives)
        return jnp.sum(per_row * valid) * loss_scale

    gathered = jnp.dot(
        selection,
        lax.all_gather(embedded, "dp", axis=0, tiled=True),
        preferred_element_type=jnp.float32,
    )
    gathered = gathered.astype(jnp.bfloat16)
    normed_all, hidden_all, activated_all, merged_all = merge_forward(gathered, stacked)
    loss_local, pullback = jax.vjp(owner_objective, merged_all.astype(jnp.float32), codebooks)
    grad_all, book_grad = pullback(jnp.ones((), jnp.float32))
    out_grad = grad_all.astype(jnp.bfloat16)
    hidden_grad = merge_backward(hidden_all, stacked, out_grad, first_rows)
    joined = jnp.concatenate([normed_all, activated_all], axis=1)
    book_total, loss_owner = lax.psum((book_grad, loss_local), "segment")
    shard_rows = uniting_weights.shape[0]
    shard_start = dp_index * shard_rows
    shard_first = shard_start + jnp.arange(shard_rows) < first_rows
    joined_piece = lax.all_gather(joined, "dp", axis=0, tiled=True)
    first_piece = lax.all_gather(hidden_grad, "dp", axis=0, tiled=True)
    second_piece = lax.all_gather(out_grad, "dp", axis=0, tiled=True)
    columns = lax.dynamic_slice_in_dim(joined_piece, shard_start, shard_rows, 1)
    segment_grad = stacked_term(columns, first_piece, second_piece, shard_first)
    uniting_grad = lax.psum(segment_grad, "segment")
    return (uniting_grad, book_total, loss_owner.reshape(1))


def per_device(*operands):
    images, texts, _, uniting_weights = operands[:4]
    segment_count, dp_count = lax.axis_size("segment"), lax.axis_size("dp")
    shard_rows = uniting_weights.shape[0]
    first_rows = images.shape[2] + texts.shape[2]
    groups = unit_groups(dp_count, shard_rows, first_rows, SIDES * segment_count)
    if dp_count % SIDES == 0 and even_units(groups, shard_rows, SIDES * segment_count):
        return per_device_parts(*operands)
    return per_device_gathered(*operands)


def solution(mesh):
    placed = (
        P("dp", None, None),
        P("dp", None, None),
        P("segment", None, None),
        P("dp", None),
        P("dp", None, None, None),
        P("dp", None, None),
        P(),
        P(),
        P(),
    )
    return jax.shard_map(
        per_device,
        mesh=mesh,
        in_specs=placed,
        out_specs=(P("dp", None), P("dp", None, None, None), P("dp")),
        check_vma=False,
    )
```

```python
import functools
import math

import jax
import jax.numpy as jnp
import numpy as np
from jax import lax
from jax.experimental import pallas as pl
from jax.experimental.pallas import tpu as pltpu
from jax.sharding import PartitionSpec as P

F32 = jnp.float32
BF16 = jnp.bfloat16

HEAD_IMG = 64
HEAD_TXT = 128
CAP = 2
OWNED = 4 * CAP
MIB = 1024 * 1024
IMAGE_GROUP = 4
LOG2_E = 1.4426950408889634
SIDES = 2
TILE = 8


norm_eps = 1e-06
rope_theta = 1000000.0
contrast_temp = 0.1
beta_weight = 1.0
highest = lax.Precision.HIGHEST


def gelu_value(inputs_f):
    return 0.5 * inputs_f * (1.0 + lax.erf(inputs_f / math.sqrt(2.0)))


def gelu_slope(inputs_f):
    return 0.5 * (1.0 + lax.erf(inputs_f / math.sqrt(2.0))) + inputs_f * jnp.exp(
        -0.5 * inputs_f * inputs_f
    ) / math.sqrt(2.0 * math.pi)


def dot_nt(a, b):
    return lax.dot_general(a, b, (((1,), (1,)), ((), ())), preferred_element_type=F32)

def dot_nn(a, b):
    return jnp.dot(a, b, preferred_element_type=F32)

def two_parts(value):
    high = value.astype(BF16)
    return jnp.concatenate([high, (value - high.astype(F32)).astype(BF16)], axis=0)

def dot_two(value, weights):
    rows = value.shape[0]
    both = dot_nn(two_parts(value), weights)
    return both[:rows] + both[rows:]

def unfold(slot_ref, first, out_ref, wide_ref, row_step):
    rows, columns = out_ref.shape
    blocks = columns // 128
    def body(step, carry):
        start = pl.multiple_of(step * row_step, row_step)
        source = pl.multiple_of(first + step * (row_step * blocks), 16)
        wide_ref[0 : row_step * blocks, :] = slot_ref[0, pl.ds(source, row_step * blocks), :].astype(F32)
        for block in range(blocks):
            piece = wide_ref[pl.ds(block, row_step, stride=blocks), :]
            out_ref[pl.ds(start, row_step), block * 128 : (block + 1) * 128] = piece.astype(BF16)
        return carry
    lax.fori_loop(0, rows // row_step, body, 0)

def image_kernel(flag_ref, image_ref, slot_ref, pooled_ref, w_in, w_out, wide, heads_mean):
    step = pl.program_id(0)
    item_count, model_width = pooled_ref.shape
    half_width = model_width // 2
    head_count = half_width // HEAD_IMG
    group, patch_count, _ = image_ref.shape

    @pl.when(step == 0)
    def _():
        unfold(slot_ref, 0, w_in, wide, 128)
        unfold(slot_ref, model_width * 12, w_out, wide, 128)

    tokens = image_ref[...].reshape(group * patch_count, model_width).astype(F32)
    centred = tokens - jnp.mean(tokens, axis=1, keepdims=True)
    variance = jnp.mean(centred * centred, axis=1, keepdims=True)
    normed = (centred * lax.rsqrt(variance + norm_eps)).astype(BF16)
    queries = (dot_nn(normed, w_in[:, :half_width]) * (LOG2_E / math.sqrt(HEAD_IMG))).astype(BF16)
    keys = dot_nn(normed, w_in[:, half_width : 2 * half_width]).astype(BF16)
    row_ids = lax.broadcasted_iota(jnp.int32, (head_count, patch_count), 0)
    flag = flag_ref[0].astype(F32)
    for member in range(group):
        rows = slice(member * patch_count, (member + 1) * patch_count)
        weights = jnp.zeros((head_count, patch_count), F32)
        for head in range(head_count):
            span = slice(head * HEAD_IMG, (head + 1) * HEAD_IMG)
            scores = dot_nt(queries[rows, span], keys[rows, span])
            exps = jnp.exp2(scores - jnp.max(scores, axis=1, keepdims=True))
            share = (1.0 / patch_count) / jnp.sum(exps, axis=1, keepdims=True)
            mean_share = jnp.sum(exps * share, axis=0, keepdims=True)
            weights = weights + jnp.where(row_ids == head, mean_share, 0.0)
        item = step * group + member
        heads_mean[pl.ds(item * head_count, head_count), :] = dot_two(weights, normed[rows])
        pooled_ref[pl.ds(item, 1), :] = jnp.mean(tokens[rows], axis=0, keepdims=True) * flag

    @pl.when(step == item_count // group - 1)
    def _():
        values = dot_two(heads_mean[...], w_in[:, 2 * half_width :])
        rows = lax.broadcasted_iota(jnp.int32, values.shape, 0)
        columns = lax.broadcasted_iota(jnp.int32, values.shape, 1)
        values = jnp.where(rows % head_count == columns // HEAD_IMG, values, 0.0)
        attended = jnp.sum(values.reshape(item_count, head_count, half_width), axis=1)
        pooled_ref[...] += dot_two(attended, w_out[...])

def image_pooled(images, slot, flag):
    item_count, patch_count, model_width = images.shape
    half_width = model_width // 2
    head_count = half_width // HEAD_IMG
    return pl.pallas_call(
        image_kernel,
        grid=(item_count // IMAGE_GROUP,),
        in_specs=[
            pl.BlockSpec(memory_space=pltpu.SMEM),
            pl.BlockSpec((IMAGE_GROUP, patch_count, model_width), lambda i: (i, 0, 0)),
            pl.BlockSpec((1, 16 * model_width, 128), lambda i: (0, 0, 0), pipeline_mode=pl.Buffered(1)),
        ],
        out_specs=pl.BlockSpec((item_count, model_width), lambda i: (0, 0)),
        out_shape=jax.ShapeDtypeStruct((item_count, model_width), F32),
        scratch_shapes=[
            pltpu.VMEM((model_width, 3 * half_width), BF16),
            pltpu.VMEM((half_width, model_width), BF16),
            pltpu.VMEM((128 * 12, 128), F32),
            pltpu.VMEM((item_count * head_count, model_width), F32),
        ],
        compiler_params=pltpu.CompilerParams(vmem_limit_bytes=40 * 1024 * 1024),
    )(flag, images, slot)

def rope_tables(tokens, repeats):
    half = HEAD_TXT // 2
    exponents = np.arange(half).astype(np.float32) * np.float32(2.0 / HEAD_TXT)
    inverse = np.exp(np.float32(-math.log(rope_theta)) * exponents).astype(np.float32)
    angles = (np.arange(tokens).astype(np.float32)[:, None] * inverse[None, :]).astype(np.float32)
    cosine = np.concatenate([np.cos(angles), np.cos(angles)], axis=1)
    sine = np.concatenate([-np.sin(angles), np.sin(angles)], axis=1)
    return np.tile(cosine, (repeats, 1)).astype(np.float32), np.tile(sine, (repeats, 1)).astype(np.float32)

def text_kernel(flag_ref, text_ref, slot_ref, cos_ref, sin_ref, pooled_ref, w_in, w_out, wide, heads_mean):
    item_count, token_count, model_width = text_ref.shape
    half_width = model_width // 2
    head_count = half_width // HEAD_TXT
    unfold(slot_ref, 0, w_in, wide, 128)
    unfold(slot_ref, model_width * 8, w_out, wide, 128)
    tokens = text_ref[...].reshape(item_count * token_count, model_width).astype(F32)
    normed = (tokens * lax.rsqrt(jnp.mean(tokens * tokens, axis=1, keepdims=True) + norm_eps)).astype(BF16)
    residual = jnp.mean(tokens.reshape(item_count, token_count, model_width), axis=1)
    cosine, sine = cos_ref[...], sin_ref[...]

    def head_columns(head):
        return dot_nn(normed, w_in[:, head * HEAD_TXT : (head + 1) * HEAD_TXT])

    def turned(head, scale):
        part = head_columns(head)
        return ((part * cosine + pltpu.roll(part, HEAD_TXT // 2, 1) * sine).astype(BF16)).astype(F32) * scale

    queries = [(turned(head, 1.0)).astype(BF16) for head in range(head_count)]
    keys = turned(head_count, 1.0).astype(BF16)
    values = head_columns(head_count + 1).astype(BF16)
    wide_columns = head_count * token_count
    key_ids = lax.broadcasted_iota(jnp.int32, (token_count, wide_columns), 0)
    query_ids = lax.broadcasted_iota(jnp.int32, (token_count, wide_columns), 1) % token_count
    allowed = key_ids <= query_ids
    own_head = lax.broadcasted_iota(jnp.int32, (8, wide_columns), 0) == (
        lax.broadcasted_iota(jnp.int32, (8, wide_columns), 1) // token_count
    )
    for item in range(item_count):
        span = slice(item * token_count, (item + 1) * token_count)
        asked = jnp.concatenate([query[span] for query in queries], axis=0)
        scores = dot_nt(keys[span], asked) * (1.0 / math.sqrt(HEAD_TXT))
        scores = jnp.where(allowed, scores, -1e30)
        exps = jnp.exp(scores - jnp.max(scores, axis=0, keepdims=True))
        share = (1.0 / token_count) / jnp.sum(exps, axis=0, keepdims=True)
        share = jnp.where(own_head, share, 0.0).astype(BF16)
        weights = dot_nt(share, exps.astype(BF16))
        heads_mean[:, item, :] = dot_two(weights, values[span])
    pooled = residual * flag_ref[0].astype(F32)
    for head in range(head_count):
        pooled = pooled + dot_two(heads_mean[head], w_out[head * HEAD_TXT : (head + 1) * HEAD_TXT, :])
    pooled_ref[...] = pooled

def text_pooled(texts, slot, flag):
    item_count, token_count, model_width = texts.shape
    half_width = model_width // 2
    inner = half_width + 2 * HEAD_TXT
    cosine, sine = rope_tables(token_count, item_count)
    vm = pl.BlockSpec(memory_space=pltpu.VMEM)
    return pl.pallas_call(
        text_kernel,
        in_specs=[pl.BlockSpec(memory_space=pltpu.SMEM)] + [vm] * 4,
        out_specs=vm,
        out_shape=jax.ShapeDtypeStruct((item_count, model_width), F32),
        scratch_shapes=[
            pltpu.VMEM((model_width, inner), BF16),
            pltpu.VMEM((half_width, model_width), BF16),
            pltpu.VMEM((128 * 12, 128), F32),
            pltpu.VMEM((8, item_count, HEAD_TXT), F32),
        ],
        compiler_params=pltpu.CompilerParams(vmem_limit_bytes=40 * 1024 * 1024),
    )(flag, texts, slot, jnp.asarray(cosine), jnp.asarray(sine))

def merge_forward(embedded, stacked):
    first_rows = embedded.shape[1]
    float_embed = embedded.astype(jnp.float32)
    normed = (
        float_embed
        * lax.rsqrt(jnp.mean(float_embed * float_embed, axis=1, keepdims=True) + norm_eps)
    ).astype(jnp.bfloat16)
    hidden = jnp.dot(normed, stacked[:first_rows], preferred_element_type=jnp.float32)
    activated = gelu_value(hidden).astype(jnp.bfloat16)
    merged = jnp.dot(activated, stacked[first_rows:], preferred_element_type=jnp.float32).astype(
        jnp.bfloat16
    )
    return (normed, hidden, activated, merged)


def merge_backward(hidden, stacked, out_grad, first_rows):
    w_second = stacked[first_rows:]
    act_grad = lax.dot_general(
        out_grad, w_second, (((1,), (1,)), ((), ())), preferred_element_type=jnp.float32
    )
    return (act_grad * gelu_slope(hidden)).astype(jnp.bfloat16)


def item_loss(merged_row, book_rows, negatives):
    emb_width = merged_row.shape[0]
    quant_tau = math.sqrt(emb_width) / 2.0
    residual = merged_row * lax.rsqrt(jnp.mean(merged_row * merged_row) + norm_eps)
    quantized = jnp.zeros_like(merged_row)
    for level_index in range(book_rows.shape[0]):
        code_rows = book_rows[level_index]
        cross_terms = jnp.dot(code_rows, residual, precision=highest)
        logits = (2.0 * cross_terms - jnp.sum(code_rows * code_rows, axis=1)) / quant_tau
        logits = logits - lax.stop_gradient(jnp.max(logits))
        exp_logits = jnp.exp(logits)
        chosen = jnp.dot(exp_logits / jnp.sum(exp_logits), code_rows, precision=highest)
        residual = residual - chosen
        quantized = quantized + chosen
    recon_error = jnp.mean(residual * residual)
    anchor = quantized * lax.rsqrt(jnp.mean(quantized * quantized) + norm_eps)
    candidates = jnp.concatenate([merged_row[None, :], negatives.astype(jnp.float32)], axis=0)
    cand_unit = candidates * lax.rsqrt(
        jnp.mean(candidates * candidates, axis=1, keepdims=True) + norm_eps
    )
    similarity = jnp.dot(cand_unit, anchor, precision=highest) / (emb_width * contrast_temp)
    top_score = lax.stop_gradient(jnp.max(similarity))
    contrast = top_score + jnp.log(jnp.sum(jnp.exp(similarity - top_score))) - similarity[0]
    return contrast + beta_weight * recon_error


def stacked_term(columns, first_grad, second_grad, in_first):
    contract = (((0,), (0,)), ((), ()))
    first_term = lax.dot_general(columns, first_grad, contract, preferred_element_type=jnp.float32)
    second_term = lax.dot_general(
        columns, second_grad, contract, preferred_element_type=jnp.float32
    )
    return jnp.where(in_first[:, None], first_term, second_term)


def cost(flops, moved):
    return pl.CostEstimate(flops=flops, bytes_accessed=moved, transcendentals=0)


def first_rows_in(shard, shard_rows, first_rows):
    return min(max(first_rows - shard * shard_rows, 0), shard_rows)


def unit_groups(shard_count, shard_rows, first_rows, part_count):
    groups = []
    for shard in range(shard_count):
        inside = first_rows_in(shard, shard_rows, first_rows)
        if inside < shard_rows:
            groups.append((shard, inside, shard * shard_rows + inside - first_rows, (shard_rows - inside) // part_count))
    return groups


def even_units(groups, shard_rows, part_count):
    return all(
        inside % TILE == 0 and share % TILE == 0 and inside + share * part_count == shard_rows
        for _, inside, _, share in groups
    )


def message_kernel(groups, rows_ref, message_ref, built, semaphores):
    shard, segment = lax.axis_index("dp"), lax.axis_index("segment")
    copies, _, columns = message_ref.shape
    shard_rows, width = rows_ref.shape
    segment_count = width // (SIDES * columns)
    first_last = groups[0][0]

    for part in range(segment_count):
        here = segment == part

        @pl.when((shard <= first_last) & here)
        def _(part=part):
            for side in range(SIDES):
                picked = []
                for _, _, base, share in groups:
                    start = base + share * (side * segment_count + part)
                    picked.append(rows_ref[:, start : start + share])
                built[side] = jnp.concatenate(picked, axis=1)

        for group_shard, inside, _, share in groups:

            @pl.when((shard == group_shard) & here)
            def _(part=part, inside=inside, share=share):
                for side in range(SIDES):
                    start = inside + share * (side * segment_count + part)
                    for block in range(width // columns):
                        lanes = slice(block * columns, (block + 1) * columns)
                        spot = inside + block * share
                        built[side, spot : spot + share, :] = rows_ref[start : start + share, lanes]

    sends = [
        pltpu.make_async_copy(built.at[copy % SIDES], message_ref.at[copy, :shard_rows], semaphores.at[copy]) for copy in range(copies)
    ]
    for send in sends:
        send.start()
    for send in sends:
        send.wait()


def weight_message(uniting_weights, groups, copies, columns):
    shard_rows = uniting_weights.shape[0]
    return pl.pallas_call(
        functools.partial(message_kernel, groups),
        in_specs=[pl.BlockSpec(memory_space=pltpu.VMEM)],
        out_specs=pl.BlockSpec(memory_space=pl.ANY),
        out_shape=jax.ShapeDtypeStruct((copies, shard_rows + 16, columns), BF16),
        scratch_shapes=[pltpu.VMEM((SIDES, shard_rows, columns), BF16), pltpu.SemaphoreType.DMA((copies,))],
        cost_estimate=cost(0, 4 * uniting_weights.size),
    )(uniting_weights)


def forward_kernel(
    groups,
    first_rows,
    mine_ref,
    twin_ref,
    own_ref,
    weights,
    block_ref,
    hidden_ref,
    active_ref,
    second_ref,
    partial_ref,
):
    shard_count, _, columns = weights.shape
    shard_rows = block_ref.shape[1]
    shard = lax.axis_index("dp")
    source_count, source_items, half = mine_ref.shape
    items, width = source_count * source_items, 2 * half
    mine = mine_ref[...].astype(F32).reshape(items, half)
    twin = twin_ref[...].astype(F32).reshape(items, half)
    first_core = lax.rem(lax.axis_index("segment"), 2) == 0
    embedded = jnp.concatenate([jnp.where(first_core, mine, twin), jnp.where(first_core, twin, mine)], axis=1)
    normed = embedded * lax.rsqrt(jnp.mean(embedded * embedded, axis=1, keepdims=True) + norm_eps)
    normed = normed.astype(BF16)
    hidden = jnp.zeros((items, columns), F32)
    own_block = jnp.zeros((items, shard_rows), BF16)
    for block in range(shard_count):
        inside = first_rows_in(block, shard_rows, first_rows)
        start = block * shard_rows
        if inside > 0:
            rows = normed[:, start : start + inside]
            hidden = hidden + dot_nn(rows, weights[block, :inside])
            if inside < shard_rows:
                rows = jnp.concatenate([rows, jnp.zeros((items, shard_rows - inside), BF16)], axis=1)
            own_block = jnp.where(shard == block, rows, own_block)
    block_ref[...] = own_block
    hidden_ref[...] = hidden
    active = gelu_value(hidden).astype(BF16)
    active_ref[...] = active
    offset = 0
    for block, inside, _, share in groups:
        for part in range(partial_ref.shape[1] // columns):
            second_ref[offset : offset + share, part * columns : (part + 1) * columns] = weights[
                block, inside + part * share : inside + (part + 1) * share, :
            ]
        offset += share
    partial_ref[...] = dot_nn(dot_nn(own_ref[...], active).astype(BF16), second_ref[...])


def merge_part(mine_half, twin_half, pieces, own, groups, shard_rows, first_rows, width):
    shard_count, _, columns = pieces.shape
    items = mine_half.shape[0] * mine_half.shape[1]
    vm = pl.BlockSpec(memory_space=pltpu.VMEM)
    return pl.pallas_call(
        functools.partial(forward_kernel, groups, first_rows),
        in_specs=[vm] * 4,
        out_specs=[vm] * 5,
        out_shape=[
            jax.ShapeDtypeStruct((items, shard_rows), BF16),
            jax.ShapeDtypeStruct((items, columns), F32),
            jax.ShapeDtypeStruct((items, columns), BF16),
            jax.ShapeDtypeStruct((columns, width), BF16),
            jax.ShapeDtypeStruct((own.shape[0], width), F32),
        ],
        cost_estimate=cost(2 * items * first_rows * columns, 2 * pieces.size),
        compiler_params=pltpu.CompilerParams(vmem_limit_bytes=8 * MIB),
    )(mine_half, twin_half, own, pieces)


def split(value):
    high = value.astype(BF16)
    return high, (value - high.astype(F32)).astype(BF16)


def exact_nt(value, high, low):
    first, second = split(value)
    rows = value.shape[0]
    both = dot_nt(jnp.concatenate([first, second], axis=0), high)
    return both[:rows] + both[rows:] + dot_nt(first, low)


def exact_nn(value, high, low):
    first, second = split(value)
    rows = value.shape[0]
    both = dot_nn(jnp.concatenate([first, second], axis=0), high)
    return both[:rows] + both[rows:] + dot_nn(first, low)


def dot_tn(a, b):
    return lax.dot_general(a, b, (((0,), (0,)), ((), ())), preferred_element_type=F32)


def exact_tn(a, b):
    a_high, a_low = split(a)
    b_high, b_low = split(b)
    return dot_tn(
        jnp.concatenate([a_high, a_low, a_high], axis=0), jnp.concatenate([b_high, b_high, b_low], axis=0)
    )


def square_sums(value):
    high, low = split(value * value)
    ones = jnp.ones((8, value.shape[1]), BF16)
    return dot_nt(ones, high) + dot_nt(ones, low)


def prepare_kernel(book_ref, bank_ref, high_ref, low_ref, norm_ref, scale_ref):
    width = bank_ref.shape[1]
    for level in range(book_ref.shape[0]):
        codes = book_ref[level]
        high, low = split(codes)
        high_ref[level] = high
        low_ref[level] = low
        norm_ref[level] = square_sums(codes)
    scale_ref[...] = lax.rsqrt(square_sums(bank_ref[...].astype(F32)) * (1.0 / width) + norm_eps)


def prepared(books, bank):
    levels, codes, _ = books.shape
    vm = pl.BlockSpec(memory_space=pltpu.VMEM)
    return pl.pallas_call(
        prepare_kernel,
        in_specs=[vm] * 2,
        out_specs=[vm] * 4,
        out_shape=[
            jax.ShapeDtypeStruct(books.shape, BF16),
            jax.ShapeDtypeStruct(books.shape, BF16),
            jax.ShapeDtypeStruct((levels, 8, codes), F32),
            jax.ShapeDtypeStruct((8, bank.shape[0]), F32),
        ],
        cost_estimate=cost(0, 12 * books.size),
        compiler_params=pltpu.CompilerParams(vmem_limit_bytes=10 * MIB),
    )(books, bank)


def quantizer_kernel(
    loss_scale,
    merged_ref,
    highs,
    lows,
    norm_ref,
    bank_ref,
    bank_scale_ref,
    count_ref,
    merged_grad_ref,
    loss_ref,
    left_ref,
    right_ref,
):
    width = merged_ref.shape[1]
    levels = highs.shape[0]
    inverse_tau = 2.0 / math.sqrt(width)
    inverse_temp = 1.0 / (width * contrast_temp)
    merged = merged_ref[...].astype(BF16).astype(F32)
    merged_scale = lax.rsqrt(jnp.mean(merged * merged, axis=1, keepdims=True) + norm_eps)
    residuals = [merged * merged_scale]
    shares, chosen_rows = [], []
    for level in range(levels):
        high, low = highs[level], lows[level]
        logits = (2.0 * exact_nt(residuals[level], high, low) - norm_ref[level]) * inverse_tau
        exps = jnp.exp(logits - jnp.max(logits, axis=1, keepdims=True))
        share = exps / jnp.sum(exps, axis=1, keepdims=True)
        chosen = exact_nn(share, high, low)
        shares.append(share)
        chosen_rows.append(chosen)
        residuals.append(residuals[level] - chosen)
    last = residuals[levels]
    quantized = chosen_rows[0]
    for chosen in chosen_rows[1:]:
        quantized = quantized + chosen
    anchor_scale = lax.rsqrt(jnp.mean(quantized * quantized, axis=1, keepdims=True) + norm_eps)
    anchor = quantized * anchor_scale
    own = jnp.sum(anchor * residuals[0], axis=1, keepdims=True) * inverse_temp
    bank = bank_ref[...]
    bank_scale = bank_scale_ref[...]
    anchor_parts = jnp.concatenate(split(anchor), axis=0)
    rows = anchor.shape[0]
    both = dot_nt(anchor_parts, bank)
    similar = (both[:rows] + both[rows:]) * bank_scale * inverse_temp
    counts = count_ref[...]
    named = counts > 0.0
    top = jnp.maximum(jnp.max(jnp.where(named, similar, own), axis=1, keepdims=True), own)
    bank_exps = jnp.where(named, jnp.exp(jnp.where(named, similar, top) - top), 0.0) * counts
    own_exp = jnp.exp(own - top)
    total = jnp.sum(bank_exps, axis=1, keepdims=True) + own_exp
    item_losses = top + jnp.log(total) - own + jnp.mean(last * last, axis=1, keepdims=True)
    loss_ref[0] = jnp.sum(item_losses) * loss_scale

    bank_weight = bank_exps / total * (loss_scale * inverse_temp)
    own_weight = (own_exp / total - 1.0) * (loss_scale * inverse_temp)
    weight_parts = jnp.concatenate(split(bank_weight * bank_scale), axis=0)
    both = dot_nn(weight_parts, bank)
    anchor_grad = both[:rows] + both[rows:] + own_weight * residuals[0]
    unit_grad = own_weight * anchor
    quantized_grad = anchor_scale * (anchor_grad - anchor * jnp.mean(anchor * anchor_grad, axis=1, keepdims=True))
    residual_grad = last * (2.0 * loss_scale / width)
    for level in reversed(range(levels)):
        high, low = highs[level], lows[level]
        chosen_grad = quantized_grad - residual_grad
        share_grad = exact_nt(chosen_grad, high, low)
        share = shares[level]
        logit_grad = share * (share_grad - jnp.sum(share * share_grad, axis=1, keepdims=True)) * (2.0 * inverse_tau)
        left_ref[level] = jnp.concatenate([share, logit_grad], axis=0)
        right_ref[level] = jnp.concatenate([chosen_grad, residuals[level]], axis=0)
        residual_grad = residual_grad + exact_nn(logit_grad, high, low)
    unit_grad = unit_grad + residual_grad
    unit = residuals[0]
    merged_grad = merged_scale * (unit_grad - unit * jnp.mean(unit * unit_grad, axis=1, keepdims=True))
    merged_grad_ref[...] = merged_grad.astype(BF16)


def quantizer(merged, ready, bank, counts, loss_scale):
    highs, lows, norms, bank_scale = ready
    levels, codes, width = highs.shape
    rows = merged.shape[0]
    vm = pl.BlockSpec(memory_space=pltpu.VMEM)
    return pl.pallas_call(
        functools.partial(quantizer_kernel, loss_scale),
        in_specs=[vm] * 7,
        out_specs=[vm, pl.BlockSpec(memory_space=pltpu.SMEM), vm, vm],
        out_shape=[
            jax.ShapeDtypeStruct(merged.shape, BF16),
            jax.ShapeDtypeStruct((1,), F32),
            jax.ShapeDtypeStruct((levels, 2 * rows, codes), F32),
            jax.ShapeDtypeStruct((levels, 2 * rows, width), F32),
        ],
        cost_estimate=cost(64 * highs.size, 4 * highs.size),
        compiler_params=pltpu.CompilerParams(vmem_limit_bytes=12 * MIB),
    )(merged, highs, lows, norms, bank, bank_scale, counts)


def codebook_kernel(left_ref, right_ref, book_ref, grad_ref):
    levels, doubled, _ = left_ref.shape
    width = right_ref.shape[2]
    rows = doubled // 2
    ones = jnp.ones((rows, 128), F32)
    for level in range(levels):
        outer = exact_tn(left_ref[level], right_ref[level])
        totals = exact_tn(left_ref[level, rows:], ones)
        for block in range(width // 128):
            span = slice(block * 128, (block + 1) * 128)
            grad_ref[level, :, span] = outer[:, span] - totals * book_ref[level, :, span]


def codebook_grad(left, right, books):
    vm = pl.BlockSpec(memory_space=pltpu.VMEM)
    return pl.pallas_call(
        codebook_kernel,
        in_specs=[vm] * 3,
        out_specs=vm,
        out_shape=jax.ShapeDtypeStruct(books.shape, F32),
        cost_estimate=cost(96 * books.size, 8 * books.size),
        compiler_params=pltpu.CompilerParams(vmem_limit_bytes=10 * MIB),
    )(left, right, books)


def backward_kernel(gathered_ref, order_ref, hidden_ref, active_ref, second_ref, out_grad_ref, sent_ref):
    owners, places, width = gathered_ref.shape
    columns = hidden_ref.shape[1]
    gathered = gathered_ref[...].astype(F32).reshape(owners * places, width).astype(BF16)
    out_grad = dot_tn(order_ref[...], gathered).astype(BF16)
    out_grad_ref[...] = out_grad
    hidden_grad = dot_nt(out_grad, second_ref[...]) * gelu_slope(hidden_ref[...])
    sent_ref[:, :columns] = hidden_grad.astype(BF16)
    sent_ref[:, columns:] = active_ref[...]


def backward_part(gathered, order, hidden, active, second):
    items, columns = hidden.shape
    vm = pl.BlockSpec(memory_space=pltpu.VMEM)
    return pl.pallas_call(
        backward_kernel,
        in_specs=[vm] * 5,
        out_specs=[vm] * 2,
        out_shape=[
            jax.ShapeDtypeStruct((items, gathered.shape[2]), BF16),
            jax.ShapeDtypeStruct((items, 2 * columns), BF16),
        ],
        cost_estimate=cost(2 * items * second.size, 2 * second.size),
        compiler_params=pltpu.CompilerParams(vmem_limit_bytes=8 * MIB),
    )(gathered, order, hidden, active, second)


def weight_grad_kernel(
    groups, block_ref, out_grad_ref, mine_ref, twin_ref, grad_ref, hidden_grad, active
):
    shard, segment = lax.axis_index("dp"), lax.axis_index("segment")
    _, items, doubled = mine_ref.shape
    cores = 2
    own_core = lax.rem(segment, cores)
    columns = doubled // 2
    shard_rows = block_ref.shape[1]
    own_side, own_row = lax.rem(shard, SIDES), segment // cores
    segment_count = hidden_grad.shape[1] // (SIDES * columns)

    def place_units(target, first):
        for side in range(SIDES):
            for other in range(segment_count):
                parts = [
                    jnp.where(
                        own_core == other % cores,
                        mine_ref[index, :, first : first + columns],
                        twin_ref[index, :, first : first + columns],
                    )
                    for index in range(4)
                ]
                same_row = own_row == other // cores
                near = jnp.where(same_row, parts[0], parts[1])
                across = jnp.where(same_row, parts[2], parts[3])
                part = jnp.where(own_side == side, near, across)
                offset = 0
                for _, _, base, share in groups:
                    spot = base + share * (side * segment_count + other)
                    target[:, spot : spot + share] = part[:, offset : offset + share]
                    offset += share

    place_units(hidden_grad, 0)
    grad_ref[...] = dot_tn(block_ref[...], hidden_grad[...])
    for group_shard, inside, base, _ in groups:

        @pl.when(shard == group_shard)
        def _(inside=inside, base=base):
            place_units(active, columns)
            wanted = active[:, base : base + shard_rows - inside]
            grad_ref[inside:, :] = dot_tn(wanted, out_grad_ref[...])


def weight_grad(block, out_grad, mine, twin, groups):
    items, shard_rows = block.shape
    width = out_grad.shape[1]
    vm = pl.BlockSpec(memory_space=pltpu.VMEM)
    return pl.pallas_call(
        functools.partial(weight_grad_kernel, groups),
        in_specs=[vm] * 4,
        out_specs=vm,
        out_shape=jax.ShapeDtypeStruct((shard_rows, width), F32),
        scratch_shapes=[pltpu.VMEM((items, width), BF16), pltpu.VMEM((items, width), BF16)],
        cost_estimate=cost(2 * items * shard_rows * width, 4 * shard_rows * width),
        compiler_params=pltpu.CompilerParams(vmem_limit_bytes=8 * MIB),
    )(block, out_grad, mine, twin)


def around(near, across, segment_count, dp_count):
    row = lax.ppermute(near, "segment", [(j, j ^ 2) for j in range(segment_count)])
    side = lax.ppermute(across, "dp", [(i, i ^ 1) for i in range(dp_count)])
    corners = [
        (j * dp_count + i, (j ^ 2) * dp_count + (i ^ 1)) for j in range(segment_count) for i in range(dp_count)
    ]
    corner = lax.ppermute(across, ("segment", "dp"), corners)
    return row, side, corner


def spread(rows, axis_name, count):
    return lax.all_to_all(
        jnp.broadcast_to(rows[None], (count,) + rows.shape), axis_name, 0, 0, tiled=True
    )


def per_device_parts(
    images, texts, section_weights, uniting_weights, codebooks, neg_bank, item_cats, cat_slot, neg_index
):
    segment_index = lax.axis_index("segment")
    segment_count = lax.axis_size("segment")
    dp_index = lax.axis_index("dp")
    dp_count = lax.axis_size("dp")
    item_count, _, image_width = images.shape
    text_width = texts.shape[2]
    first_rows = image_width + text_width
    shard_rows, width = uniting_weights.shape
    columns = width // (SIDES * segment_count)
    groups = unit_groups(dp_count, shard_rows, first_rows, SIDES * segment_count)
    message = weight_message(uniting_weights, groups, dp_count, columns)
    flag = (1 - segment_index % 2).astype(jnp.int32).reshape(1)
    flag, message = lax.optimization_barrier((flag, message))
    pieces = lax.all_to_all(message, "dp", 0, 0, tiled=True)
    pooled = pooled_features(images, texts, section_weights, segment_index, flag)
    pooled = pooled + lax.ppermute(pooled, "segment", [(i, i ^ 1) for i in range(segment_count)])
    mine = pooled.astype(BF16)
    other = lax.ppermute(mine, "segment", [(i, i ^ 2) for i in range(segment_count)])
    is_image = segment_index < 2
    embedded = jnp.concatenate(
        [jnp.where(is_image, mine, other)[:, :image_width], jnp.where(is_image, other, mine)], axis=1
    )
    embedded, pieces, books = lax.optimization_barrier((embedded, pieces, codebooks[0]))
    half = first_rows // 2
    embedded_half = jnp.where(segment_index % 2 == 0, embedded[:, :half], embedded[:, half:])
    mine_half = spread(embedded_half, "dp", dp_count)
    twin_half = lax.ppermute(mine_half, "segment", [(i, i ^ 1) for i in range(segment_count)])

    pair = item_cats.shape[1] // dp_count
    cats = item_cats.reshape(segment_count, dp_count, pair).transpose(1, 0, 2).reshape(-1)
    items = cats.shape[0]
    slots = jnp.sum(
        jnp.where(cats[:, None] == jnp.arange(cat_slot.shape[0])[None, :], cat_slot[None, :], 0), axis=1
    )
    ids = jnp.arange(items)
    rank = jnp.sum(jnp.where((slots[None, :] == slots[:, None]) & (ids[None, :] < ids[:, None]), 1, 0), axis=1)
    owned = segment_count * CAP
    order = (ids[:, None] == (slots * owned + rank)[None, :]).astype(BF16)
    own = lax.dynamic_slice_in_dim(order, dp_index * owned, owned, 0)
    across_own = lax.dynamic_slice_in_dim(order, (dp_index ^ 1) * owned, owned, 0)
    both_own = jnp.concatenate([own, across_own], axis=0)
    negatives = neg_index.reshape(segment_count, dp_count, pair, -1).transpose(1, 0, 2, 3).reshape(items, -1)
    own_negatives = jnp.dot(own.astype(F32), negatives.astype(F32), precision=highest)
    bank = neg_bank[0]
    ready = prepared(books, bank)
    bank_ids = jnp.arange(bank.shape[0]).astype(F32)
    counts = jnp.sum((own_negatives[:, :, None] == bank_ids[None, None, :]).astype(F32), axis=1)

    block, hidden, active, second, partial = merge_part(
        mine_half, twin_half, pieces, both_own, groups, shard_rows, first_rows, width
    )
    partial = partial + lax.ppermute(partial, "segment", [(i, i ^ 1) for i in range(segment_count)])
    row, side, corner = around(partial[:owned], partial[owned:], segment_count, dp_count)
    merged = (partial[:owned] + row) + (side + corner)
    merged_grad, loss, left, right = quantizer(merged, ready, bank, counts, 1.0 / math.sqrt(items))
    gathered = spread(merged_grad, "dp", dp_count)
    book_grad = codebook_grad(left, right, books)
    out_grad, sent = backward_part(gathered, order, hidden, active, second)
    mine = jnp.stack((sent,) + around(sent, sent, segment_count, dp_count))
    mine, book_grad = lax.optimization_barrier((mine, book_grad))
    twin = lax.ppermute(mine, "segment", [(i, i ^ 1) for i in range(segment_count)])
    uniting_grad = weight_grad(block, out_grad, mine, twin, groups)
    return (uniting_grad, book_grad[None], loss)


def pooled_features(images, texts, section_weights, segment_index, flag):
    image_width, text_width = images.shape[2], texts.shape[2]

    def image_branch(operands):
        pooled = image_pooled(operands[0], operands[2], flag)
        return jnp.pad(pooled, ((0, 0), (0, text_width - image_width)))

    def text_branch(operands):
        return text_pooled(operands[1], operands[2], flag)

    return lax.cond(segment_index < 2, image_branch, text_branch, (images, texts, section_weights))


def per_device_gathered(
    images,
    texts,
    section_weights,
    uniting_weights,
    codebooks,
    neg_bank,
    item_cats,
    cat_slot,
    neg_index,
):
    segment_index = lax.axis_index("segment")
    segment_count = lax.axis_size("segment")
    dp_index = lax.axis_index("dp")
    dp_count = lax.axis_size("dp")
    group_index = segment_index % 2
    item_count = images.shape[0]

    flag = (1 - group_index).astype(jnp.int32).reshape(1)
    pooled = pooled_features(images, texts, section_weights, segment_index, flag)
    image_width = images.shape[2]
    is_image = segment_index < 2
    packed = jnp.concatenate(
        [jnp.where(is_image, pooled[:, :image_width], 0.0), jnp.where(is_image, 0.0, pooled)], axis=1
    )
    embedded = lax.psum_scatter(packed, "segment", scatter_dimension=0, tiled=True).astype(
        jnp.bfloat16
    )
    stacked = lax.all_gather(uniting_weights, "dp", axis=0, tiled=True)
    first_rows = embedded.shape[1]
    cat_per_dev = codebooks.shape[0]
    slot_count = cat_per_dev * CAP
    row_total = item_cats.shape[1]
    cats_all = item_cats.reshape(-1)
    entry_count = cats_all.shape[0]
    entry_ids = jnp.arange(entry_count)
    category_match = cats_all[:, None] == jnp.arange(cat_slot.shape[0])[None, :]
    entry_slots = jnp.sum(jnp.where(category_match, cat_slot[None, :], 0), axis=1)
    entry_owner = entry_slots // cat_per_dev
    entry_local = entry_slots % cat_per_dev
    entry_row = entry_ids // row_total
    earlier = entry_ids[None, :] < entry_ids[:, None]
    same_cat = (cats_all[:, None] == cats_all[None, :]) & (entry_row[:, None] == entry_row[None, :])
    entry_rank = jnp.sum(jnp.where(earlier & same_cat, 1, 0), axis=1)
    entry_place = entry_local * CAP + entry_rank
    entry_position = entry_row * slot_count + entry_place
    owned = entry_owner == dp_index
    all_slots = segment_count * slot_count
    slot_match_all = owned[None, :] & (entry_position[None, :] == jnp.arange(all_slots)[:, None])
    view_match = lax.dynamic_slice(
        slot_match_all,
        (segment_index * slot_count, segment_index * row_total),
        (slot_count, row_total),
    )
    view_base = segment_index * row_total
    view_slots = view_match.shape[0]
    selection = view_match.astype(jnp.bfloat16)
    valid = jnp.sum(view_match.astype(jnp.float32), axis=1)
    slot_item = jnp.sum(
        jnp.where(view_match, jnp.arange(view_match.shape[1])[None, :] + view_base, 0), axis=1
    )
    slot_negs = jnp.take(neg_index.reshape(entry_count, -1), slot_item, axis=0)
    slot_local = jnp.arange(view_slots) % slot_count // CAP
    bank_rows = neg_bank.reshape(-1, neg_bank.shape[2])
    negatives = jnp.take(bank_rows, slot_local[:, None] * neg_bank.shape[1] + slot_negs, axis=0)
    loss_scale = 1.0 / math.sqrt(dp_count * item_count)

    def owner_objective(merged_float, books):
        per_row = jax.vmap(item_loss)(merged_float, books[slot_local], negatives)
        return jnp.sum(per_row * valid) * loss_scale

    gathered = jnp.dot(
        selection,
        lax.all_gather(embedded, "dp", axis=0, tiled=True),
        preferred_element_type=jnp.float32,
    )
    gathered = gathered.astype(jnp.bfloat16)
    normed_all, hidden_all, activated_all, merged_all = merge_forward(gathered, stacked)
    loss_local, pullback = jax.vjp(owner_objective, merged_all.astype(jnp.float32), codebooks)
    grad_all, book_grad = pullback(jnp.ones((), jnp.float32))
    out_grad = grad_all.astype(jnp.bfloat16)
    hidden_grad = merge_backward(hidden_all, stacked, out_grad, first_rows)
    joined = jnp.concatenate([normed_all, activated_all], axis=1)
    book_total, loss_owner = lax.psum((book_grad, loss_local), "segment")
    shard_rows = uniting_weights.shape[0]
    shard_start = dp_index * shard_rows
    shard_first = shard_start + jnp.arange(shard_rows) < first_rows
    joined_piece = lax.all_gather(joined, "dp", axis=0, tiled=True)
    first_piece = lax.all_gather(hidden_grad, "dp", axis=0, tiled=True)
    second_piece = lax.all_gather(out_grad, "dp", axis=0, tiled=True)
    columns = lax.dynamic_slice_in_dim(joined_piece, shard_start, shard_rows, 1)
    segment_grad = stacked_term(columns, first_piece, second_piece, shard_first)
    uniting_grad = lax.psum(segment_grad, "segment")
    return (uniting_grad, book_total, loss_owner.reshape(1))


def per_device(*operands):
    images, texts, _, uniting_weights = operands[:4]
    segment_count, dp_count = lax.axis_size("segment"), lax.axis_size("dp")
    shard_rows = uniting_weights.shape[0]
    first_rows = images.shape[2] + texts.shape[2]
    groups = unit_groups(dp_count, shard_rows, first_rows, SIDES * segment_count)
    if dp_count % SIDES == 0 and even_units(groups, shard_rows, SIDES * segment_count):
        return per_device_parts(*operands)
    return per_device_gathered(*operands)


def solution(mesh):
    placed = (
        P("dp", None, None),
        P("dp", None, None),
        P("segment", None, None),
        P("dp", None),
        P("dp", None, None, None),
        P("dp", None, None),
        P(),
        P(),
        P(),
    )
    return jax.shard_map(
        per_device,
        mesh=mesh,
        in_specs=placed,
        out_specs=(P("dp", None), P("dp", None, None, None), P("dp")),
        check_vma=False,
    )
```

```python
import functools
import math

import jax
import jax.numpy as jnp
import numpy as np
from jax import lax
from jax.experimental import pallas as pl
from jax.experimental.pallas import tpu as pltpu
from jax.sharding import PartitionSpec as P

F32 = jnp.float32
BF16 = jnp.bfloat16

HEAD_IMG = 64
HEAD_TXT = 128
CAP = 2
OWNED = 4 * CAP
MIB = 1024 * 1024
IMAGE_GROUP = 4
PROJECT_LANES = 512
LOG2_E = 1.4426950408889634
SIDES = 2
TILE = 8


norm_eps = 1e-06
rope_theta = 1000000.0
contrast_temp = 0.1
beta_weight = 1.0
highest = lax.Precision.HIGHEST


def gelu_value(inputs_f):
    return 0.5 * inputs_f * (1.0 + lax.erf(inputs_f / math.sqrt(2.0)))


def gelu_slope(inputs_f):
    return 0.5 * (1.0 + lax.erf(inputs_f / math.sqrt(2.0))) + inputs_f * jnp.exp(
        -0.5 * inputs_f * inputs_f
    ) / math.sqrt(2.0 * math.pi)


def dot_nt(a, b):
    return lax.dot_general(a, b, (((1,), (1,)), ((), ())), preferred_element_type=F32)

def dot_nn(a, b):
    return jnp.dot(a, b, preferred_element_type=F32)

def two_parts(value):
    high = value.astype(BF16)
    return jnp.concatenate([high, (value - high.astype(F32)).astype(BF16)], axis=0)

def dot_two(value, weights):
    rows = value.shape[0]
    both = dot_nn(two_parts(value), weights)
    return both[:rows] + both[rows:]

def unfold(slot_ref, first, out_ref, wide_ref, row_step):
    rows, columns = out_ref.shape
    blocks = columns // 128
    def body(step, carry):
        start = pl.multiple_of(step * row_step, row_step)
        source = pl.multiple_of(first + step * (row_step * blocks), 16)
        wide_ref[0 : row_step * blocks, :] = slot_ref[0, pl.ds(source, row_step * blocks), :].astype(F32)
        for block in range(blocks):
            piece = wide_ref[pl.ds(block, row_step, stride=blocks), :]
            out_ref[pl.ds(start, row_step), block * 128 : (block + 1) * 128] = piece.astype(BF16)
        return carry
    lax.fori_loop(0, rows // row_step, body, 0)

def image_kernel(
    flag_ref, image_hbm, slot_hbm, pooled_ref, image, rows_in, rows_out, w_in, w_out, wide, normed, joined, heads_mean, semaphores
):
    item_count, patch_count, model_width = image.shape
    half_width = model_width // 2
    head_count = half_width // HEAD_IMG
    groups = item_count // IMAGE_GROUP
    group_rows = IMAGE_GROUP * patch_count
    in_rows, out_rows = rows_in.shape[1], rows_out.shape[1]
    members = [pl.ds(index * IMAGE_GROUP, IMAGE_GROUP) for index in range(groups)]
    fetches = [pltpu.make_async_copy(image_hbm.at[span], image.at[span], semaphores.at[index]) for index, span in enumerate(members)]
    fetch_in = pltpu.make_async_copy(slot_hbm.at[:, pl.ds(0, in_rows)], rows_in, semaphores.at[groups])
    fetch_out = pltpu.make_async_copy(slot_hbm.at[:, pl.ds(in_rows, out_rows)], rows_out, semaphores.at[groups + 1])
    fetches[0].start()
    fetch_in.start()
    for fetch in fetches[1:]:
        fetch.start()
    fetch_out.start()
    flag = flag_ref[0].astype(F32)

    def normalize(index):
        fetches[index].wait()
        for member in range(index * IMAGE_GROUP, (index + 1) * IMAGE_GROUP):
            tokens = image[member].astype(F32)
            centred = tokens - jnp.mean(tokens, axis=1, keepdims=True)
            variance = jnp.mean(centred * centred, axis=1, keepdims=True)
            normed[member] = (centred * lax.rsqrt(variance + norm_eps)).astype(BF16)
            pooled_ref[member : member + 1, :] = jnp.mean(tokens, axis=0, keepdims=True) * flag

    def project(index, part):
        lanes = slice(part * PROJECT_LANES, (part + 1) * PROJECT_LANES)
        span = slice(index * IMAGE_GROUP, (index + 1) * IMAGE_GROUP)
        result = dot_nn(normed[span].reshape(group_rows, model_width), w_in[:, lanes])
        if (part + 1) * PROJECT_LANES <= half_width:
            result = result * (LOG2_E / math.sqrt(HEAD_IMG))
        joined[index, :, lanes] = result.astype(BF16)

    parts = 2 * half_width // PROJECT_LANES
    row_ids = lax.broadcasted_iota(jnp.int32, (head_count, patch_count), 0)
    normalize(0)
    fetch_in.wait()
    unfold(rows_in, 0, w_in, wide, 128)
    for part in range(parts):
        project(0, part)
    units = IMAGE_GROUP * head_count
    for index in range(groups):
        if index + 1 < groups:
            normalize(index + 1)
        for member in range(IMAGE_GROUP):
            rows = slice(member * patch_count, (member + 1) * patch_count)
            weights = jnp.zeros((head_count, patch_count), F32)
            for head in range(head_count):
                unit = member * head_count + head
                if index + 1 < groups and unit * parts % units < parts:
                    project(index + 1, unit * parts // units)
                span = slice(head * HEAD_IMG, (head + 1) * HEAD_IMG)
                key_span = slice(half_width + head * HEAD_IMG, half_width + (head + 1) * HEAD_IMG)
                scores = dot_nt(joined[index, rows, span], joined[index, rows, key_span])
                exps = jnp.exp2(scores - jnp.max(scores, axis=1, keepdims=True))
                share = (1.0 / patch_count) / jnp.sum(exps, axis=1, keepdims=True)
                mean_share = jnp.sum(exps * share, axis=0, keepdims=True)
                weights = weights + jnp.where(row_ids == head, mean_share, 0.0)
            item = index * IMAGE_GROUP + member
            heads_mean[item * head_count : (item + 1) * head_count, :] = dot_two(weights, normed[item])
    fetch_out.wait()
    unfold(rows_out, 0, w_out, wide, 128)
    values = dot_two(heads_mean[...], w_in[:, 2 * half_width :])
    rows = lax.broadcasted_iota(jnp.int32, values.shape, 0)
    columns = lax.broadcasted_iota(jnp.int32, values.shape, 1)
    values = jnp.where(rows % head_count == columns // HEAD_IMG, values, 0.0)
    attended = jnp.sum(values.reshape(item_count, head_count, half_width), axis=1)
    pooled_ref[...] += dot_two(attended, w_out[...])


def image_pooled(images, slot, flag):
    item_count, patch_count, model_width = images.shape
    half_width = model_width // 2
    head_count = half_width // HEAD_IMG
    groups = item_count // IMAGE_GROUP
    anywhere = pl.BlockSpec(memory_space=pl.ANY)
    return pl.pallas_call(
        image_kernel,
        in_specs=[pl.BlockSpec(memory_space=pltpu.SMEM), anywhere, anywhere],
        out_specs=pl.BlockSpec(memory_space=pltpu.VMEM),
        out_shape=jax.ShapeDtypeStruct((item_count, model_width), F32),
        scratch_shapes=[
            pltpu.VMEM(images.shape, BF16),
            pltpu.VMEM((1, 12 * model_width, 128), BF16),
            pltpu.VMEM((1, 4 * model_width, 128), BF16),
            pltpu.VMEM((model_width, 3 * half_width), BF16),
            pltpu.VMEM((half_width, model_width), BF16),
            pltpu.VMEM((128 * 12, 128), F32),
            pltpu.VMEM(images.shape, BF16),
            pltpu.VMEM((groups, IMAGE_GROUP * patch_count, 2 * half_width), BF16),
            pltpu.VMEM((item_count * head_count, model_width), F32),
            pltpu.SemaphoreType.DMA((groups + 2,)),
        ],
        compiler_params=pltpu.CompilerParams(vmem_limit_bytes=44 * 1024 * 1024),
    )(flag, images, slot)


def rope_tables(tokens, repeats):
    half = HEAD_TXT // 2
    exponents = np.arange(half).astype(np.float32) * np.float32(2.0 / HEAD_TXT)
    inverse = np.exp(np.float32(-math.log(rope_theta)) * exponents).astype(np.float32)
    angles = (np.arange(tokens).astype(np.float32)[:, None] * inverse[None, :]).astype(np.float32)
    cosine = np.concatenate([np.cos(angles), np.cos(angles)], axis=1)
    sine = np.concatenate([-np.sin(angles), np.sin(angles)], axis=1)
    return np.tile(cosine, (repeats, 1)).astype(np.float32), np.tile(sine, (repeats, 1)).astype(np.float32)

def text_kernel(flag_ref, text_ref, slot_ref, cos_ref, sin_ref, pooled_ref, w_in, w_out, wide, heads_mean):
    item_count, token_count, model_width = text_ref.shape
    half_width = model_width // 2
    head_count = half_width // HEAD_TXT
    unfold(slot_ref, 0, w_in, wide, 128)
    unfold(slot_ref, model_width * 8, w_out, wide, 128)
    tokens = text_ref[...].reshape(item_count * token_count, model_width).astype(F32)
    normed = (tokens * lax.rsqrt(jnp.mean(tokens * tokens, axis=1, keepdims=True) + norm_eps)).astype(BF16)
    residual = jnp.mean(tokens.reshape(item_count, token_count, model_width), axis=1)
    cosine, sine = cos_ref[...], sin_ref[...]

    def head_columns(head):
        return dot_nn(normed, w_in[:, head * HEAD_TXT : (head + 1) * HEAD_TXT])

    def turned(head, scale):
        part = head_columns(head)
        return ((part * cosine + pltpu.roll(part, HEAD_TXT // 2, 1) * sine).astype(BF16)).astype(F32) * scale

    queries = [(turned(head, 1.0)).astype(BF16) for head in range(head_count)]
    keys = turned(head_count, 1.0).astype(BF16)
    values = head_columns(head_count + 1).astype(BF16)
    wide_columns = head_count * token_count
    key_ids = lax.broadcasted_iota(jnp.int32, (token_count, wide_columns), 0)
    query_ids = lax.broadcasted_iota(jnp.int32, (token_count, wide_columns), 1) % token_count
    allowed = key_ids <= query_ids
    own_head = lax.broadcasted_iota(jnp.int32, (8, wide_columns), 0) == (
        lax.broadcasted_iota(jnp.int32, (8, wide_columns), 1) // token_count
    )
    for item in range(item_count):
        span = slice(item * token_count, (item + 1) * token_count)
        asked = jnp.concatenate([query[span] for query in queries], axis=0)
        scores = dot_nt(keys[span], asked) * (1.0 / math.sqrt(HEAD_TXT))
        scores = jnp.where(allowed, scores, -1e30)
        exps = jnp.exp(scores - jnp.max(scores, axis=0, keepdims=True))
        share = (1.0 / token_count) / jnp.sum(exps, axis=0, keepdims=True)
        share = jnp.where(own_head, share, 0.0).astype(BF16)
        weights = dot_nt(share, exps.astype(BF16))
        heads_mean[:, item, :] = dot_two(weights, values[span])
    pooled = residual * flag_ref[0].astype(F32)
    for head in range(head_count):
        pooled = pooled + dot_two(heads_mean[head], w_out[head * HEAD_TXT : (head + 1) * HEAD_TXT, :])
    pooled_ref[...] = pooled

def text_pooled(texts, slot, flag):
    item_count, token_count, model_width = texts.shape
    half_width = model_width // 2
    inner = half_width + 2 * HEAD_TXT
    cosine, sine = rope_tables(token_count, item_count)
    vm = pl.BlockSpec(memory_space=pltpu.VMEM)
    return pl.pallas_call(
        text_kernel,
        in_specs=[pl.BlockSpec(memory_space=pltpu.SMEM)] + [vm] * 4,
        out_specs=vm,
        out_shape=jax.ShapeDtypeStruct((item_count, model_width), F32),
        scratch_shapes=[
            pltpu.VMEM((model_width, inner), BF16),
            pltpu.VMEM((half_width, model_width), BF16),
            pltpu.VMEM((128 * 12, 128), F32),
            pltpu.VMEM((8, item_count, HEAD_TXT), F32),
        ],
        compiler_params=pltpu.CompilerParams(vmem_limit_bytes=40 * 1024 * 1024),
    )(flag, texts, slot, jnp.asarray(cosine), jnp.asarray(sine))

def merge_forward(embedded, stacked):
    first_rows = embedded.shape[1]
    float_embed = embedded.astype(jnp.float32)
    normed = (
        float_embed
        * lax.rsqrt(jnp.mean(float_embed * float_embed, axis=1, keepdims=True) + norm_eps)
    ).astype(jnp.bfloat16)
    hidden = jnp.dot(normed, stacked[:first_rows], preferred_element_type=jnp.float32)
    activated = gelu_value(hidden).astype(jnp.bfloat16)
    merged = jnp.dot(activated, stacked[first_rows:], preferred_element_type=jnp.float32).astype(
        jnp.bfloat16
    )
    return (normed, hidden, activated, merged)


def merge_backward(hidden, stacked, out_grad, first_rows):
    w_second = stacked[first_rows:]
    act_grad = lax.dot_general(
        out_grad, w_second, (((1,), (1,)), ((), ())), preferred_element_type=jnp.float32
    )
    return (act_grad * gelu_slope(hidden)).astype(jnp.bfloat16)


def item_loss(merged_row, book_rows, negatives):
    emb_width = merged_row.shape[0]
    quant_tau = math.sqrt(emb_width) / 2.0
    residual = merged_row * lax.rsqrt(jnp.mean(merged_row * merged_row) + norm_eps)
    quantized = jnp.zeros_like(merged_row)
    for level_index in range(book_rows.shape[0]):
        code_rows = book_rows[level_index]
        cross_terms = jnp.dot(code_rows, residual, precision=highest)
        logits = (2.0 * cross_terms - jnp.sum(code_rows * code_rows, axis=1)) / quant_tau
        logits = logits - lax.stop_gradient(jnp.max(logits))
        exp_logits = jnp.exp(logits)
        chosen = jnp.dot(exp_logits / jnp.sum(exp_logits), code_rows, precision=highest)
        residual = residual - chosen
        quantized = quantized + chosen
    recon_error = jnp.mean(residual * residual)
    anchor = quantized * lax.rsqrt(jnp.mean(quantized * quantized) + norm_eps)
    candidates = jnp.concatenate([merged_row[None, :], negatives.astype(jnp.float32)], axis=0)
    cand_unit = candidates * lax.rsqrt(
        jnp.mean(candidates * candidates, axis=1, keepdims=True) + norm_eps
    )
    similarity = jnp.dot(cand_unit, anchor, precision=highest) / (emb_width * contrast_temp)
    top_score = lax.stop_gradient(jnp.max(similarity))
    contrast = top_score + jnp.log(jnp.sum(jnp.exp(similarity - top_score))) - similarity[0]
    return contrast + beta_weight * recon_error


def stacked_term(columns, first_grad, second_grad, in_first):
    contract = (((0,), (0,)), ((), ()))
    first_term = lax.dot_general(columns, first_grad, contract, preferred_element_type=jnp.float32)
    second_term = lax.dot_general(
        columns, second_grad, contract, preferred_element_type=jnp.float32
    )
    return jnp.where(in_first[:, None], first_term, second_term)


def cost(flops, moved):
    return pl.CostEstimate(flops=flops, bytes_accessed=moved, transcendentals=0)


def first_rows_in(shard, shard_rows, first_rows):
    return min(max(first_rows - shard * shard_rows, 0), shard_rows)


def unit_groups(shard_count, shard_rows, first_rows, part_count):
    groups = []
    for shard in range(shard_count):
        inside = first_rows_in(shard, shard_rows, first_rows)
        if inside < shard_rows:
            groups.append((shard, inside, shard * shard_rows + inside - first_rows, (shard_rows - inside) // part_count))
    return groups


def even_units(groups, shard_rows, part_count):
    return all(
        inside % TILE == 0 and share % TILE == 0 and inside + share * part_count == shard_rows
        for _, inside, _, share in groups
    )


def message_kernel(groups, rows_ref, message_ref, built, semaphores):
    shard, segment = lax.axis_index("dp"), lax.axis_index("segment")
    copies, _, columns = message_ref.shape
    row_count, width = rows_ref.shape
    segment_count = width // (SIDES * columns)
    first_last = groups[0][0]

    for part in range(segment_count):
        here = segment == part

        @pl.when((shard <= first_last) & here)
        def _(part=part):
            for side in range(SIDES):
                picked = []
                for _, _, base, share in groups:
                    start = base + share * (side * segment_count + part)
                    picked.append(rows_ref[:, start : start + share])
                built[side] = jnp.concatenate(picked, axis=1)

        for group_shard, inside, _, share in groups:

            @pl.when((shard == group_shard) & here)
            def _(part=part, inside=inside, share=share):
                for side in range(SIDES):
                    start = inside + share * (side * segment_count + part)
                    low = start // 16 * 16
                    high = min(row_count, -(-(start + share) // 16) * 16)
                    taken = rows_ref[low:high, :].astype(F32)[start - low : start - low + share]
                    pieces = [taken[:, block * columns : (block + 1) * columns] for block in range(width // columns)]
                    built[side, inside:, :] = jnp.concatenate(pieces, axis=0).astype(BF16)

    sends = [
        pltpu.make_async_copy(built.at[copy % SIDES], message_ref.at[copy, :row_count], semaphores.at[copy]) for copy in range(copies)
    ]
    for send in sends:
        send.start()
    for send in sends:
        send.wait()


def weight_message(uniting_weights, groups, copies, columns):
    shard_rows = uniting_weights.shape[0]
    return pl.pallas_call(
        functools.partial(message_kernel, groups),
        in_specs=[pl.BlockSpec(memory_space=pltpu.VMEM)],
        out_specs=pl.BlockSpec(memory_space=pl.ANY),
        out_shape=jax.ShapeDtypeStruct((copies, shard_rows + 16, columns), BF16),
        scratch_shapes=[pltpu.VMEM((SIDES, shard_rows, columns), BF16), pltpu.SemaphoreType.DMA((copies,))],
        cost_estimate=cost(0, 4 * uniting_weights.size),
    )(uniting_weights)


def forward_kernel(
    groups,
    first_rows,
    mine_ref,
    twin_ref,
    own_ref,
    weights,
    block_ref,
    hidden_ref,
    active_ref,
    second_ref,
    partial_ref,
):
    shard_count, _, columns = weights.shape
    shard_rows = block_ref.shape[1]
    shard = lax.axis_index("dp")
    source_count, source_items, half = mine_ref.shape
    items, width = source_count * source_items, 2 * half
    mine = mine_ref[...].astype(F32).reshape(items, half)
    twin = twin_ref[...].astype(F32).reshape(items, half)
    first_core = lax.rem(lax.axis_index("segment"), 2) == 0
    embedded = jnp.concatenate([jnp.where(first_core, mine, twin), jnp.where(first_core, twin, mine)], axis=1)
    normed = embedded * lax.rsqrt(jnp.mean(embedded * embedded, axis=1, keepdims=True) + norm_eps)
    normed = normed.astype(BF16)
    hidden = jnp.zeros((items, columns), F32)
    own_block = jnp.zeros((items, shard_rows), BF16)
    for block in range(shard_count):
        inside = first_rows_in(block, shard_rows, first_rows)
        start = block * shard_rows
        if inside > 0:
            rows = normed[:, start : start + inside]
            hidden = hidden + dot_nn(rows, weights[block, :inside])
            if inside < shard_rows:
                rows = jnp.concatenate([rows, jnp.zeros((items, shard_rows - inside), BF16)], axis=1)
            own_block = jnp.where(shard == block, rows, own_block)
    block_ref[...] = own_block
    hidden_ref[...] = hidden
    active = gelu_value(hidden).astype(BF16)
    active_ref[...] = active
    lines = []
    for block, inside, _, share in groups:
        rows = weights[block, inside:shard_rows, :].astype(F32)
        pieces = [rows[part * share : (part + 1) * share] for part in range(partial_ref.shape[1] // columns)]
        lines.append(jnp.concatenate(pieces, axis=1))
    second_ref[...] = jnp.concatenate(lines, axis=0).astype(BF16)
    partial_ref[...] = dot_nn(dot_nn(own_ref[...], active).astype(BF16), second_ref[...])


def merge_part(mine_half, twin_half, pieces, own, groups, shard_rows, first_rows, width):
    shard_count, _, columns = pieces.shape
    items = mine_half.shape[0] * mine_half.shape[1]
    vm = pl.BlockSpec(memory_space=pltpu.VMEM)
    return pl.pallas_call(
        functools.partial(forward_kernel, groups, first_rows),
        in_specs=[vm] * 4,
        out_specs=[vm] * 5,
        out_shape=[
            jax.ShapeDtypeStruct((items, shard_rows), BF16),
            jax.ShapeDtypeStruct((items, columns), F32),
            jax.ShapeDtypeStruct((items, columns), BF16),
            jax.ShapeDtypeStruct((columns, width), BF16),
            jax.ShapeDtypeStruct((own.shape[0], width), F32),
        ],
        cost_estimate=cost(2 * items * first_rows * columns, 2 * pieces.size),
        compiler_params=pltpu.CompilerParams(vmem_limit_bytes=8 * MIB),
    )(mine_half, twin_half, own, pieces)


def split(value):
    high = value.astype(BF16)
    return high, (value - high.astype(F32)).astype(BF16)


def exact_nt(value, high, low):
    first, second = split(value)
    rows = value.shape[0]
    both = dot_nt(jnp.concatenate([first, second], axis=0), high)
    return both[:rows] + both[rows:] + dot_nt(first, low)


def exact_nn(value, high, low):
    first, second = split(value)
    rows = value.shape[0]
    both = dot_nn(jnp.concatenate([first, second], axis=0), high)
    return both[:rows] + both[rows:] + dot_nn(first, low)


def dot_tn(a, b):
    return lax.dot_general(a, b, (((0,), (0,)), ((), ())), preferred_element_type=F32)


def exact_tn(a, b):
    a_high, a_low = split(a)
    b_high, b_low = split(b)
    return dot_tn(
        jnp.concatenate([a_high, a_low, a_high], axis=0), jnp.concatenate([b_high, b_high, b_low], axis=0)
    )


def square_sums(value):
    high, low = split(value * value)
    ones = jnp.ones((8, value.shape[1]), BF16)
    return dot_nt(ones, high) + dot_nt(ones, low)


def prepare_kernel(book_ref, bank_ref, high_ref, low_ref, norm_ref, scale_ref):
    width = bank_ref.shape[1]
    for level in range(book_ref.shape[0]):
        codes = book_ref[level]
        high, low = split(codes)
        high_ref[level] = high
        low_ref[level] = low
        norm_ref[level] = square_sums(codes)
    scale_ref[...] = lax.rsqrt(square_sums(bank_ref[...].astype(F32)) * (1.0 / width) + norm_eps)


def prepared(books, bank):
    levels, codes, _ = books.shape
    vm = pl.BlockSpec(memory_space=pltpu.VMEM)
    return pl.pallas_call(
        prepare_kernel,
        in_specs=[vm] * 2,
        out_specs=[vm] * 4,
        out_shape=[
            jax.ShapeDtypeStruct(books.shape, BF16),
            jax.ShapeDtypeStruct(books.shape, BF16),
            jax.ShapeDtypeStruct((levels, 8, codes), F32),
            jax.ShapeDtypeStruct((8, bank.shape[0]), F32),
        ],
        cost_estimate=cost(0, 12 * books.size),
        compiler_params=pltpu.CompilerParams(vmem_limit_bytes=10 * MIB),
    )(books, bank)


def quantizer_kernel(
    loss_scale,
    merged_ref,
    highs,
    lows,
    norm_ref,
    bank_ref,
    bank_scale_ref,
    count_ref,
    merged_grad_ref,
    loss_ref,
    left_ref,
    right_ref,
):
    width = merged_ref.shape[1]
    levels = highs.shape[0]
    inverse_tau = 2.0 / math.sqrt(width)
    inverse_temp = 1.0 / (width * contrast_temp)
    merged = merged_ref[...].astype(BF16).astype(F32)
    merged_scale = lax.rsqrt(jnp.mean(merged * merged, axis=1, keepdims=True) + norm_eps)
    residuals = [merged * merged_scale]
    shares, chosen_rows = [], []
    for level in range(levels):
        high, low = highs[level], lows[level]
        logits = (2.0 * exact_nt(residuals[level], high, low) - norm_ref[level]) * inverse_tau
        exps = jnp.exp(logits - jnp.max(logits, axis=1, keepdims=True))
        share = exps / jnp.sum(exps, axis=1, keepdims=True)
        chosen = exact_nn(share, high, low)
        shares.append(share)
        chosen_rows.append(chosen)
        residuals.append(residuals[level] - chosen)
    last = residuals[levels]
    quantized = chosen_rows[0]
    for chosen in chosen_rows[1:]:
        quantized = quantized + chosen
    anchor_scale = lax.rsqrt(jnp.mean(quantized * quantized, axis=1, keepdims=True) + norm_eps)
    anchor = quantized * anchor_scale
    own = jnp.sum(anchor * residuals[0], axis=1, keepdims=True) * inverse_temp
    bank = bank_ref[...]
    bank_scale = bank_scale_ref[...]
    anchor_parts = jnp.concatenate(split(anchor), axis=0)
    rows = anchor.shape[0]
    both = dot_nt(anchor_parts, bank)
    similar = (both[:rows] + both[rows:]) * bank_scale * inverse_temp
    counts = count_ref[...]
    named = counts > 0.0
    top = jnp.maximum(jnp.max(jnp.where(named, similar, own), axis=1, keepdims=True), own)
    bank_exps = jnp.where(named, jnp.exp(jnp.where(named, similar, top) - top), 0.0) * counts
    own_exp = jnp.exp(own - top)
    total = jnp.sum(bank_exps, axis=1, keepdims=True) + own_exp
    item_losses = top + jnp.log(total) - own + jnp.mean(last * last, axis=1, keepdims=True)
    loss_ref[0] = jnp.sum(item_losses) * loss_scale

    bank_weight = bank_exps / total * (loss_scale * inverse_temp)
    own_weight = (own_exp / total - 1.0) * (loss_scale * inverse_temp)
    weight_parts = jnp.concatenate(split(bank_weight * bank_scale), axis=0)
    both = dot_nn(weight_parts, bank)
    anchor_grad = both[:rows] + both[rows:] + own_weight * residuals[0]
    unit_grad = own_weight * anchor
    quantized_grad = anchor_scale * (anchor_grad - anchor * jnp.mean(anchor * anchor_grad, axis=1, keepdims=True))
    residual_grad = last * (2.0 * loss_scale / width)
    for level in reversed(range(levels)):
        high, low = highs[level], lows[level]
        chosen_grad = quantized_grad - residual_grad
        share_grad = exact_nt(chosen_grad, high, low)
        share = shares[level]
        logit_grad = share * (share_grad - jnp.sum(share * share_grad, axis=1, keepdims=True)) * (2.0 * inverse_tau)
        left_ref[level] = jnp.concatenate([share, logit_grad], axis=0)
        right_ref[level] = jnp.concatenate([chosen_grad, residuals[level]], axis=0)
        residual_grad = residual_grad + exact_nn(logit_grad, high, low)
    unit_grad = unit_grad + residual_grad
    unit = residuals[0]
    merged_grad = merged_scale * (unit_grad - unit * jnp.mean(unit * unit_grad, axis=1, keepdims=True))
    merged_grad_ref[...] = merged_grad.astype(BF16)


def quantizer(merged, ready, bank, counts, loss_scale):
    highs, lows, norms, bank_scale = ready
    levels, codes, width = highs.shape
    rows = merged.shape[0]
    vm = pl.BlockSpec(memory_space=pltpu.VMEM)
    return pl.pallas_call(
        functools.partial(quantizer_kernel, loss_scale),
        in_specs=[vm] * 7,
        out_specs=[vm, pl.BlockSpec(memory_space=pltpu.SMEM), vm, vm],
        out_shape=[
            jax.ShapeDtypeStruct(merged.shape, BF16),
            jax.ShapeDtypeStruct((1,), F32),
            jax.ShapeDtypeStruct((levels, 2 * rows, codes), F32),
            jax.ShapeDtypeStruct((levels, 2 * rows, width), F32),
        ],
        cost_estimate=cost(64 * highs.size, 4 * highs.size),
        compiler_params=pltpu.CompilerParams(vmem_limit_bytes=12 * MIB),
    )(merged, highs, lows, norms, bank, bank_scale, counts)


def codebook_kernel(left_ref, right_ref, book_ref, grad_ref):
    levels, doubled, _ = left_ref.shape
    width = right_ref.shape[2]
    rows = doubled // 2
    ones = jnp.ones((rows, 128), F32)
    for level in range(levels):
        outer = exact_tn(left_ref[level], right_ref[level])
        totals = exact_tn(left_ref[level, rows:], ones)
        for block in range(width // 128):
            span = slice(block * 128, (block + 1) * 128)
            grad_ref[level, :, span] = outer[:, span] - totals * book_ref[level, :, span]


def codebook_grad(left, right, books):
    vm = pl.BlockSpec(memory_space=pltpu.VMEM)
    return pl.pallas_call(
        codebook_kernel,
        in_specs=[vm] * 3,
        out_specs=vm,
        out_shape=jax.ShapeDtypeStruct(books.shape, F32),
        cost_estimate=cost(96 * books.size, 8 * books.size),
        compiler_params=pltpu.CompilerParams(vmem_limit_bytes=10 * MIB),
    )(left, right, books)


def backward_kernel(gathered_ref, order_ref, hidden_ref, active_ref, second_ref, out_grad_ref, sent_ref):
    owners, places, width = gathered_ref.shape
    columns = hidden_ref.shape[1]
    gathered = gathered_ref[...].astype(F32).reshape(owners * places, width).astype(BF16)
    out_grad = dot_tn(order_ref[...], gathered).astype(BF16)
    out_grad_ref[...] = out_grad
    hidden_grad = dot_nt(out_grad, second_ref[...]) * gelu_slope(hidden_ref[...])
    sent_ref[:, :columns] = hidden_grad.astype(BF16)
    sent_ref[:, columns:] = active_ref[...]


def backward_part(gathered, order, hidden, active, second):
    items, columns = hidden.shape
    vm = pl.BlockSpec(memory_space=pltpu.VMEM)
    return pl.pallas_call(
        backward_kernel,
        in_specs=[vm] * 5,
        out_specs=[vm] * 2,
        out_shape=[
            jax.ShapeDtypeStruct((items, gathered.shape[2]), BF16),
            jax.ShapeDtypeStruct((items, 2 * columns), BF16),
        ],
        cost_estimate=cost(2 * items * second.size, 2 * second.size),
        compiler_params=pltpu.CompilerParams(vmem_limit_bytes=8 * MIB),
    )(gathered, order, hidden, active, second)


def weight_grad_kernel(
    groups, block_ref, out_grad_ref, mine_ref, twin_ref, grad_ref, hidden_grad, active
):
    shard, segment = lax.axis_index("dp"), lax.axis_index("segment")
    _, items, doubled = mine_ref.shape
    cores = 2
    own_core = lax.rem(segment, cores)
    columns = doubled // 2
    shard_rows = block_ref.shape[1]
    own_side, own_row = lax.rem(shard, SIDES), segment // cores
    segment_count = hidden_grad.shape[1] // (SIDES * columns)

    def place_units(target, first):
        for side in range(SIDES):
            for other in range(segment_count):
                parts = [
                    jnp.where(
                        own_core == other % cores,
                        mine_ref[index, :, first : first + columns],
                        twin_ref[index, :, first : first + columns],
                    )
                    for index in range(4)
                ]
                same_row = own_row == other // cores
                near = jnp.where(same_row, parts[0], parts[1])
                across = jnp.where(same_row, parts[2], parts[3])
                part = jnp.where(own_side == side, near, across)
                offset = 0
                for _, _, base, share in groups:
                    spot = base + share * (side * segment_count + other)
                    target[:, spot : spot + share] = part[:, offset : offset + share]
                    offset += share

    place_units(hidden_grad, 0)
    grad_ref[...] = dot_tn(block_ref[...], hidden_grad[...])
    for group_shard, inside, base, _ in groups:

        @pl.when(shard == group_shard)
        def _(inside=inside, base=base):
            place_units(active, columns)
            wanted = active[:, base : base + shard_rows - inside]
            grad_ref[inside:, :] = dot_tn(wanted, out_grad_ref[...])


def weight_grad(block, out_grad, mine, twin, groups):
    items, shard_rows = block.shape
    width = out_grad.shape[1]
    vm = pl.BlockSpec(memory_space=pltpu.VMEM)
    return pl.pallas_call(
        functools.partial(weight_grad_kernel, groups),
        in_specs=[vm] * 4,
        out_specs=vm,
        out_shape=jax.ShapeDtypeStruct((shard_rows, width), F32),
        scratch_shapes=[pltpu.VMEM((items, width), BF16), pltpu.VMEM((items, width), BF16)],
        cost_estimate=cost(2 * items * shard_rows * width, 4 * shard_rows * width),
        compiler_params=pltpu.CompilerParams(vmem_limit_bytes=8 * MIB),
    )(block, out_grad, mine, twin)


def around(near, across, segment_count, dp_count):
    row = lax.ppermute(near, "segment", [(j, j ^ 2) for j in range(segment_count)])
    side = lax.ppermute(across, "dp", [(i, i ^ 1) for i in range(dp_count)])
    corners = [
        (j * dp_count + i, (j ^ 2) * dp_count + (i ^ 1)) for j in range(segment_count) for i in range(dp_count)
    ]
    corner = lax.ppermute(across, ("segment", "dp"), corners)
    return row, side, corner


def spread(rows, axis_name, count):
    return lax.all_to_all(
        jnp.broadcast_to(rows[None], (count,) + rows.shape), axis_name, 0, 0, tiled=True
    )


def per_device_parts(
    images, texts, section_weights, uniting_weights, codebooks, neg_bank, item_cats, cat_slot, neg_index
):
    segment_index = lax.axis_index("segment")
    segment_count = lax.axis_size("segment")
    dp_index = lax.axis_index("dp")
    dp_count = lax.axis_size("dp")
    item_count, _, image_width = images.shape
    text_width = texts.shape[2]
    first_rows = image_width + text_width
    shard_rows, width = uniting_weights.shape
    columns = width // (SIDES * segment_count)
    groups = unit_groups(dp_count, shard_rows, first_rows, SIDES * segment_count)
    message = weight_message(uniting_weights, groups, dp_count, columns)
    flag = (1 - segment_index % 2).astype(jnp.int32).reshape(1)
    flag, message = lax.optimization_barrier((flag, message))
    pieces = lax.all_to_all(message, "dp", 0, 0, tiled=True)
    pooled = pooled_features(images, texts, section_weights, segment_index, flag)
    pooled = pooled + lax.ppermute(pooled, "segment", [(i, i ^ 1) for i in range(segment_count)])
    mine = pooled.astype(BF16)
    other = lax.ppermute(mine, "segment", [(i, i ^ 2) for i in range(segment_count)])
    is_image = segment_index < 2
    embedded = jnp.concatenate(
        [jnp.where(is_image, mine, other)[:, :image_width], jnp.where(is_image, other, mine)], axis=1
    )
    embedded, pieces, books = lax.optimization_barrier((embedded, pieces, codebooks[0]))
    half = first_rows // 2
    embedded_half = jnp.where(segment_index % 2 == 0, embedded[:, :half], embedded[:, half:])
    mine_half = spread(embedded_half, "dp", dp_count)
    twin_half = lax.ppermute(mine_half, "segment", [(i, i ^ 1) for i in range(segment_count)])

    pair = item_cats.shape[1] // dp_count
    cats = item_cats.reshape(segment_count, dp_count, pair).transpose(1, 0, 2).reshape(-1)
    items = cats.shape[0]
    slots = jnp.sum(
        jnp.where(cats[:, None] == jnp.arange(cat_slot.shape[0])[None, :], cat_slot[None, :], 0), axis=1
    )
    ids = jnp.arange(items)
    rank = jnp.sum(jnp.where((slots[None, :] == slots[:, None]) & (ids[None, :] < ids[:, None]), 1, 0), axis=1)
    owned = segment_count * CAP
    order = (ids[:, None] == (slots * owned + rank)[None, :]).astype(BF16)
    own = lax.dynamic_slice_in_dim(order, dp_index * owned, owned, 0)
    across_own = lax.dynamic_slice_in_dim(order, (dp_index ^ 1) * owned, owned, 0)
    both_own = jnp.concatenate([own, across_own], axis=0)
    negatives = neg_index.reshape(segment_count, dp_count, pair, -1).transpose(1, 0, 2, 3).reshape(items, -1)
    own_negatives = jnp.dot(own.astype(F32), negatives.astype(F32), precision=highest)
    bank = neg_bank[0]
    ready = prepared(books, bank)
    bank_ids = jnp.arange(bank.shape[0]).astype(F32)
    counts = jnp.sum((own_negatives[:, :, None] == bank_ids[None, None, :]).astype(F32), axis=1)

    block, hidden, active, second, partial = merge_part(
        mine_half, twin_half, pieces, both_own, groups, shard_rows, first_rows, width
    )
    partial = partial + lax.ppermute(partial, "segment", [(i, i ^ 1) for i in range(segment_count)])
    row, side, corner = around(partial[:owned], partial[owned:], segment_count, dp_count)
    merged = (partial[:owned] + row) + (side + corner)
    merged_grad, loss, left, right = quantizer(merged, ready, bank, counts, 1.0 / math.sqrt(items))
    gathered = spread(merged_grad, "dp", dp_count)
    book_grad = codebook_grad(left, right, books)
    out_grad, sent = backward_part(gathered, order, hidden, active, second)
    mine = jnp.stack((sent,) + around(sent, sent, segment_count, dp_count))
    mine, book_grad = lax.optimization_barrier((mine, book_grad))
    twin = lax.ppermute(mine, "segment", [(i, i ^ 1) for i in range(segment_count)])
    uniting_grad = weight_grad(block, out_grad, mine, twin, groups)
    return (uniting_grad, book_grad[None], loss)


def pooled_features(images, texts, section_weights, segment_index, flag):
    image_width, text_width = images.shape[2], texts.shape[2]

    def image_branch(operands):
        pooled = image_pooled(operands[0], operands[2], flag)
        return jnp.pad(pooled, ((0, 0), (0, text_width - image_width)))

    def text_branch(operands):
        return text_pooled(operands[1], operands[2], flag)

    return lax.cond(segment_index < 2, image_branch, text_branch, (images, texts, section_weights))


def per_device_gathered(
    images,
    texts,
    section_weights,
    uniting_weights,
    codebooks,
    neg_bank,
    item_cats,
    cat_slot,
    neg_index,
):
    segment_index = lax.axis_index("segment")
    segment_count = lax.axis_size("segment")
    dp_index = lax.axis_index("dp")
    dp_count = lax.axis_size("dp")
    group_index = segment_index % 2
    item_count = images.shape[0]

    flag = (1 - group_index).astype(jnp.int32).reshape(1)
    pooled = pooled_features(images, texts, section_weights, segment_index, flag)
    image_width = images.shape[2]
    is_image = segment_index < 2
    packed = jnp.concatenate(
        [jnp.where(is_image, pooled[:, :image_width], 0.0), jnp.where(is_image, 0.0, pooled)], axis=1
    )
    embedded = lax.psum_scatter(packed, "segment", scatter_dimension=0, tiled=True).astype(
        jnp.bfloat16
    )
    stacked = lax.all_gather(uniting_weights, "dp", axis=0, tiled=True)
    first_rows = embedded.shape[1]
    cat_per_dev = codebooks.shape[0]
    slot_count = cat_per_dev * CAP
    row_total = item_cats.shape[1]
    cats_all = item_cats.reshape(-1)
    entry_count = cats_all.shape[0]
    entry_ids = jnp.arange(entry_count)
    category_match = cats_all[:, None] == jnp.arange(cat_slot.shape[0])[None, :]
    entry_slots = jnp.sum(jnp.where(category_match, cat_slot[None, :], 0), axis=1)
    entry_owner = entry_slots // cat_per_dev
    entry_local = entry_slots % cat_per_dev
    entry_row = entry_ids // row_total
    earlier = entry_ids[None, :] < entry_ids[:, None]
    same_cat = (cats_all[:, None] == cats_all[None, :]) & (entry_row[:, None] == entry_row[None, :])
    entry_rank = jnp.sum(jnp.where(earlier & same_cat, 1, 0), axis=1)
    entry_place = entry_local * CAP + entry_rank
    entry_position = entry_row * slot_count + entry_place
    owned = entry_owner == dp_index
    all_slots = segment_count * slot_count
    slot_match_all = owned[None, :] & (entry_position[None, :] == jnp.arange(all_slots)[:, None])
    view_match = lax.dynamic_slice(
        slot_match_all,
        (segment_index * slot_count, segment_index * row_total),
        (slot_count, row_total),
    )
    view_base = segment_index * row_total
    view_slots = view_match.shape[0]
    selection = view_match.astype(jnp.bfloat16)
    valid = jnp.sum(view_match.astype(jnp.float32), axis=1)
    slot_item = jnp.sum(
        jnp.where(view_match, jnp.arange(view_match.shape[1])[None, :] + view_base, 0), axis=1
    )
    slot_negs = jnp.take(neg_index.reshape(entry_count, -1), slot_item, axis=0)
    slot_local = jnp.arange(view_slots) % slot_count // CAP
    bank_rows = neg_bank.reshape(-1, neg_bank.shape[2])
    negatives = jnp.take(bank_rows, slot_local[:, None] * neg_bank.shape[1] + slot_negs, axis=0)
    loss_scale = 1.0 / math.sqrt(dp_count * item_count)

    def owner_objective(merged_float, books):
        per_row = jax.vmap(item_loss)(merged_float, books[slot_local], negatives)
        return jnp.sum(per_row * valid) * loss_scale

    gathered = jnp.dot(
        selection,
        lax.all_gather(embedded, "dp", axis=0, tiled=True),
        preferred_element_type=jnp.float32,
    )
    gathered = gathered.astype(jnp.bfloat16)
    normed_all, hidden_all, activated_all, merged_all = merge_forward(gathered, stacked)
    loss_local, pullback = jax.vjp(owner_objective, merged_all.astype(jnp.float32), codebooks)
    grad_all, book_grad = pullback(jnp.ones((), jnp.float32))
    out_grad = grad_all.astype(jnp.bfloat16)
    hidden_grad = merge_backward(hidden_all, stacked, out_grad, first_rows)
    joined = jnp.concatenate([normed_all, activated_all], axis=1)
    book_total, loss_owner = lax.psum((book_grad, loss_local), "segment")
    shard_rows = uniting_weights.shape[0]
    shard_start = dp_index * shard_rows
    shard_first = shard_start + jnp.arange(shard_rows) < first_rows
    joined_piece = lax.all_gather(joined, "dp", axis=0, tiled=True)
    first_piece = lax.all_gather(hidden_grad, "dp", axis=0, tiled=True)
    second_piece = lax.all_gather(out_grad, "dp", axis=0, tiled=True)
    columns = lax.dynamic_slice_in_dim(joined_piece, shard_start, shard_rows, 1)
    segment_grad = stacked_term(columns, first_piece, second_piece, shard_first)
    uniting_grad = lax.psum(segment_grad, "segment")
    return (uniting_grad, book_total, loss_owner.reshape(1))


def per_device(*operands):
    images, texts, _, uniting_weights = operands[:4]
    segment_count, dp_count = lax.axis_size("segment"), lax.axis_size("dp")
    shard_rows = uniting_weights.shape[0]
    first_rows = images.shape[2] + texts.shape[2]
    groups = unit_groups(dp_count, shard_rows, first_rows, SIDES * segment_count)
    if dp_count % SIDES == 0 and even_units(groups, shard_rows, SIDES * segment_count):
        return per_device_parts(*operands)
    return per_device_gathered(*operands)


def solution(mesh):
    placed = (
        P("dp", None, None),
        P("dp", None, None),
        P("segment", None, None),
        P("dp", None),
        P("dp", None, None, None),
        P("dp", None, None),
        P(),
        P(),
        P(),
    )
    return jax.shard_map(
        per_device,
        mesh=mesh,
        in_specs=placed,
        out_specs=(P("dp", None), P("dp", None, None, None), P("dp")),
        check_vma=False,
    )
```

```python
import functools
import math

import jax
import jax.numpy as jnp
import numpy as np
from jax import lax
from jax.experimental import pallas as pl
from jax.experimental.pallas import tpu as pltpu
from jax.sharding import PartitionSpec as P

F32 = jnp.float32
BF16 = jnp.bfloat16

HEAD_IMG = 64
HEAD_TXT = 128
CAP = 2
OWNED = 4 * CAP
MIB = 1024 * 1024
IMAGE_GROUP = 4
PROJECT_LANES = 256
OUT_STEP = 128
LOG2_E = 1.4426950408889634
SIDES = 2
TILE = 8


norm_eps = 1e-06
rope_theta = 1000000.0
contrast_temp = 0.1
beta_weight = 1.0
highest = lax.Precision.HIGHEST


def gelu_value(inputs_f):
    return 0.5 * inputs_f * (1.0 + lax.erf(inputs_f / math.sqrt(2.0)))


def gelu_slope(inputs_f):
    return 0.5 * (1.0 + lax.erf(inputs_f / math.sqrt(2.0))) + inputs_f * jnp.exp(
        -0.5 * inputs_f * inputs_f
    ) / math.sqrt(2.0 * math.pi)


def dot_nt(a, b):
    return lax.dot_general(a, b, (((1,), (1,)), ((), ())), preferred_element_type=F32)

def dot_nn(a, b):
    return jnp.dot(a, b, preferred_element_type=F32)

def two_parts(value):
    high = value.astype(BF16)
    return jnp.concatenate([high, (value - high.astype(F32)).astype(BF16)], axis=0)

def dot_two(value, weights):
    rows = value.shape[0]
    both = dot_nn(two_parts(value), weights)
    return both[:rows] + both[rows:]

def unfold_step(slot_ref, first, out_ref, wide_ref, row_step, step):
    blocks = out_ref.shape[1] // 128
    start = step * row_step
    source = first + step * (row_step * blocks)
    if not isinstance(step, int):
        start, source = pl.multiple_of(start, row_step), pl.multiple_of(source, 16)
    wide_ref[0 : row_step * blocks, :] = slot_ref[0, pl.ds(source, row_step * blocks), :].astype(F32)
    for block in range(blocks):
        piece = wide_ref[pl.ds(block, row_step, stride=blocks), :]
        out_ref[pl.ds(start, row_step), block * 128 : (block + 1) * 128] = piece.astype(BF16)


def unfold(slot_ref, first, out_ref, wide_ref, row_step):
    def body(step, carry):
        unfold_step(slot_ref, first, out_ref, wide_ref, row_step, step)
        return carry

    lax.fori_loop(0, out_ref.shape[0] // row_step, body, 0)


def image_kernel(
    flag_ref, image_hbm, slot_hbm, pooled_ref, image, rows_in, rows_out, w_in, w_out, wide, normed, joined, heads_mean, semaphores
):
    item_count, patch_count, model_width = image.shape
    half_width = model_width // 2
    head_count = half_width // HEAD_IMG
    groups = item_count // IMAGE_GROUP
    group_rows = IMAGE_GROUP * patch_count
    in_rows, out_rows = rows_in.shape[1], rows_out.shape[1]
    members = [pl.ds(index * IMAGE_GROUP, IMAGE_GROUP) for index in range(groups)]
    fetches = [pltpu.make_async_copy(image_hbm.at[span], image.at[span], semaphores.at[index]) for index, span in enumerate(members)]
    fetch_in = pltpu.make_async_copy(slot_hbm.at[:, pl.ds(0, in_rows)], rows_in, semaphores.at[groups])
    fetch_out = pltpu.make_async_copy(slot_hbm.at[:, pl.ds(in_rows, out_rows)], rows_out, semaphores.at[groups + 1])
    fetches[0].start()
    fetch_in.start()
    for fetch in fetches[1:]:
        fetch.start()
    fetch_out.start()
    flag = flag_ref[0].astype(F32)

    def normalize(first, last):
        for member in range(first, last):
            tokens = image[member].astype(F32)
            centred = tokens - jnp.mean(tokens, axis=1, keepdims=True)
            variance = jnp.mean(centred * centred, axis=1, keepdims=True)
            normed[member] = (centred * lax.rsqrt(variance + norm_eps)).astype(BF16)
            pooled_ref[member : member + 1, :] = jnp.mean(tokens, axis=0, keepdims=True) * flag

    def project(index, part):
        lanes = slice(part * PROJECT_LANES, (part + 1) * PROJECT_LANES)
        span = slice(index * IMAGE_GROUP, (index + 1) * IMAGE_GROUP)
        result = dot_nn(normed[span].reshape(group_rows, model_width), w_in[:, lanes])
        if (part + 1) * PROJECT_LANES <= half_width:
            result = result * (LOG2_E / math.sqrt(HEAD_IMG))
        joined[index, :, lanes] = result.astype(BF16)

    parts = 2 * half_width // PROJECT_LANES
    row_ids = lax.broadcasted_iota(jnp.int32, (head_count, patch_count), 0)
    fetches[0].wait()
    normalize(0, IMAGE_GROUP)
    fetch_in.wait()
    unfold(rows_in, 0, w_in, wide, 128)
    for fetch in fetches[1:]:
        fetch.wait()
    fetch_out.wait()
    half = IMAGE_GROUP + IMAGE_GROUP // 2
    for part in range(parts):
        project(0, part)
        if part == 0:
            normalize(IMAGE_GROUP, half)
    normalize(half, item_count)
    out_steps = half_width // OUT_STEP
    units = IMAGE_GROUP * head_count
    for index in range(groups):
        for member in range(IMAGE_GROUP):
            rows = slice(member * patch_count, (member + 1) * patch_count)
            weights = jnp.zeros((head_count, patch_count), F32)
            for head in range(head_count):
                unit = member * head_count + head
                if index + 1 < groups and unit * parts % units < parts:
                    project(index + 1, unit * parts // units)
                if index + 1 == groups and unit * out_steps % units < out_steps:
                    unfold_step(rows_out, 0, w_out, wide, OUT_STEP, unit * out_steps // units)
                span = slice(head * HEAD_IMG, (head + 1) * HEAD_IMG)
                key_span = slice(half_width + head * HEAD_IMG, half_width + (head + 1) * HEAD_IMG)
                scores = dot_nt(joined[index, rows, span], joined[index, rows, key_span])
                exps = jnp.exp2(scores - jnp.max(scores, axis=1, keepdims=True))
                share = (1.0 / patch_count) / jnp.sum(exps, axis=1, keepdims=True)
                mean_share = jnp.sum(exps * share, axis=0, keepdims=True)
                weights = weights + jnp.where(row_ids == head, mean_share, 0.0)
            item = index * IMAGE_GROUP + member
            heads_mean[item * head_count : (item + 1) * head_count, :] = dot_two(weights, normed[item])
    values = dot_two(heads_mean[...], w_in[:, 2 * half_width :])
    rows = lax.broadcasted_iota(jnp.int32, values.shape, 0)
    columns = lax.broadcasted_iota(jnp.int32, values.shape, 1)
    values = jnp.where(rows % head_count == columns // HEAD_IMG, values, 0.0)
    attended = jnp.sum(values.reshape(item_count, head_count, half_width), axis=1)
    pooled_ref[...] += dot_two(attended, w_out[...])


def image_pooled(images, slot, flag):
    item_count, patch_count, model_width = images.shape
    half_width = model_width // 2
    head_count = half_width // HEAD_IMG
    groups = item_count // IMAGE_GROUP
    anywhere = pl.BlockSpec(memory_space=pl.ANY)
    return pl.pallas_call(
        image_kernel,
        in_specs=[pl.BlockSpec(memory_space=pltpu.SMEM), anywhere, anywhere],
        out_specs=pl.BlockSpec(memory_space=pltpu.VMEM),
        out_shape=jax.ShapeDtypeStruct((item_count, model_width), F32),
        scratch_shapes=[
            pltpu.VMEM(images.shape, BF16),
            pltpu.VMEM((1, 12 * model_width, 128), BF16),
            pltpu.VMEM((1, 4 * model_width, 128), BF16),
            pltpu.VMEM((model_width, 3 * half_width), BF16),
            pltpu.VMEM((half_width, model_width), BF16),
            pltpu.VMEM((128 * 12, 128), F32),
            pltpu.VMEM(images.shape, BF16),
            pltpu.VMEM((groups, IMAGE_GROUP * patch_count, 2 * half_width), BF16),
            pltpu.VMEM((item_count * head_count, model_width), F32),
            pltpu.SemaphoreType.DMA((groups + 2,)),
        ],
        compiler_params=pltpu.CompilerParams(vmem_limit_bytes=44 * 1024 * 1024),
    )(flag, images, slot)


def rope_tables(tokens, repeats):
    half = HEAD_TXT // 2
    exponents = np.arange(half).astype(np.float32) * np.float32(2.0 / HEAD_TXT)
    inverse = np.exp(np.float32(-math.log(rope_theta)) * exponents).astype(np.float32)
    angles = (np.arange(tokens).astype(np.float32)[:, None] * inverse[None, :]).astype(np.float32)
    cosine = np.concatenate([np.cos(angles), np.cos(angles)], axis=1)
    sine = np.concatenate([-np.sin(angles), np.sin(angles)], axis=1)
    return np.tile(cosine, (repeats, 1)).astype(np.float32), np.tile(sine, (repeats, 1)).astype(np.float32)

def text_kernel(flag_ref, text_ref, slot_ref, cos_ref, sin_ref, pooled_ref, w_in, w_out, wide, heads_mean):
    item_count, token_count, model_width = text_ref.shape
    half_width = model_width // 2
    head_count = half_width // HEAD_TXT
    unfold(slot_ref, 0, w_in, wide, 128)
    unfold(slot_ref, model_width * 8, w_out, wide, 128)
    tokens = text_ref[...].reshape(item_count * token_count, model_width).astype(F32)
    normed = (tokens * lax.rsqrt(jnp.mean(tokens * tokens, axis=1, keepdims=True) + norm_eps)).astype(BF16)
    residual = jnp.mean(tokens.reshape(item_count, token_count, model_width), axis=1)
    cosine, sine = cos_ref[...], sin_ref[...]

    def head_columns(head):
        return dot_nn(normed, w_in[:, head * HEAD_TXT : (head + 1) * HEAD_TXT])

    def turned(head, scale):
        part = head_columns(head)
        return ((part * cosine + pltpu.roll(part, HEAD_TXT // 2, 1) * sine).astype(BF16)).astype(F32) * scale

    queries = [(turned(head, 1.0)).astype(BF16) for head in range(head_count)]
    keys = turned(head_count, 1.0).astype(BF16)
    values = head_columns(head_count + 1).astype(BF16)
    wide_columns = head_count * token_count
    key_ids = lax.broadcasted_iota(jnp.int32, (token_count, wide_columns), 0)
    query_ids = lax.broadcasted_iota(jnp.int32, (token_count, wide_columns), 1) % token_count
    allowed = key_ids <= query_ids
    own_head = lax.broadcasted_iota(jnp.int32, (8, wide_columns), 0) == (
        lax.broadcasted_iota(jnp.int32, (8, wide_columns), 1) // token_count
    )
    for item in range(item_count):
        span = slice(item * token_count, (item + 1) * token_count)
        asked = jnp.concatenate([query[span] for query in queries], axis=0)
        scores = dot_nt(keys[span], asked) * (1.0 / math.sqrt(HEAD_TXT))
        scores = jnp.where(allowed, scores, -1e30)
        exps = jnp.exp(scores - jnp.max(scores, axis=0, keepdims=True))
        share = (1.0 / token_count) / jnp.sum(exps, axis=0, keepdims=True)
        share = jnp.where(own_head, share, 0.0).astype(BF16)
        weights = dot_nt(share, exps.astype(BF16))
        heads_mean[:, item, :] = dot_two(weights, values[span])
    pooled = residual * flag_ref[0].astype(F32)
    for head in range(head_count):
        pooled = pooled + dot_two(heads_mean[head], w_out[head * HEAD_TXT : (head + 1) * HEAD_TXT, :])
    pooled_ref[...] = pooled

def text_pooled(texts, slot, flag):
    item_count, token_count, model_width = texts.shape
    half_width = model_width // 2
    inner = half_width + 2 * HEAD_TXT
    cosine, sine = rope_tables(token_count, item_count)
    vm = pl.BlockSpec(memory_space=pltpu.VMEM)
    return pl.pallas_call(
        text_kernel,
        in_specs=[pl.BlockSpec(memory_space=pltpu.SMEM)] + [vm] * 4,
        out_specs=vm,
        out_shape=jax.ShapeDtypeStruct((item_count, model_width), F32),
        scratch_shapes=[
            pltpu.VMEM((model_width, inner), BF16),
            pltpu.VMEM((half_width, model_width), BF16),
            pltpu.VMEM((128 * 12, 128), F32),
            pltpu.VMEM((8, item_count, HEAD_TXT), F32),
        ],
        compiler_params=pltpu.CompilerParams(vmem_limit_bytes=40 * 1024 * 1024),
    )(flag, texts, slot, jnp.asarray(cosine), jnp.asarray(sine))

def merge_forward(embedded, stacked):
    first_rows = embedded.shape[1]
    float_embed = embedded.astype(jnp.float32)
    normed = (
        float_embed
        * lax.rsqrt(jnp.mean(float_embed * float_embed, axis=1, keepdims=True) + norm_eps)
    ).astype(jnp.bfloat16)
    hidden = jnp.dot(normed, stacked[:first_rows], preferred_element_type=jnp.float32)
    activated = gelu_value(hidden).astype(jnp.bfloat16)
    merged = jnp.dot(activated, stacked[first_rows:], preferred_element_type=jnp.float32).astype(
        jnp.bfloat16
    )
    return (normed, hidden, activated, merged)


def merge_backward(hidden, stacked, out_grad, first_rows):
    w_second = stacked[first_rows:]
    act_grad = lax.dot_general(
        out_grad, w_second, (((1,), (1,)), ((), ())), preferred_element_type=jnp.float32
    )
    return (act_grad * gelu_slope(hidden)).astype(jnp.bfloat16)


def item_loss(merged_row, book_rows, negatives):
    emb_width = merged_row.shape[0]
    quant_tau = math.sqrt(emb_width) / 2.0
    residual = merged_row * lax.rsqrt(jnp.mean(merged_row * merged_row) + norm_eps)
    quantized = jnp.zeros_like(merged_row)
    for level_index in range(book_rows.shape[0]):
        code_rows = book_rows[level_index]
        cross_terms = jnp.dot(code_rows, residual, precision=highest)
        logits = (2.0 * cross_terms - jnp.sum(code_rows * code_rows, axis=1)) / quant_tau
        logits = logits - lax.stop_gradient(jnp.max(logits))
        exp_logits = jnp.exp(logits)
        chosen = jnp.dot(exp_logits / jnp.sum(exp_logits), code_rows, precision=highest)
        residual = residual - chosen
        quantized = quantized + chosen
    recon_error = jnp.mean(residual * residual)
    anchor = quantized * lax.rsqrt(jnp.mean(quantized * quantized) + norm_eps)
    candidates = jnp.concatenate([merged_row[None, :], negatives.astype(jnp.float32)], axis=0)
    cand_unit = candidates * lax.rsqrt(
        jnp.mean(candidates * candidates, axis=1, keepdims=True) + norm_eps
    )
    similarity = jnp.dot(cand_unit, anchor, precision=highest) / (emb_width * contrast_temp)
    top_score = lax.stop_gradient(jnp.max(similarity))
    contrast = top_score + jnp.log(jnp.sum(jnp.exp(similarity - top_score))) - similarity[0]
    return contrast + beta_weight * recon_error


def stacked_term(columns, first_grad, second_grad, in_first):
    contract = (((0,), (0,)), ((), ()))
    first_term = lax.dot_general(columns, first_grad, contract, preferred_element_type=jnp.float32)
    second_term = lax.dot_general(
        columns, second_grad, contract, preferred_element_type=jnp.float32
    )
    return jnp.where(in_first[:, None], first_term, second_term)


def cost(flops, moved):
    return pl.CostEstimate(flops=flops, bytes_accessed=moved, transcendentals=0)


def first_rows_in(shard, shard_rows, first_rows):
    return min(max(first_rows - shard * shard_rows, 0), shard_rows)


def unit_groups(shard_count, shard_rows, first_rows, part_count):
    groups = []
    for shard in range(shard_count):
        inside = first_rows_in(shard, shard_rows, first_rows)
        if inside < shard_rows:
            groups.append((shard, inside, shard * shard_rows + inside - first_rows, (shard_rows - inside) // part_count))
    return groups


def even_units(groups, shard_rows, part_count):
    return all(
        inside % TILE == 0 and share % TILE == 0 and inside + share * part_count == shard_rows
        for _, inside, _, share in groups
    )


def message_kernel(groups, rows_ref, message_ref, built, semaphores):
    shard, segment = lax.axis_index("dp"), lax.axis_index("segment")
    copies, _, columns = message_ref.shape
    row_count, width = rows_ref.shape
    segment_count = width // (SIDES * columns)
    first_last = groups[0][0]

    for part in range(segment_count):
        here = segment == part

        @pl.when((shard <= first_last) & here)
        def _(part=part):
            for side in range(SIDES):
                picked = []
                for _, _, base, share in groups:
                    start = base + share * (side * segment_count + part)
                    picked.append(rows_ref[:, start : start + share])
                built[side] = jnp.concatenate(picked, axis=1)

        for group_shard, inside, _, share in groups:

            @pl.when((shard == group_shard) & here)
            def _(part=part, inside=inside, share=share):
                for side in range(SIDES):
                    start = inside + share * (side * segment_count + part)
                    low = start // 16 * 16
                    high = min(row_count, -(-(start + share) // 16) * 16)
                    taken = rows_ref[low:high, :].astype(F32)[start - low : start - low + share]
                    pieces = [taken[:, block * columns : (block + 1) * columns] for block in range(width // columns)]
                    built[side, inside:, :] = jnp.concatenate(pieces, axis=0).astype(BF16)

    sends = [
        pltpu.make_async_copy(built.at[copy % SIDES], message_ref.at[copy, :row_count], semaphores.at[copy]) for copy in range(copies)
    ]
    for send in sends:
        send.start()
    for send in sends:
        send.wait()


def weight_message(uniting_weights, groups, copies, columns):
    shard_rows = uniting_weights.shape[0]
    return pl.pallas_call(
        functools.partial(message_kernel, groups),
        in_specs=[pl.BlockSpec(memory_space=pltpu.VMEM)],
        out_specs=pl.BlockSpec(memory_space=pl.ANY),
        out_shape=jax.ShapeDtypeStruct((copies, shard_rows + 16, columns), BF16),
        scratch_shapes=[pltpu.VMEM((SIDES, shard_rows, columns), BF16), pltpu.SemaphoreType.DMA((copies,))],
        cost_estimate=cost(0, 4 * uniting_weights.size),
    )(uniting_weights)


def forward_kernel(
    groups,
    first_rows,
    mine_ref,
    twin_ref,
    own_ref,
    weights,
    block_ref,
    hidden_ref,
    active_ref,
    second_ref,
    partial_ref,
):
    shard_count, _, columns = weights.shape
    shard_rows = block_ref.shape[1]
    shard = lax.axis_index("dp")
    source_count, source_items, half = mine_ref.shape
    items, width = source_count * source_items, 2 * half
    mine = mine_ref[...].astype(F32).reshape(items, half)
    twin = twin_ref[...].astype(F32).reshape(items, half)
    first_core = lax.rem(lax.axis_index("segment"), 2) == 0
    embedded = jnp.concatenate([jnp.where(first_core, mine, twin), jnp.where(first_core, twin, mine)], axis=1)
    normed = embedded * lax.rsqrt(jnp.mean(embedded * embedded, axis=1, keepdims=True) + norm_eps)
    normed = normed.astype(BF16)
    hidden = jnp.zeros((items, columns), F32)
    own_block = jnp.zeros((items, shard_rows), BF16)
    for block in range(shard_count):
        inside = first_rows_in(block, shard_rows, first_rows)
        start = block * shard_rows
        if inside > 0:
            rows = normed[:, start : start + inside]
            hidden = hidden + dot_nn(rows, weights[block, :inside])
            if inside < shard_rows:
                rows = jnp.concatenate([rows, jnp.zeros((items, shard_rows - inside), BF16)], axis=1)
            own_block = jnp.where(shard == block, rows, own_block)
    block_ref[...] = own_block
    hidden_ref[...] = hidden
    active = gelu_value(hidden).astype(BF16)
    active_ref[...] = active
    lines = []
    for block, inside, _, share in groups:
        rows = weights[block, inside:shard_rows, :].astype(F32)
        pieces = [rows[part * share : (part + 1) * share] for part in range(partial_ref.shape[1] // columns)]
        lines.append(jnp.concatenate(pieces, axis=1))
    second_ref[...] = jnp.concatenate(lines, axis=0).astype(BF16)
    partial_ref[...] = dot_nn(dot_nn(own_ref[...], active).astype(BF16), second_ref[...])


def merge_part(mine_half, twin_half, pieces, own, groups, shard_rows, first_rows, width):
    shard_count, _, columns = pieces.shape
    items = mine_half.shape[0] * mine_half.shape[1]
    vm = pl.BlockSpec(memory_space=pltpu.VMEM)
    return pl.pallas_call(
        functools.partial(forward_kernel, groups, first_rows),
        in_specs=[vm] * 4,
        out_specs=[vm] * 5,
        out_shape=[
            jax.ShapeDtypeStruct((items, shard_rows), BF16),
            jax.ShapeDtypeStruct((items, columns), F32),
            jax.ShapeDtypeStruct((items, columns), BF16),
            jax.ShapeDtypeStruct((columns, width), BF16),
            jax.ShapeDtypeStruct((own.shape[0], width), F32),
        ],
        cost_estimate=cost(2 * items * first_rows * columns, 2 * pieces.size),
        compiler_params=pltpu.CompilerParams(vmem_limit_bytes=8 * MIB),
    )(mine_half, twin_half, own, pieces)


def split(value):
    high = value.astype(BF16)
    return high, (value - high.astype(F32)).astype(BF16)


def exact_nt(value, high, low):
    first, second = split(value)
    rows = value.shape[0]
    both = dot_nt(jnp.concatenate([first, second], axis=0), high)
    return both[:rows] + both[rows:] + dot_nt(first, low)


def exact_nn(value, high, low):
    first, second = split(value)
    rows = value.shape[0]
    both = dot_nn(jnp.concatenate([first, second], axis=0), high)
    return both[:rows] + both[rows:] + dot_nn(first, low)


def dot_tn(a, b):
    return lax.dot_general(a, b, (((0,), (0,)), ((), ())), preferred_element_type=F32)


def exact_tn(a, b):
    a_high, a_low = split(a)
    b_high, b_low = split(b)
    return dot_tn(
        jnp.concatenate([a_high, a_low, a_high], axis=0), jnp.concatenate([b_high, b_high, b_low], axis=0)
    )


def square_sums(value):
    high, low = split(value * value)
    ones = jnp.ones((8, value.shape[1]), BF16)
    return dot_nt(ones, high) + dot_nt(ones, low)


def prepare_kernel(book_ref, bank_ref, high_ref, low_ref, norm_ref, scale_ref):
    width = bank_ref.shape[1]
    for level in range(book_ref.shape[0]):
        codes = book_ref[level]
        high, low = split(codes)
        high_ref[level] = high
        low_ref[level] = low
        norm_ref[level] = square_sums(codes)
    scale_ref[...] = lax.rsqrt(square_sums(bank_ref[...].astype(F32)) * (1.0 / width) + norm_eps)


def prepared(books, bank):
    levels, codes, _ = books.shape
    vm = pl.BlockSpec(memory_space=pltpu.VMEM)
    return pl.pallas_call(
        prepare_kernel,
        in_specs=[vm] * 2,
        out_specs=[vm] * 4,
        out_shape=[
            jax.ShapeDtypeStruct(books.shape, BF16),
            jax.ShapeDtypeStruct(books.shape, BF16),
            jax.ShapeDtypeStruct((levels, 8, codes), F32),
            jax.ShapeDtypeStruct((8, bank.shape[0]), F32),
        ],
        cost_estimate=cost(0, 12 * books.size),
        compiler_params=pltpu.CompilerParams(vmem_limit_bytes=10 * MIB),
    )(books, bank)


def quantizer_kernel(
    loss_scale,
    merged_ref,
    highs,
    lows,
    norm_ref,
    bank_ref,
    bank_scale_ref,
    count_ref,
    merged_grad_ref,
    loss_ref,
    left_ref,
    right_ref,
):
    width = merged_ref.shape[1]
    levels = highs.shape[0]
    inverse_tau = 2.0 / math.sqrt(width)
    inverse_temp = 1.0 / (width * contrast_temp)
    merged = merged_ref[...].astype(BF16).astype(F32)
    merged_scale = lax.rsqrt(jnp.mean(merged * merged, axis=1, keepdims=True) + norm_eps)
    residuals = [merged * merged_scale]
    shares, chosen_rows = [], []
    for level in range(levels):
        high, low = highs[level], lows[level]
        logits = (2.0 * exact_nt(residuals[level], high, low) - norm_ref[level]) * inverse_tau
        exps = jnp.exp(logits - jnp.max(logits, axis=1, keepdims=True))
        share = exps / jnp.sum(exps, axis=1, keepdims=True)
        chosen = exact_nn(share, high, low)
        shares.append(share)
        chosen_rows.append(chosen)
        residuals.append(residuals[level] - chosen)
    last = residuals[levels]
    quantized = chosen_rows[0]
    for chosen in chosen_rows[1:]:
        quantized = quantized + chosen
    anchor_scale = lax.rsqrt(jnp.mean(quantized * quantized, axis=1, keepdims=True) + norm_eps)
    anchor = quantized * anchor_scale
    own = jnp.sum(anchor * residuals[0], axis=1, keepdims=True) * inverse_temp
    bank = bank_ref[...]
    bank_scale = bank_scale_ref[...]
    anchor_parts = jnp.concatenate(split(anchor), axis=0)
    rows = anchor.shape[0]
    both = dot_nt(anchor_parts, bank)
    similar = (both[:rows] + both[rows:]) * bank_scale * inverse_temp
    counts = count_ref[...]
    named = counts > 0.0
    top = jnp.maximum(jnp.max(jnp.where(named, similar, own), axis=1, keepdims=True), own)
    bank_exps = jnp.where(named, jnp.exp(jnp.where(named, similar, top) - top), 0.0) * counts
    own_exp = jnp.exp(own - top)
    total = jnp.sum(bank_exps, axis=1, keepdims=True) + own_exp
    item_losses = top + jnp.log(total) - own + jnp.mean(last * last, axis=1, keepdims=True)
    loss_ref[0] = jnp.sum(item_losses) * loss_scale

    bank_weight = bank_exps / total * (loss_scale * inverse_temp)
    own_weight = (own_exp / total - 1.0) * (loss_scale * inverse_temp)
    weight_parts = jnp.concatenate(split(bank_weight * bank_scale), axis=0)
    both = dot_nn(weight_parts, bank)
    anchor_grad = both[:rows] + both[rows:] + own_weight * residuals[0]
    unit_grad = own_weight * anchor
    quantized_grad = anchor_scale * (anchor_grad - anchor * jnp.mean(anchor * anchor_grad, axis=1, keepdims=True))
    residual_grad = last * (2.0 * loss_scale / width)
    for level in reversed(range(levels)):
        high, low = highs[level], lows[level]
        chosen_grad = quantized_grad - residual_grad
        share_grad = exact_nt(chosen_grad, high, low)
        share = shares[level]
        logit_grad = share * (share_grad - jnp.sum(share * share_grad, axis=1, keepdims=True)) * (2.0 * inverse_tau)
        left_ref[level] = jnp.concatenate([share, logit_grad], axis=0)
        right_ref[level] = jnp.concatenate([chosen_grad, residuals[level]], axis=0)
        residual_grad = residual_grad + exact_nn(logit_grad, high, low)
    unit_grad = unit_grad + residual_grad
    unit = residuals[0]
    merged_grad = merged_scale * (unit_grad - unit * jnp.mean(unit * unit_grad, axis=1, keepdims=True))
    merged_grad_ref[...] = merged_grad.astype(BF16)


def quantizer(merged, ready, bank, counts, loss_scale):
    highs, lows, norms, bank_scale = ready
    levels, codes, width = highs.shape
    rows = merged.shape[0]
    vm = pl.BlockSpec(memory_space=pltpu.VMEM)
    return pl.pallas_call(
        functools.partial(quantizer_kernel, loss_scale),
        in_specs=[vm] * 7,
        out_specs=[vm, pl.BlockSpec(memory_space=pltpu.SMEM), vm, vm],
        out_shape=[
            jax.ShapeDtypeStruct(merged.shape, BF16),
            jax.ShapeDtypeStruct((1,), F32),
            jax.ShapeDtypeStruct((levels, 2 * rows, codes), F32),
            jax.ShapeDtypeStruct((levels, 2 * rows, width), F32),
        ],
        cost_estimate=cost(64 * highs.size, 4 * highs.size),
        compiler_params=pltpu.CompilerParams(vmem_limit_bytes=12 * MIB),
    )(merged, highs, lows, norms, bank, bank_scale, counts)


def codebook_kernel(left_ref, right_ref, book_ref, grad_ref):
    levels, doubled, _ = left_ref.shape
    width = right_ref.shape[2]
    rows = doubled // 2
    ones = jnp.ones((rows, 128), F32)
    for level in range(levels):
        outer = exact_tn(left_ref[level], right_ref[level])
        totals = exact_tn(left_ref[level, rows:], ones)
        for block in range(width // 128):
            span = slice(block * 128, (block + 1) * 128)
            grad_ref[level, :, span] = outer[:, span] - totals * book_ref[level, :, span]


def codebook_grad(left, right, books):
    vm = pl.BlockSpec(memory_space=pltpu.VMEM)
    return pl.pallas_call(
        codebook_kernel,
        in_specs=[vm] * 3,
        out_specs=vm,
        out_shape=jax.ShapeDtypeStruct(books.shape, F32),
        cost_estimate=cost(96 * books.size, 8 * books.size),
        compiler_params=pltpu.CompilerParams(vmem_limit_bytes=10 * MIB),
    )(left, right, books)


def backward_kernel(gathered_ref, order_ref, hidden_ref, active_ref, second_ref, out_grad_ref, sent_ref):
    owners, places, width = gathered_ref.shape
    columns = hidden_ref.shape[1]
    gathered = gathered_ref[...].astype(F32).reshape(owners * places, width).astype(BF16)
    out_grad = dot_tn(order_ref[...], gathered).astype(BF16)
    out_grad_ref[...] = out_grad
    hidden_grad = dot_nt(out_grad, second_ref[...]) * gelu_slope(hidden_ref[...])
    sent_ref[:, :columns] = hidden_grad.astype(BF16)
    sent_ref[:, columns:] = active_ref[...]


def backward_part(gathered, order, hidden, active, second):
    items, columns = hidden.shape
    vm = pl.BlockSpec(memory_space=pltpu.VMEM)
    return pl.pallas_call(
        backward_kernel,
        in_specs=[vm] * 5,
        out_specs=[vm] * 2,
        out_shape=[
            jax.ShapeDtypeStruct((items, gathered.shape[2]), BF16),
            jax.ShapeDtypeStruct((items, 2 * columns), BF16),
        ],
        cost_estimate=cost(2 * items * second.size, 2 * second.size),
        compiler_params=pltpu.CompilerParams(vmem_limit_bytes=8 * MIB),
    )(gathered, order, hidden, active, second)


def weight_grad_kernel(
    groups, block_ref, out_grad_ref, mine_ref, twin_ref, grad_ref, hidden_grad, active
):
    shard, segment = lax.axis_index("dp"), lax.axis_index("segment")
    _, items, doubled = mine_ref.shape
    cores = 2
    own_core = lax.rem(segment, cores)
    columns = doubled // 2
    shard_rows = block_ref.shape[1]
    own_side, own_row = lax.rem(shard, SIDES), segment // cores
    segment_count = hidden_grad.shape[1] // (SIDES * columns)

    def place_units(target, first):
        for side in range(SIDES):
            for other in range(segment_count):
                parts = [
                    jnp.where(
                        own_core == other % cores,
                        mine_ref[index, :, first : first + columns],
                        twin_ref[index, :, first : first + columns],
                    )
                    for index in range(4)
                ]
                same_row = own_row == other // cores
                near = jnp.where(same_row, parts[0], parts[1])
                across = jnp.where(same_row, parts[2], parts[3])
                part = jnp.where(own_side == side, near, across)
                offset = 0
                for _, _, base, share in groups:
                    spot = base + share * (side * segment_count + other)
                    target[:, spot : spot + share] = part[:, offset : offset + share]
                    offset += share

    place_units(hidden_grad, 0)
    grad_ref[...] = dot_tn(block_ref[...], hidden_grad[...])
    for group_shard, inside, base, _ in groups:

        @pl.when(shard == group_shard)
        def _(inside=inside, base=base):
            place_units(active, columns)
            wanted = active[:, base : base + shard_rows - inside]
            grad_ref[inside:, :] = dot_tn(wanted, out_grad_ref[...])


def weight_grad(block, out_grad, mine, twin, groups):
    items, shard_rows = block.shape
    width = out_grad.shape[1]
    vm = pl.BlockSpec(memory_space=pltpu.VMEM)
    return pl.pallas_call(
        functools.partial(weight_grad_kernel, groups),
        in_specs=[vm] * 4,
        out_specs=vm,
        out_shape=jax.ShapeDtypeStruct((shard_rows, width), F32),
        scratch_shapes=[pltpu.VMEM((items, width), BF16), pltpu.VMEM((items, width), BF16)],
        cost_estimate=cost(2 * items * shard_rows * width, 4 * shard_rows * width),
        compiler_params=pltpu.CompilerParams(vmem_limit_bytes=8 * MIB),
    )(block, out_grad, mine, twin)


def around(near, across, segment_count, dp_count):
    row = lax.ppermute(near, "segment", [(j, j ^ 2) for j in range(segment_count)])
    side = lax.ppermute(across, "dp", [(i, i ^ 1) for i in range(dp_count)])
    corners = [
        (j * dp_count + i, (j ^ 2) * dp_count + (i ^ 1)) for j in range(segment_count) for i in range(dp_count)
    ]
    corner = lax.ppermute(across, ("segment", "dp"), corners)
    return row, side, corner


def spread(rows, axis_name, count):
    return lax.all_to_all(
        jnp.broadcast_to(rows[None], (count,) + rows.shape), axis_name, 0, 0, tiled=True
    )


def per_device_parts(
    images, texts, section_weights, uniting_weights, codebooks, neg_bank, item_cats, cat_slot, neg_index
):
    segment_index = lax.axis_index("segment")
    segment_count = lax.axis_size("segment")
    dp_index = lax.axis_index("dp")
    dp_count = lax.axis_size("dp")
    item_count, _, image_width = images.shape
    text_width = texts.shape[2]
    first_rows = image_width + text_width
    shard_rows, width = uniting_weights.shape
    columns = width // (SIDES * segment_count)
    groups = unit_groups(dp_count, shard_rows, first_rows, SIDES * segment_count)
    message = weight_message(uniting_weights, groups, dp_count, columns)
    flag = (1 - segment_index % 2).astype(jnp.int32).reshape(1)
    flag, message = lax.optimization_barrier((flag, message))
    pieces = lax.all_to_all(message, "dp", 0, 0, tiled=True)
    pooled = pooled_features(images, texts, section_weights, segment_index, flag)
    pooled = pooled + lax.ppermute(pooled, "segment", [(i, i ^ 1) for i in range(segment_count)])
    mine = pooled.astype(BF16)
    other = lax.ppermute(mine, "segment", [(i, i ^ 2) for i in range(segment_count)])
    is_image = segment_index < 2
    embedded = jnp.concatenate(
        [jnp.where(is_image, mine, other)[:, :image_width], jnp.where(is_image, other, mine)], axis=1
    )
    embedded, pieces, books = lax.optimization_barrier((embedded, pieces, codebooks[0]))
    half = first_rows // 2
    embedded_half = jnp.where(segment_index % 2 == 0, embedded[:, :half], embedded[:, half:])
    mine_half = spread(embedded_half, "dp", dp_count)
    twin_half = lax.ppermute(mine_half, "segment", [(i, i ^ 1) for i in range(segment_count)])

    pair = item_cats.shape[1] // dp_count
    cats = item_cats.reshape(segment_count, dp_count, pair).transpose(1, 0, 2).reshape(-1)
    items = cats.shape[0]
    slots = jnp.sum(
        jnp.where(cats[:, None] == jnp.arange(cat_slot.shape[0])[None, :], cat_slot[None, :], 0), axis=1
    )
    ids = jnp.arange(items)
    rank = jnp.sum(jnp.where((slots[None, :] == slots[:, None]) & (ids[None, :] < ids[:, None]), 1, 0), axis=1)
    owned = segment_count * CAP
    order = (ids[:, None] == (slots * owned + rank)[None, :]).astype(BF16)
    own = lax.dynamic_slice_in_dim(order, dp_index * owned, owned, 0)
    across_own = lax.dynamic_slice_in_dim(order, (dp_index ^ 1) * owned, owned, 0)
    both_own = jnp.concatenate([own, across_own], axis=0)
    negatives = neg_index.reshape(segment_count, dp_count, pair, -1).transpose(1, 0, 2, 3).reshape(items, -1)
    own_negatives = jnp.dot(own.astype(F32), negatives.astype(F32), precision=highest)
    bank = neg_bank[0]
    ready = prepared(books, bank)
    bank_ids = jnp.arange(bank.shape[0]).astype(F32)
    counts = jnp.sum((own_negatives[:, :, None] == bank_ids[None, None, :]).astype(F32), axis=1)

    block, hidden, active, second, partial = merge_part(
        mine_half, twin_half, pieces, both_own, groups, shard_rows, first_rows, width
    )
    partial = partial + lax.ppermute(partial, "segment", [(i, i ^ 1) for i in range(segment_count)])
    row, side, corner = around(partial[:owned], partial[owned:], segment_count, dp_count)
    merged = (partial[:owned] + row) + (side + corner)
    merged_grad, loss, left, right = quantizer(merged, ready, bank, counts, 1.0 / math.sqrt(items))
    gathered = spread(merged_grad, "dp", dp_count)
    book_grad = codebook_grad(left, right, books)
    out_grad, sent = backward_part(gathered, order, hidden, active, second)
    mine = jnp.stack((sent,) + around(sent, sent, segment_count, dp_count))
    mine, book_grad = lax.optimization_barrier((mine, book_grad))
    twin = lax.ppermute(mine, "segment", [(i, i ^ 1) for i in range(segment_count)])
    uniting_grad = weight_grad(block, out_grad, mine, twin, groups)
    return (uniting_grad, book_grad[None], loss)


def pooled_features(images, texts, section_weights, segment_index, flag):
    image_width, text_width = images.shape[2], texts.shape[2]

    def image_branch(operands):
        pooled = image_pooled(operands[0], operands[2], flag)
        return jnp.pad(pooled, ((0, 0), (0, text_width - image_width)))

    def text_branch(operands):
        return text_pooled(operands[1], operands[2], flag)

    return lax.cond(segment_index < 2, image_branch, text_branch, (images, texts, section_weights))


def per_device_gathered(
    images,
    texts,
    section_weights,
    uniting_weights,
    codebooks,
    neg_bank,
    item_cats,
    cat_slot,
    neg_index,
):
    segment_index = lax.axis_index("segment")
    segment_count = lax.axis_size("segment")
    dp_index = lax.axis_index("dp")
    dp_count = lax.axis_size("dp")
    group_index = segment_index % 2
    item_count = images.shape[0]

    flag = (1 - group_index).astype(jnp.int32).reshape(1)
    pooled = pooled_features(images, texts, section_weights, segment_index, flag)
    image_width = images.shape[2]
    is_image = segment_index < 2
    packed = jnp.concatenate(
        [jnp.where(is_image, pooled[:, :image_width], 0.0), jnp.where(is_image, 0.0, pooled)], axis=1
    )
    embedded = lax.psum_scatter(packed, "segment", scatter_dimension=0, tiled=True).astype(
        jnp.bfloat16
    )
    stacked = lax.all_gather(uniting_weights, "dp", axis=0, tiled=True)
    first_rows = embedded.shape[1]
    cat_per_dev = codebooks.shape[0]
    slot_count = cat_per_dev * CAP
    row_total = item_cats.shape[1]
    cats_all = item_cats.reshape(-1)
    entry_count = cats_all.shape[0]
    entry_ids = jnp.arange(entry_count)
    category_match = cats_all[:, None] == jnp.arange(cat_slot.shape[0])[None, :]
    entry_slots = jnp.sum(jnp.where(category_match, cat_slot[None, :], 0), axis=1)
    entry_owner = entry_slots // cat_per_dev
    entry_local = entry_slots % cat_per_dev
    entry_row = entry_ids // row_total
    earlier = entry_ids[None, :] < entry_ids[:, None]
    same_cat = (cats_all[:, None] == cats_all[None, :]) & (entry_row[:, None] == entry_row[None, :])
    entry_rank = jnp.sum(jnp.where(earlier & same_cat, 1, 0), axis=1)
    entry_place = entry_local * CAP + entry_rank
    entry_position = entry_row * slot_count + entry_place
    owned = entry_owner == dp_index
    all_slots = segment_count * slot_count
    slot_match_all = owned[None, :] & (entry_position[None, :] == jnp.arange(all_slots)[:, None])
    view_match = lax.dynamic_slice(
        slot_match_all,
        (segment_index * slot_count, segment_index * row_total),
        (slot_count, row_total),
    )
    view_base = segment_index * row_total
    view_slots = view_match.shape[0]
    selection = view_match.astype(jnp.bfloat16)
    valid = jnp.sum(view_match.astype(jnp.float32), axis=1)
    slot_item = jnp.sum(
        jnp.where(view_match, jnp.arange(view_match.shape[1])[None, :] + view_base, 0), axis=1
    )
    slot_negs = jnp.take(neg_index.reshape(entry_count, -1), slot_item, axis=0)
    slot_local = jnp.arange(view_slots) % slot_count // CAP
    bank_rows = neg_bank.reshape(-1, neg_bank.shape[2])
    negatives = jnp.take(bank_rows, slot_local[:, None] * neg_bank.shape[1] + slot_negs, axis=0)
    loss_scale = 1.0 / math.sqrt(dp_count * item_count)

    def owner_objective(merged_float, books):
        per_row = jax.vmap(item_loss)(merged_float, books[slot_local], negatives)
        return jnp.sum(per_row * valid) * loss_scale

    gathered = jnp.dot(
        selection,
        lax.all_gather(embedded, "dp", axis=0, tiled=True),
        preferred_element_type=jnp.float32,
    )
    gathered = gathered.astype(jnp.bfloat16)
    normed_all, hidden_all, activated_all, merged_all = merge_forward(gathered, stacked)
    loss_local, pullback = jax.vjp(owner_objective, merged_all.astype(jnp.float32), codebooks)
    grad_all, book_grad = pullback(jnp.ones((), jnp.float32))
    out_grad = grad_all.astype(jnp.bfloat16)
    hidden_grad = merge_backward(hidden_all, stacked, out_grad, first_rows)
    joined = jnp.concatenate([normed_all, activated_all], axis=1)
    book_total, loss_owner = lax.psum((book_grad, loss_local), "segment")
    shard_rows = uniting_weights.shape[0]
    shard_start = dp_index * shard_rows
    shard_first = shard_start + jnp.arange(shard_rows) < first_rows
    joined_piece = lax.all_gather(joined, "dp", axis=0, tiled=True)
    first_piece = lax.all_gather(hidden_grad, "dp", axis=0, tiled=True)
    second_piece = lax.all_gather(out_grad, "dp", axis=0, tiled=True)
    columns = lax.dynamic_slice_in_dim(joined_piece, shard_start, shard_rows, 1)
    segment_grad = stacked_term(columns, first_piece, second_piece, shard_first)
    uniting_grad = lax.psum(segment_grad, "segment")
    return (uniting_grad, book_total, loss_owner.reshape(1))


def per_device(*operands):
    images, texts, _, uniting_weights = operands[:4]
    segment_count, dp_count = lax.axis_size("segment"), lax.axis_size("dp")
    shard_rows = uniting_weights.shape[0]
    first_rows = images.shape[2] + texts.shape[2]
    groups = unit_groups(dp_count, shard_rows, first_rows, SIDES * segment_count)
    if dp_count % SIDES == 0 and even_units(groups, shard_rows, SIDES * segment_count):
        return per_device_parts(*operands)
    return per_device_gathered(*operands)


def solution(mesh):
    placed = (
        P("dp", None, None),
        P("dp", None, None),
        P("segment", None, None),
        P("dp", None),
        P("dp", None, None, None),
        P("dp", None, None),
        P(),
        P(),
        P(),
    )
    return jax.shard_map(
        per_device,
        mesh=mesh,
        in_specs=placed,
        out_specs=(P("dp", None), P("dp", None, None, None), P("dp")),
        check_vma=False,
    )
```

```python
import functools
import math

import jax
import jax.numpy as jnp
import numpy as np
from jax import lax
from jax.experimental import pallas as pl
from jax.experimental.pallas import tpu as pltpu
from jax.sharding import PartitionSpec as P

F32 = jnp.float32
BF16 = jnp.bfloat16

HEAD_IMG = 64
HEAD_TXT = 128
CAP = 2
OWNED = 4 * CAP
MIB = 1024 * 1024
IMAGE_GROUP = 4
PROJECT_LANES = 256
OUT_STEP = 128
GRAD_ROWS = 128
LOG2_E = 1.4426950408889634
SIDES = 2
TILE = 8


norm_eps = 1e-06
rope_theta = 1000000.0
contrast_temp = 0.1
beta_weight = 1.0
highest = lax.Precision.HIGHEST


def gelu_value(inputs_f):
    return 0.5 * inputs_f * (1.0 + lax.erf(inputs_f / math.sqrt(2.0)))


def gelu_slope(inputs_f):
    return 0.5 * (1.0 + lax.erf(inputs_f / math.sqrt(2.0))) + inputs_f * jnp.exp(
        -0.5 * inputs_f * inputs_f
    ) / math.sqrt(2.0 * math.pi)


def dot_nt(a, b):
    return lax.dot_general(a, b, (((1,), (1,)), ((), ())), preferred_element_type=F32)

def dot_nn(a, b):
    return jnp.dot(a, b, preferred_element_type=F32)

def two_parts(value):
    high = value.astype(BF16)
    return jnp.concatenate([high, (value - high.astype(F32)).astype(BF16)], axis=0)

def dot_two(value, weights):
    rows = value.shape[0]
    both = dot_nn(two_parts(value), weights)
    return both[:rows] + both[rows:]

def unfold_step(slot_ref, first, out_ref, wide_ref, row_step, step):
    blocks = out_ref.shape[1] // 128
    start = step * row_step
    source = first + step * (row_step * blocks)
    if not isinstance(step, int):
        start, source = pl.multiple_of(start, row_step), pl.multiple_of(source, 16)
    wide_ref[0 : row_step * blocks, :] = slot_ref[0, pl.ds(source, row_step * blocks), :].astype(F32)
    for block in range(blocks):
        piece = wide_ref[pl.ds(block, row_step, stride=blocks), :]
        out_ref[pl.ds(start, row_step), block * 128 : (block + 1) * 128] = piece.astype(BF16)


def unfold(slot_ref, first, out_ref, wide_ref, row_step):
    def body(step, carry):
        unfold_step(slot_ref, first, out_ref, wide_ref, row_step, step)
        return carry

    lax.fori_loop(0, out_ref.shape[0] // row_step, body, 0)


def image_kernel(
    flag_ref, image_hbm, slot_hbm, pooled_ref, image, rows_in, rows_out, w_in, w_out, wide, normed, joined, heads_mean, semaphores
):
    item_count, patch_count, model_width = image.shape
    half_width = model_width // 2
    head_count = half_width // HEAD_IMG
    groups = item_count // IMAGE_GROUP
    group_rows = IMAGE_GROUP * patch_count
    in_rows, out_rows = rows_in.shape[1], rows_out.shape[1]
    members = [pl.ds(index * IMAGE_GROUP, IMAGE_GROUP) for index in range(groups)]
    fetches = [pltpu.make_async_copy(image_hbm.at[span], image.at[span], semaphores.at[index]) for index, span in enumerate(members)]
    fetch_in = pltpu.make_async_copy(slot_hbm.at[:, pl.ds(0, in_rows)], rows_in, semaphores.at[groups])
    fetch_out = pltpu.make_async_copy(slot_hbm.at[:, pl.ds(in_rows, out_rows)], rows_out, semaphores.at[groups + 1])
    fetches[0].start()
    fetch_in.start()
    for fetch in fetches[1:]:
        fetch.start()
    fetch_out.start()
    flag = flag_ref[0].astype(F32)

    def normalize(first, last):
        for member in range(first, last):
            tokens = image[member].astype(F32)
            centred = tokens - jnp.mean(tokens, axis=1, keepdims=True)
            variance = jnp.mean(centred * centred, axis=1, keepdims=True)
            normed[member] = (centred * lax.rsqrt(variance + norm_eps)).astype(BF16)
            pooled_ref[member : member + 1, :] = jnp.mean(tokens, axis=0, keepdims=True) * flag

    def project(index, part):
        lanes = slice(part * PROJECT_LANES, (part + 1) * PROJECT_LANES)
        span = slice(index * IMAGE_GROUP, (index + 1) * IMAGE_GROUP)
        result = dot_nn(normed[span].reshape(group_rows, model_width), w_in[:, lanes])
        if (part + 1) * PROJECT_LANES <= half_width:
            result = result * (LOG2_E / math.sqrt(HEAD_IMG))
        joined[index, :, lanes] = result.astype(BF16)

    parts = 2 * half_width // PROJECT_LANES
    row_ids = lax.broadcasted_iota(jnp.int32, (head_count, patch_count), 0)
    fetches[0].wait()
    normalize(0, IMAGE_GROUP)
    fetch_in.wait()
    unfold(rows_in, 0, w_in, wide, 128)
    for fetch in fetches[1:]:
        fetch.wait()
    fetch_out.wait()
    for part in range(parts):
        project(0, part)
        normalize(IMAGE_GROUP + part, IMAGE_GROUP + part + 1)
    out_steps = half_width // OUT_STEP
    units = IMAGE_GROUP * head_count
    for index in range(groups):
        for member in range(IMAGE_GROUP):
            rows = slice(member * patch_count, (member + 1) * patch_count)
            weights = jnp.zeros((head_count, patch_count), F32)
            for head in range(head_count):
                unit = member * head_count + head
                if index + 1 < groups and unit * parts % units < parts:
                    project(index + 1, unit * parts // units)
                if index + 1 == groups and unit * out_steps % units < out_steps:
                    unfold_step(rows_out, 0, w_out, wide, OUT_STEP, unit * out_steps // units)
                span = slice(head * HEAD_IMG, (head + 1) * HEAD_IMG)
                key_span = slice(half_width + head * HEAD_IMG, half_width + (head + 1) * HEAD_IMG)
                scores = dot_nt(joined[index, rows, span], joined[index, rows, key_span])
                exps = jnp.exp2(scores - jnp.max(scores, axis=1, keepdims=True))
                share = (1.0 / patch_count) / jnp.sum(exps, axis=1, keepdims=True)
                mean_share = jnp.sum(exps * share, axis=0, keepdims=True)
                weights = weights + jnp.where(row_ids == head, mean_share, 0.0)
            item = index * IMAGE_GROUP + member
            heads_mean[item * head_count : (item + 1) * head_count, :] = dot_two(weights, normed[item])
    values = dot_two(heads_mean[...], w_in[:, 2 * half_width :])
    rows = lax.broadcasted_iota(jnp.int32, values.shape, 0)
    columns = lax.broadcasted_iota(jnp.int32, values.shape, 1)
    values = jnp.where(rows % head_count == columns // HEAD_IMG, values, 0.0)
    attended = jnp.sum(values.reshape(item_count, head_count, half_width), axis=1)
    pooled_ref[...] += dot_two(attended, w_out[...])


def image_pooled(images, slot, flag):
    item_count, patch_count, model_width = images.shape
    half_width = model_width // 2
    head_count = half_width // HEAD_IMG
    groups = item_count // IMAGE_GROUP
    anywhere = pl.BlockSpec(memory_space=pl.ANY)
    return pl.pallas_call(
        image_kernel,
        in_specs=[pl.BlockSpec(memory_space=pltpu.SMEM), anywhere, anywhere],
        out_specs=pl.BlockSpec(memory_space=pltpu.VMEM),
        out_shape=jax.ShapeDtypeStruct((item_count, model_width), F32),
        scratch_shapes=[
            pltpu.VMEM(images.shape, BF16),
            pltpu.VMEM((1, 12 * model_width, 128), BF16),
            pltpu.VMEM((1, 4 * model_width, 128), BF16),
            pltpu.VMEM((model_width, 3 * half_width), BF16),
            pltpu.VMEM((half_width, model_width), BF16),
            pltpu.VMEM((128 * 12, 128), F32),
            pltpu.VMEM(images.shape, BF16),
            pltpu.VMEM((groups, IMAGE_GROUP * patch_count, 2 * half_width), BF16),
            pltpu.VMEM((item_count * head_count, model_width), F32),
            pltpu.SemaphoreType.DMA((groups + 2,)),
        ],
        compiler_params=pltpu.CompilerParams(vmem_limit_bytes=44 * 1024 * 1024),
    )(flag, images, slot)


def rope_tables(tokens, repeats):
    half = HEAD_TXT // 2
    exponents = np.arange(half).astype(np.float32) * np.float32(2.0 / HEAD_TXT)
    inverse = np.exp(np.float32(-math.log(rope_theta)) * exponents).astype(np.float32)
    angles = (np.arange(tokens).astype(np.float32)[:, None] * inverse[None, :]).astype(np.float32)
    cosine = np.concatenate([np.cos(angles), np.cos(angles)], axis=1)
    sine = np.concatenate([-np.sin(angles), np.sin(angles)], axis=1)
    return np.tile(cosine, (repeats, 1)).astype(np.float32), np.tile(sine, (repeats, 1)).astype(np.float32)

def text_kernel(flag_ref, text_ref, slot_ref, cos_ref, sin_ref, pooled_ref, w_in, w_out, wide, heads_mean):
    item_count, token_count, model_width = text_ref.shape
    half_width = model_width // 2
    head_count = half_width // HEAD_TXT
    unfold(slot_ref, 0, w_in, wide, 128)
    unfold(slot_ref, model_width * 8, w_out, wide, 128)
    tokens = text_ref[...].reshape(item_count * token_count, model_width).astype(F32)
    normed = (tokens * lax.rsqrt(jnp.mean(tokens * tokens, axis=1, keepdims=True) + norm_eps)).astype(BF16)
    residual = jnp.mean(tokens.reshape(item_count, token_count, model_width), axis=1)
    cosine, sine = cos_ref[...], sin_ref[...]

    def head_columns(head):
        return dot_nn(normed, w_in[:, head * HEAD_TXT : (head + 1) * HEAD_TXT])

    def turned(head, scale):
        part = head_columns(head)
        return ((part * cosine + pltpu.roll(part, HEAD_TXT // 2, 1) * sine).astype(BF16)).astype(F32) * scale

    queries = [(turned(head, 1.0)).astype(BF16) for head in range(head_count)]
    keys = turned(head_count, 1.0).astype(BF16)
    values = head_columns(head_count + 1).astype(BF16)
    wide_columns = head_count * token_count
    key_ids = lax.broadcasted_iota(jnp.int32, (token_count, wide_columns), 0)
    query_ids = lax.broadcasted_iota(jnp.int32, (token_count, wide_columns), 1) % token_count
    allowed = key_ids <= query_ids
    own_head = lax.broadcasted_iota(jnp.int32, (8, wide_columns), 0) == (
        lax.broadcasted_iota(jnp.int32, (8, wide_columns), 1) // token_count
    )
    for item in range(item_count):
        span = slice(item * token_count, (item + 1) * token_count)
        asked = jnp.concatenate([query[span] for query in queries], axis=0)
        scores = dot_nt(keys[span], asked) * (1.0 / math.sqrt(HEAD_TXT))
        scores = jnp.where(allowed, scores, -1e30)
        exps = jnp.exp(scores - jnp.max(scores, axis=0, keepdims=True))
        share = (1.0 / token_count) / jnp.sum(exps, axis=0, keepdims=True)
        share = jnp.where(own_head, share, 0.0).astype(BF16)
        weights = dot_nt(share, exps.astype(BF16))
        heads_mean[:, item, :] = dot_two(weights, values[span])
    pooled = residual * flag_ref[0].astype(F32)
    for head in range(head_count):
        pooled = pooled + dot_two(heads_mean[head], w_out[head * HEAD_TXT : (head + 1) * HEAD_TXT, :])
    pooled_ref[...] = pooled

def text_pooled(texts, slot, flag):
    item_count, token_count, model_width = texts.shape
    half_width = model_width // 2
    inner = half_width + 2 * HEAD_TXT
    cosine, sine = rope_tables(token_count, item_count)
    vm = pl.BlockSpec(memory_space=pltpu.VMEM)
    return pl.pallas_call(
        text_kernel,
        in_specs=[pl.BlockSpec(memory_space=pltpu.SMEM)] + [vm] * 4,
        out_specs=vm,
        out_shape=jax.ShapeDtypeStruct((item_count, model_width), F32),
        scratch_shapes=[
            pltpu.VMEM((model_width, inner), BF16),
            pltpu.VMEM((half_width, model_width), BF16),
            pltpu.VMEM((128 * 12, 128), F32),
            pltpu.VMEM((8, item_count, HEAD_TXT), F32),
        ],
        compiler_params=pltpu.CompilerParams(vmem_limit_bytes=40 * 1024 * 1024),
    )(flag, texts, slot, jnp.asarray(cosine), jnp.asarray(sine))

def merge_forward(embedded, stacked):
    first_rows = embedded.shape[1]
    float_embed = embedded.astype(jnp.float32)
    normed = (
        float_embed
        * lax.rsqrt(jnp.mean(float_embed * float_embed, axis=1, keepdims=True) + norm_eps)
    ).astype(jnp.bfloat16)
    hidden = jnp.dot(normed, stacked[:first_rows], preferred_element_type=jnp.float32)
    activated = gelu_value(hidden).astype(jnp.bfloat16)
    merged = jnp.dot(activated, stacked[first_rows:], preferred_element_type=jnp.float32).astype(
        jnp.bfloat16
    )
    return (normed, hidden, activated, merged)


def merge_backward(hidden, stacked, out_grad, first_rows):
    w_second = stacked[first_rows:]
    act_grad = lax.dot_general(
        out_grad, w_second, (((1,), (1,)), ((), ())), preferred_element_type=jnp.float32
    )
    return (act_grad * gelu_slope(hidden)).astype(jnp.bfloat16)


def item_loss(merged_row, book_rows, negatives):
    emb_width = merged_row.shape[0]
    quant_tau = math.sqrt(emb_width) / 2.0
    residual = merged_row * lax.rsqrt(jnp.mean(merged_row * merged_row) + norm_eps)
    quantized = jnp.zeros_like(merged_row)
    for level_index in range(book_rows.shape[0]):
        code_rows = book_rows[level_index]
        cross_terms = jnp.dot(code_rows, residual, precision=highest)
        logits = (2.0 * cross_terms - jnp.sum(code_rows * code_rows, axis=1)) / quant_tau
        logits = logits - lax.stop_gradient(jnp.max(logits))
        exp_logits = jnp.exp(logits)
        chosen = jnp.dot(exp_logits / jnp.sum(exp_logits), code_rows, precision=highest)
        residual = residual - chosen
        quantized = quantized + chosen
    recon_error = jnp.mean(residual * residual)
    anchor = quantized * lax.rsqrt(jnp.mean(quantized * quantized) + norm_eps)
    candidates = jnp.concatenate([merged_row[None, :], negatives.astype(jnp.float32)], axis=0)
    cand_unit = candidates * lax.rsqrt(
        jnp.mean(candidates * candidates, axis=1, keepdims=True) + norm_eps
    )
    similarity = jnp.dot(cand_unit, anchor, precision=highest) / (emb_width * contrast_temp)
    top_score = lax.stop_gradient(jnp.max(similarity))
    contrast = top_score + jnp.log(jnp.sum(jnp.exp(similarity - top_score))) - similarity[0]
    return contrast + beta_weight * recon_error


def stacked_term(columns, first_grad, second_grad, in_first):
    contract = (((0,), (0,)), ((), ()))
    first_term = lax.dot_general(columns, first_grad, contract, preferred_element_type=jnp.float32)
    second_term = lax.dot_general(
        columns, second_grad, contract, preferred_element_type=jnp.float32
    )
    return jnp.where(in_first[:, None], first_term, second_term)


def cost(flops, moved):
    return pl.CostEstimate(flops=flops, bytes_accessed=moved, transcendentals=0)


def first_rows_in(shard, shard_rows, first_rows):
    return min(max(first_rows - shard * shard_rows, 0), shard_rows)


def unit_groups(shard_count, shard_rows, first_rows, part_count):
    groups = []
    for shard in range(shard_count):
        inside = first_rows_in(shard, shard_rows, first_rows)
        if inside < shard_rows:
            groups.append((shard, inside, shard * shard_rows + inside - first_rows, (shard_rows - inside) // part_count))
    return groups


def even_units(groups, shard_rows, part_count):
    return all(
        inside % TILE == 0 and share % TILE == 0 and inside + share * part_count == shard_rows
        for _, inside, _, share in groups
    )


def message_kernel(groups, rows_ref, message_ref, built, semaphores):
    shard, segment = lax.axis_index("dp"), lax.axis_index("segment")
    copies, _, columns = message_ref.shape
    row_count, width = rows_ref.shape
    segment_count = width // (SIDES * columns)
    first_last = groups[0][0]

    for part in range(segment_count):
        here = segment == part

        @pl.when((shard <= first_last) & here)
        def _(part=part):
            for side in range(SIDES):
                picked = []
                for _, _, base, share in groups:
                    start = base + share * (side * segment_count + part)
                    picked.append(rows_ref[:, start : start + share])
                built[side] = jnp.concatenate(picked, axis=1)

        for group_shard, inside, _, share in groups:

            @pl.when((shard == group_shard) & here)
            def _(part=part, inside=inside, share=share):
                for side in range(SIDES):
                    start = inside + share * (side * segment_count + part)
                    low = start // 16 * 16
                    high = min(row_count, -(-(start + share) // 16) * 16)
                    taken = rows_ref[low:high, :].astype(F32)[start - low : start - low + share]
                    pieces = [taken[:, block * columns : (block + 1) * columns] for block in range(width // columns)]
                    built[side, inside:, :] = jnp.concatenate(pieces, axis=0).astype(BF16)

    sends = [
        pltpu.make_async_copy(built.at[copy % SIDES], message_ref.at[copy, :row_count], semaphores.at[copy]) for copy in range(copies)
    ]
    for send in sends:
        send.start()
    for send in sends:
        send.wait()


def weight_message(uniting_weights, groups, copies, columns):
    shard_rows = uniting_weights.shape[0]
    return pl.pallas_call(
        functools.partial(message_kernel, groups),
        in_specs=[pl.BlockSpec(memory_space=pltpu.VMEM)],
        out_specs=pl.BlockSpec(memory_space=pl.ANY),
        out_shape=jax.ShapeDtypeStruct((copies, shard_rows + 16, columns), BF16),
        scratch_shapes=[pltpu.VMEM((SIDES, shard_rows, columns), BF16), pltpu.SemaphoreType.DMA((copies,))],
        cost_estimate=cost(0, 4 * uniting_weights.size),
    )(uniting_weights)


def forward_kernel(
    groups,
    first_rows,
    mine_ref,
    twin_ref,
    own_ref,
    weights,
    block_ref,
    hidden_ref,
    active_ref,
    second_ref,
    partial_ref,
):
    shard_count, _, columns = weights.shape
    shard_rows = block_ref.shape[1]
    shard = lax.axis_index("dp")
    source_count, source_items, half = mine_ref.shape
    items, width = source_count * source_items, 2 * half
    mine = mine_ref[...].astype(F32).reshape(items, half)
    twin = twin_ref[...].astype(F32).reshape(items, half)
    first_core = lax.rem(lax.axis_index("segment"), 2) == 0
    embedded = jnp.concatenate([jnp.where(first_core, mine, twin), jnp.where(first_core, twin, mine)], axis=1)
    normed = embedded * lax.rsqrt(jnp.mean(embedded * embedded, axis=1, keepdims=True) + norm_eps)
    normed = normed.astype(BF16)
    hidden = jnp.zeros((items, columns), F32)
    own_block = jnp.zeros((items, shard_rows), BF16)
    for block in range(shard_count):
        inside = first_rows_in(block, shard_rows, first_rows)
        start = block * shard_rows
        if inside > 0:
            rows = normed[:, start : start + inside]
            hidden = hidden + dot_nn(rows, weights[block, :inside])
            if inside < shard_rows:
                rows = jnp.concatenate([rows, jnp.zeros((items, shard_rows - inside), BF16)], axis=1)
            own_block = jnp.where(shard == block, rows, own_block)
    block_ref[...] = own_block
    hidden_ref[...] = hidden
    active = gelu_value(hidden).astype(BF16)
    active_ref[...] = active
    lines = []
    for block, inside, _, share in groups:
        rows = weights[block, inside:shard_rows, :].astype(F32)
        pieces = [rows[part * share : (part + 1) * share] for part in range(partial_ref.shape[1] // columns)]
        lines.append(jnp.concatenate(pieces, axis=1))
    second_ref[...] = jnp.concatenate(lines, axis=0).astype(BF16)
    partial_ref[...] = dot_nn(dot_nn(own_ref[...], active).astype(BF16), second_ref[...])


def merge_part(mine_half, twin_half, pieces, own, groups, shard_rows, first_rows, width):
    shard_count, _, columns = pieces.shape
    items = mine_half.shape[0] * mine_half.shape[1]
    vm = pl.BlockSpec(memory_space=pltpu.VMEM)
    return pl.pallas_call(
        functools.partial(forward_kernel, groups, first_rows),
        in_specs=[vm] * 4,
        out_specs=[vm] * 5,
        out_shape=[
            jax.ShapeDtypeStruct((items, shard_rows), BF16),
            jax.ShapeDtypeStruct((items, columns), F32),
            jax.ShapeDtypeStruct((items, columns), BF16),
            jax.ShapeDtypeStruct((columns, width), BF16),
            jax.ShapeDtypeStruct((own.shape[0], width), F32),
        ],
        cost_estimate=cost(2 * items * first_rows * columns, 2 * pieces.size),
        compiler_params=pltpu.CompilerParams(vmem_limit_bytes=8 * MIB),
    )(mine_half, twin_half, own, pieces)


def split(value):
    high = value.astype(BF16)
    return high, (value - high.astype(F32)).astype(BF16)


def exact_nt(value, high, low):
    first, second = split(value)
    rows = value.shape[0]
    both = dot_nt(jnp.concatenate([first, second], axis=0), high)
    return both[:rows] + both[rows:] + dot_nt(first, low)


def exact_nn(value, high, low):
    first, second = split(value)
    rows = value.shape[0]
    both = dot_nn(jnp.concatenate([first, second], axis=0), high)
    return both[:rows] + both[rows:] + dot_nn(first, low)


def dot_tn(a, b):
    return lax.dot_general(a, b, (((0,), (0,)), ((), ())), preferred_element_type=F32)


def exact_tn(a, b):
    a_high, a_low = split(a)
    b_high, b_low = split(b)
    return dot_tn(
        jnp.concatenate([a_high, a_low, a_high], axis=0), jnp.concatenate([b_high, b_high, b_low], axis=0)
    )


def square_sums(value):
    high, low = split(value * value)
    ones = jnp.ones((8, value.shape[1]), BF16)
    return dot_nt(ones, high) + dot_nt(ones, low)


def prepare_kernel(book_ref, bank_ref, high_ref, low_ref, norm_ref, scale_ref):
    width = bank_ref.shape[1]
    for level in range(book_ref.shape[0]):
        codes = book_ref[level]
        high, low = split(codes)
        high_ref[level] = high
        low_ref[level] = low
        norm_ref[level] = square_sums(codes)
    scale_ref[...] = lax.rsqrt(square_sums(bank_ref[...].astype(F32)) * (1.0 / width) + norm_eps)


def prepared(books, bank):
    levels, codes, _ = books.shape
    vm = pl.BlockSpec(memory_space=pltpu.VMEM)
    return pl.pallas_call(
        prepare_kernel,
        in_specs=[vm] * 2,
        out_specs=[vm] * 4,
        out_shape=[
            jax.ShapeDtypeStruct(books.shape, BF16),
            jax.ShapeDtypeStruct(books.shape, BF16),
            jax.ShapeDtypeStruct((levels, 8, codes), F32),
            jax.ShapeDtypeStruct((8, bank.shape[0]), F32),
        ],
        cost_estimate=cost(0, 12 * books.size),
        compiler_params=pltpu.CompilerParams(vmem_limit_bytes=10 * MIB),
    )(books, bank)


def quantizer_kernel(
    loss_scale,
    merged_ref,
    highs,
    lows,
    norm_ref,
    bank_ref,
    bank_scale_ref,
    count_ref,
    merged_grad_ref,
    loss_ref,
    left_ref,
    right_ref,
):
    width = merged_ref.shape[1]
    levels = highs.shape[0]
    inverse_tau = 2.0 / math.sqrt(width)
    inverse_temp = 1.0 / (width * contrast_temp)
    merged = merged_ref[...].astype(BF16).astype(F32)
    merged_scale = lax.rsqrt(jnp.mean(merged * merged, axis=1, keepdims=True) + norm_eps)
    residuals = [merged * merged_scale]
    shares, chosen_rows = [], []
    for level in range(levels):
        high, low = highs[level], lows[level]
        logits = (2.0 * exact_nt(residuals[level], high, low) - norm_ref[level]) * inverse_tau
        exps = jnp.exp(logits - jnp.max(logits, axis=1, keepdims=True))
        share = exps / jnp.sum(exps, axis=1, keepdims=True)
        chosen = exact_nn(share, high, low)
        shares.append(share)
        chosen_rows.append(chosen)
        residuals.append(residuals[level] - chosen)
    last = residuals[levels]
    quantized = chosen_rows[0]
    for chosen in chosen_rows[1:]:
        quantized = quantized + chosen
    anchor_scale = lax.rsqrt(jnp.mean(quantized * quantized, axis=1, keepdims=True) + norm_eps)
    anchor = quantized * anchor_scale
    own = jnp.sum(anchor * residuals[0], axis=1, keepdims=True) * inverse_temp
    bank = bank_ref[...]
    bank_scale = bank_scale_ref[...]
    anchor_parts = jnp.concatenate(split(anchor), axis=0)
    rows = anchor.shape[0]
    both = dot_nt(anchor_parts, bank)
    similar = (both[:rows] + both[rows:]) * bank_scale * inverse_temp
    counts = count_ref[...]
    named = counts > 0.0
    top = jnp.maximum(jnp.max(jnp.where(named, similar, own), axis=1, keepdims=True), own)
    bank_exps = jnp.where(named, jnp.exp(jnp.where(named, similar, top) - top), 0.0) * counts
    own_exp = jnp.exp(own - top)
    total = jnp.sum(bank_exps, axis=1, keepdims=True) + own_exp
    item_losses = top + jnp.log(total) - own + jnp.mean(last * last, axis=1, keepdims=True)
    loss_ref[0] = jnp.sum(item_losses) * loss_scale

    bank_weight = bank_exps / total * (loss_scale * inverse_temp)
    own_weight = (own_exp / total - 1.0) * (loss_scale * inverse_temp)
    weight_parts = jnp.concatenate(split(bank_weight * bank_scale), axis=0)
    both = dot_nn(weight_parts, bank)
    anchor_grad = both[:rows] + both[rows:] + own_weight * residuals[0]
    unit_grad = own_weight * anchor
    quantized_grad = anchor_scale * (anchor_grad - anchor * jnp.mean(anchor * anchor_grad, axis=1, keepdims=True))
    residual_grad = last * (2.0 * loss_scale / width)
    for level in reversed(range(levels)):
        high, low = highs[level], lows[level]
        chosen_grad = quantized_grad - residual_grad
        share_grad = exact_nt(chosen_grad, high, low)
        share = shares[level]
        logit_grad = share * (share_grad - jnp.sum(share * share_grad, axis=1, keepdims=True)) * (2.0 * inverse_tau)
        left_ref[level] = jnp.concatenate([share, logit_grad], axis=0)
        right_ref[level] = jnp.concatenate([chosen_grad, residuals[level]], axis=0)
        residual_grad = residual_grad + exact_nn(logit_grad, high, low)
    unit_grad = unit_grad + residual_grad
    unit = residuals[0]
    merged_grad = merged_scale * (unit_grad - unit * jnp.mean(unit * unit_grad, axis=1, keepdims=True))
    merged_grad_ref[...] = merged_grad.astype(BF16)


def quantizer(merged, ready, bank, counts, loss_scale):
    highs, lows, norms, bank_scale = ready
    levels, codes, width = highs.shape
    rows = merged.shape[0]
    vm = pl.BlockSpec(memory_space=pltpu.VMEM)
    return pl.pallas_call(
        functools.partial(quantizer_kernel, loss_scale),
        in_specs=[vm] * 7,
        out_specs=[vm, pl.BlockSpec(memory_space=pltpu.SMEM), vm, vm],
        out_shape=[
            jax.ShapeDtypeStruct(merged.shape, BF16),
            jax.ShapeDtypeStruct((1,), F32),
            jax.ShapeDtypeStruct((levels, 2 * rows, codes), F32),
            jax.ShapeDtypeStruct((levels, 2 * rows, width), F32),
        ],
        cost_estimate=cost(64 * highs.size, 4 * highs.size),
        compiler_params=pltpu.CompilerParams(vmem_limit_bytes=12 * MIB),
    )(merged, highs, lows, norms, bank, bank_scale, counts)


def codebook_kernel(left_ref, right_ref, book_ref, grad_ref):
    levels, doubled, _ = left_ref.shape
    width = right_ref.shape[2]
    rows = doubled // 2
    ones = jnp.ones((rows, 128), F32)
    for level in range(levels):
        outer = exact_tn(left_ref[level], right_ref[level])
        totals = exact_tn(left_ref[level, rows:], ones)
        for block in range(width // 128):
            span = slice(block * 128, (block + 1) * 128)
            grad_ref[level, :, span] = outer[:, span] - totals * book_ref[level, :, span]


def codebook_grad(left, right, books):
    vm = pl.BlockSpec(memory_space=pltpu.VMEM)
    return pl.pallas_call(
        codebook_kernel,
        in_specs=[vm] * 3,
        out_specs=vm,
        out_shape=jax.ShapeDtypeStruct(books.shape, F32),
        cost_estimate=cost(96 * books.size, 8 * books.size),
        compiler_params=pltpu.CompilerParams(vmem_limit_bytes=10 * MIB),
    )(left, right, books)


def backward_kernel(gathered_ref, order_ref, hidden_ref, active_ref, second_ref, out_grad_ref, sent_ref):
    owners, places, width = gathered_ref.shape
    columns = hidden_ref.shape[1]
    gathered = gathered_ref[...].astype(F32).reshape(owners * places, width).astype(BF16)
    out_grad = dot_tn(order_ref[...], gathered).astype(BF16)
    out_grad_ref[...] = out_grad
    hidden_grad = dot_nt(out_grad, second_ref[...]) * gelu_slope(hidden_ref[...])
    sent_ref[:, :columns] = hidden_grad.astype(BF16)
    sent_ref[:, columns:] = active_ref[...]


def backward_part(gathered, order, hidden, active, second):
    items, columns = hidden.shape
    vm = pl.BlockSpec(memory_space=pltpu.VMEM)
    return pl.pallas_call(
        backward_kernel,
        in_specs=[vm] * 5,
        out_specs=[vm] * 2,
        out_shape=[
            jax.ShapeDtypeStruct((items, gathered.shape[2]), BF16),
            jax.ShapeDtypeStruct((items, 2 * columns), BF16),
        ],
        cost_estimate=cost(2 * items * second.size, 2 * second.size),
        compiler_params=pltpu.CompilerParams(vmem_limit_bytes=8 * MIB),
    )(gathered, order, hidden, active, second)


def weight_grad_kernel(
    groups, block_ref, out_grad_ref, mine_ref, twin_ref, grad_ref, hidden_grad, active, built, semaphores
):
    shard, segment = lax.axis_index("dp"), lax.axis_index("segment")
    _, items, doubled = mine_ref.shape
    cores = 2
    own_core = lax.rem(segment, cores)
    columns = doubled // 2
    shard_rows = block_ref.shape[1]
    own_side, own_row = lax.rem(shard, SIDES), segment // cores
    segment_count = hidden_grad.shape[1] // (SIDES * columns)

    def place_units(target, first):
        for side in range(SIDES):
            for other in range(segment_count):
                parts = [
                    jnp.where(
                        own_core == other % cores,
                        mine_ref[index, :, first : first + columns],
                        twin_ref[index, :, first : first + columns],
                    )
                    for index in range(4)
                ]
                same_row = own_row == other // cores
                near = jnp.where(same_row, parts[0], parts[1])
                across = jnp.where(same_row, parts[2], parts[3])
                part = jnp.where(own_side == side, near, across)
                offset = 0
                for _, _, base, share in groups:
                    spot = base + share * (side * segment_count + other)
                    target[:, spot : spot + share] = part[:, offset : offset + share]
                    offset += share

    place_units(hidden_grad, 0)

    @pl.when(shard >= groups[0][0])
    def _():
        place_units(active, columns)

    edges = [*range(0, shard_rows, GRAD_ROWS), shard_rows]
    sends = []
    for index, (low, high) in enumerate(zip(edges[:-1], edges[1:])):
        built[low:high, :] = dot_tn(block_ref[:, low:high], hidden_grad[...])
        for group_shard, inside, base, _ in groups:
            if high > inside:
                first = max(low, inside)

                @pl.when(shard == group_shard)
                def _(inside=inside, base=base, first=first, high=high):
                    wanted = active[:, base + first - inside : base + high - inside]
                    built[first:high, :] = dot_tn(wanted, out_grad_ref[...])

        send = pltpu.make_async_copy(built.at[low:high], grad_ref.at[low:high], semaphores.at[index])
        send.start()
        sends.append(send)
    for send in sends:
        send.wait()


def weight_grad(block, out_grad, mine, twin, groups):
    items, shard_rows = block.shape
    width = out_grad.shape[1]
    vm = pl.BlockSpec(memory_space=pltpu.VMEM)
    return pl.pallas_call(
        functools.partial(weight_grad_kernel, groups),
        in_specs=[vm] * 4,
        out_specs=pl.BlockSpec(memory_space=pl.ANY),
        out_shape=jax.ShapeDtypeStruct((shard_rows, width), F32),
        scratch_shapes=[
            pltpu.VMEM((items, width), BF16),
            pltpu.VMEM((items, width), BF16),
            pltpu.VMEM((shard_rows, width), F32),
            pltpu.SemaphoreType.DMA((-(-shard_rows // GRAD_ROWS),)),
        ],
        cost_estimate=cost(2 * items * shard_rows * width, 4 * shard_rows * width),
        compiler_params=pltpu.CompilerParams(vmem_limit_bytes=8 * MIB),
    )(block, out_grad, mine, twin)


def around(near, across, segment_count, dp_count):
    row = lax.ppermute(near, "segment", [(j, j ^ 2) for j in range(segment_count)])
    side = lax.ppermute(across, "dp", [(i, i ^ 1) for i in range(dp_count)])
    corners = [
        (j * dp_count + i, (j ^ 2) * dp_count + (i ^ 1)) for j in range(segment_count) for i in range(dp_count)
    ]
    corner = lax.ppermute(across, ("segment", "dp"), corners)
    return row, side, corner


def spread(rows, axis_name, count):
    return lax.all_to_all(
        jnp.broadcast_to(rows[None], (count,) + rows.shape), axis_name, 0, 0, tiled=True
    )


def per_device_parts(
    images, texts, section_weights, uniting_weights, codebooks, neg_bank, item_cats, cat_slot, neg_index
):
    segment_index = lax.axis_index("segment")
    segment_count = lax.axis_size("segment")
    dp_index = lax.axis_index("dp")
    dp_count = lax.axis_size("dp")
    item_count, _, image_width = images.shape
    text_width = texts.shape[2]
    first_rows = image_width + text_width
    shard_rows, width = uniting_weights.shape
    columns = width // (SIDES * segment_count)
    groups = unit_groups(dp_count, shard_rows, first_rows, SIDES * segment_count)
    message = weight_message(uniting_weights, groups, dp_count, columns)
    flag = (1 - segment_index % 2).astype(jnp.int32).reshape(1)
    flag, message = lax.optimization_barrier((flag, message))
    pieces = lax.all_to_all(message, "dp", 0, 0, tiled=True)
    pooled = pooled_features(images, texts, section_weights, segment_index, flag)
    pooled = pooled + lax.ppermute(pooled, "segment", [(i, i ^ 1) for i in range(segment_count)])
    mine = pooled.astype(BF16)
    other = lax.ppermute(mine, "segment", [(i, i ^ 2) for i in range(segment_count)])
    is_image = segment_index < 2
    embedded = jnp.concatenate(
        [jnp.where(is_image, mine, other)[:, :image_width], jnp.where(is_image, other, mine)], axis=1
    )
    embedded, pieces, books = lax.optimization_barrier((embedded, pieces, codebooks[0]))
    half = first_rows // 2
    embedded_half = jnp.where(segment_index % 2 == 0, embedded[:, :half], embedded[:, half:])
    mine_half = spread(embedded_half, "dp", dp_count)
    twin_half = lax.ppermute(mine_half, "segment", [(i, i ^ 1) for i in range(segment_count)])

    pair = item_cats.shape[1] // dp_count
    cats = item_cats.reshape(segment_count, dp_count, pair).transpose(1, 0, 2).reshape(-1)
    items = cats.shape[0]
    slots = jnp.sum(
        jnp.where(cats[:, None] == jnp.arange(cat_slot.shape[0])[None, :], cat_slot[None, :], 0), axis=1
    )
    ids = jnp.arange(items)
    rank = jnp.sum(jnp.where((slots[None, :] == slots[:, None]) & (ids[None, :] < ids[:, None]), 1, 0), axis=1)
    owned = segment_count * CAP
    order = (ids[:, None] == (slots * owned + rank)[None, :]).astype(BF16)
    own = lax.dynamic_slice_in_dim(order, dp_index * owned, owned, 0)
    across_own = lax.dynamic_slice_in_dim(order, (dp_index ^ 1) * owned, owned, 0)
    both_own = jnp.concatenate([own, across_own], axis=0)
    negatives = neg_index.reshape(segment_count, dp_count, pair, -1).transpose(1, 0, 2, 3).reshape(items, -1)
    own_negatives = jnp.dot(own.astype(F32), negatives.astype(F32), precision=highest)
    bank = neg_bank[0]
    ready = prepared(books, bank)
    bank_ids = jnp.arange(bank.shape[0]).astype(F32)
    counts = jnp.sum((own_negatives[:, :, None] == bank_ids[None, None, :]).astype(F32), axis=1)

    block, hidden, active, second, partial = merge_part(
        mine_half, twin_half, pieces, both_own, groups, shard_rows, first_rows, width
    )
    partial = partial + lax.ppermute(partial, "segment", [(i, i ^ 1) for i in range(segment_count)])
    row, side, corner = around(partial[:owned], partial[owned:], segment_count, dp_count)
    merged = (partial[:owned] + row) + (side + corner)
    merged_grad, loss, left, right = quantizer(merged, ready, bank, counts, 1.0 / math.sqrt(items))
    gathered = spread(merged_grad, "dp", dp_count)
    book_grad = codebook_grad(left, right, books)
    out_grad, sent = backward_part(gathered, order, hidden, active, second)
    mine = jnp.stack((sent,) + around(sent, sent, segment_count, dp_count))
    mine, book_grad = lax.optimization_barrier((mine, book_grad))
    twin = lax.ppermute(mine, "segment", [(i, i ^ 1) for i in range(segment_count)])
    uniting_grad = weight_grad(block, out_grad, mine, twin, groups)
    return (uniting_grad, book_grad[None], loss)


def pooled_features(images, texts, section_weights, segment_index, flag):
    image_width, text_width = images.shape[2], texts.shape[2]

    def image_branch(operands):
        pooled = image_pooled(operands[0], operands[2], flag)
        return jnp.pad(pooled, ((0, 0), (0, text_width - image_width)))

    def text_branch(operands):
        return text_pooled(operands[1], operands[2], flag)

    return lax.cond(segment_index < 2, image_branch, text_branch, (images, texts, section_weights))


def per_device_gathered(
    images,
    texts,
    section_weights,
    uniting_weights,
    codebooks,
    neg_bank,
    item_cats,
    cat_slot,
    neg_index,
):
    segment_index = lax.axis_index("segment")
    segment_count = lax.axis_size("segment")
    dp_index = lax.axis_index("dp")
    dp_count = lax.axis_size("dp")
    group_index = segment_index % 2
    item_count = images.shape[0]

    flag = (1 - group_index).astype(jnp.int32).reshape(1)
    pooled = pooled_features(images, texts, section_weights, segment_index, flag)
    image_width = images.shape[2]
    is_image = segment_index < 2
    packed = jnp.concatenate(
        [jnp.where(is_image, pooled[:, :image_width], 0.0), jnp.where(is_image, 0.0, pooled)], axis=1
    )
    embedded = lax.psum_scatter(packed, "segment", scatter_dimension=0, tiled=True).astype(
        jnp.bfloat16
    )
    stacked = lax.all_gather(uniting_weights, "dp", axis=0, tiled=True)
    first_rows = embedded.shape[1]
    cat_per_dev = codebooks.shape[0]
    slot_count = cat_per_dev * CAP
    row_total = item_cats.shape[1]
    cats_all = item_cats.reshape(-1)
    entry_count = cats_all.shape[0]
    entry_ids = jnp.arange(entry_count)
    category_match = cats_all[:, None] == jnp.arange(cat_slot.shape[0])[None, :]
    entry_slots = jnp.sum(jnp.where(category_match, cat_slot[None, :], 0), axis=1)
    entry_owner = entry_slots // cat_per_dev
    entry_local = entry_slots % cat_per_dev
    entry_row = entry_ids // row_total
    earlier = entry_ids[None, :] < entry_ids[:, None]
    same_cat = (cats_all[:, None] == cats_all[None, :]) & (entry_row[:, None] == entry_row[None, :])
    entry_rank = jnp.sum(jnp.where(earlier & same_cat, 1, 0), axis=1)
    entry_place = entry_local * CAP + entry_rank
    entry_position = entry_row * slot_count + entry_place
    owned = entry_owner == dp_index
    all_slots = segment_count * slot_count
    slot_match_all = owned[None, :] & (entry_position[None, :] == jnp.arange(all_slots)[:, None])
    view_match = lax.dynamic_slice(
        slot_match_all,
        (segment_index * slot_count, segment_index * row_total),
        (slot_count, row_total),
    )
    view_base = segment_index * row_total
    view_slots = view_match.shape[0]
    selection = view_match.astype(jnp.bfloat16)
    valid = jnp.sum(view_match.astype(jnp.float32), axis=1)
    slot_item = jnp.sum(
        jnp.where(view_match, jnp.arange(view_match.shape[1])[None, :] + view_base, 0), axis=1
    )
    slot_negs = jnp.take(neg_index.reshape(entry_count, -1), slot_item, axis=0)
    slot_local = jnp.arange(view_slots) % slot_count // CAP
    bank_rows = neg_bank.reshape(-1, neg_bank.shape[2])
    negatives = jnp.take(bank_rows, slot_local[:, None] * neg_bank.shape[1] + slot_negs, axis=0)
    loss_scale = 1.0 / math.sqrt(dp_count * item_count)

    def owner_objective(merged_float, books):
        per_row = jax.vmap(item_loss)(merged_float, books[slot_local], negatives)
        return jnp.sum(per_row * valid) * loss_scale

    gathered = jnp.dot(
        selection,
        lax.all_gather(embedded, "dp", axis=0, tiled=True),
        preferred_element_type=jnp.float32,
    )
    gathered = gathered.astype(jnp.bfloat16)
    normed_all, hidden_all, activated_all, merged_all = merge_forward(gathered, stacked)
    loss_local, pullback = jax.vjp(owner_objective, merged_all.astype(jnp.float32), codebooks)
    grad_all, book_grad = pullback(jnp.ones((), jnp.float32))
    out_grad = grad_all.astype(jnp.bfloat16)
    hidden_grad = merge_backward(hidden_all, stacked, out_grad, first_rows)
    joined = jnp.concatenate([normed_all, activated_all], axis=1)
    book_total, loss_owner = lax.psum((book_grad, loss_local), "segment")
    shard_rows = uniting_weights.shape[0]
    shard_start = dp_index * shard_rows
    shard_first = shard_start + jnp.arange(shard_rows) < first_rows
    joined_piece = lax.all_gather(joined, "dp", axis=0, tiled=True)
    first_piece = lax.all_gather(hidden_grad, "dp", axis=0, tiled=True)
    second_piece = lax.all_gather(out_grad, "dp", axis=0, tiled=True)
    columns = lax.dynamic_slice_in_dim(joined_piece, shard_start, shard_rows, 1)
    segment_grad = stacked_term(columns, first_piece, second_piece, shard_first)
    uniting_grad = lax.psum(segment_grad, "segment")
    return (uniting_grad, book_total, loss_owner.reshape(1))


def per_device(*operands):
    images, texts, _, uniting_weights = operands[:4]
    segment_count, dp_count = lax.axis_size("segment"), lax.axis_size("dp")
    shard_rows = uniting_weights.shape[0]
    first_rows = images.shape[2] + texts.shape[2]
    groups = unit_groups(dp_count, shard_rows, first_rows, SIDES * segment_count)
    if dp_count % SIDES == 0 and even_units(groups, shard_rows, SIDES * segment_count):
        return per_device_parts(*operands)
    return per_device_gathered(*operands)


def solution(mesh):
    placed = (
        P("dp", None, None),
        P("dp", None, None),
        P("segment", None, None),
        P("dp", None),
        P("dp", None, None, None),
        P("dp", None, None),
        P(),
        P(),
        P(),
    )
    return jax.shard_map(
        per_device,
        mesh=mesh,
        in_specs=placed,
        out_specs=(P("dp", None), P("dp", None, None, None), P("dp")),
        check_vma=False,
    )
```
